32 devices in a mesh: dp: 4 (over y, x), tensor: 8 (over z, core).
Axes of the slice: x: 2, y: 2, z: 4, core: 2. Of those that a mesh axis runs over, the one named last changes fastest.
Arguments:
- layer_input: bfloat16 [2, 4, 1536, 1536], P(None, 'dp', 'tensor'), may hold values from -6 to 6
- lengths: int32 [2, 4], P(None, 'dp'), may hold values from 1 to 1536, as said below
- attn_gain: bfloat16 [1536], P(('dp', 'tensor')), may hold values from 0.099609375 to 1.8984375
- query_proj: bfloat16 [1536, 1536], P(('dp', 'tensor')), may hold values from -0.15625 to 0.15625
- query_bias: bfloat16 [1536], P(('dp', 'tensor')), may hold values from -3 to 3
- key_proj: bfloat16 [1536, 256], P(('dp', 'tensor')), may hold values from -0.15625 to 0.15625
- key_bias: bfloat16 [256], P(('dp', 'tensor')), may hold values from -3 to 3
- value_proj: bfloat16 [1536, 256], P(('dp', 'tensor')), may hold values from -0.15625 to 0.15625
- value_bias: bfloat16 [256], P(('dp', 'tensor')), may hold values from -3 to 3
- out_proj: bfloat16 [1536, 1536], P(('dp', 'tensor')), may hold values from -2 to 2
- mlp_gain: bfloat16 [1536], P(('dp', 'tensor')), may hold values from 0.099609375 to 1.8984375
- gate_proj: bfloat16 [1536, 8960], P(None, 'tensor'), may hold values from -0.15625 to 0.15625
- up_proj: bfloat16 [1536, 8960], P(None, 'tensor'), may hold values from -0.15625 to 0.15625
- down_proj: bfloat16 [8960, 1536], P('tensor'), may hold values from -0.0625 to 0.0625
- cotangent: bfloat16 [2, 4, 1536, 1536], P(None, 'dp', 'tensor'), may hold values from -6 to 6
Outputs:
- layer_output: bfloat16 [2, 4, 1536, 1536], P(None, 'dp', 'tensor')
- grad_input: float32 [2, 4, 1536, 1536], P(None, 'dp', 'tensor')
- grad_attn_gain: float32 [1536], P(('dp', 'tensor'))
- grad_query_proj: float32 [1536, 1536], P(('dp', 'tensor'))
- grad_query_bias: float32 [1536], P(('dp', 'tensor'))
- grad_key_proj: float32 [1536, 256], P(('dp', 'tensor'))
- grad_key_bias: float32 [256], P(('dp', 'tensor'))
- grad_value_proj: float32 [1536, 256], P(('dp', 'tensor'))
- grad_value_bias: float32 [256], P(('dp', 'tensor'))
- grad_out_proj: float32 [1536, 1536], P(('dp', 'tensor'))
- grad_mlp_gain: float32 [1536], P(('dp', 'tensor'))
- grad_gate_proj: float32 [1536, 8960], P(None, 'tensor')
- grad_up_proj: float32 [1536, 8960], P(None, 'tensor')
- grad_down_proj: float32 [8960, 1536], P('tensor')
The draws below stay inside these ranges and needn't reach their ends.
Inputs may be any that keep to these rules, and one draw needn't show every extreme that they name: `lengths`: right padding: in each column (the 2 sequences of one index of dp) at least one sequence has all 1536 tokens; every sequence has at least one token.
All inputs are finite; a program needn't handle non-finite values.
Results may differ from the reference program's by a relative error of at most 0.025.
Values may be sent and summed in bfloat16 or wider, within the bound.
A program may use at most 320 MiB of HBM per device.

```python
import jax
import jax.numpy as jnp
from jax import lax

D = 1536
FF = 8960
H = 12
KV = 2
HD = 128
LEN = 1536
MICRO = 2
SEQS = 4


def draw_lengths(key, part):
    key = jax.random.fold_in(key, 11)
    first, second = jax.random.split(key)
    base = jax.random.randint(first, (MICRO, SEQS), 1, LEN + 1)
    full_row = jax.random.randint(second, (1, SEQS), 0, MICRO)
    picked = jnp.arange(MICRO, dtype=jnp.int32)[:, None] == full_row
    return jnp.where(picked, LEN, base).astype(jnp.int32)


def block_scale(stream_key, dims, cuts, low, high):
    level = 1.0
    for axis_at, shards_of in cuts:
        heights = jax.random.uniform(jax.random.fold_in(jax.random.fold_in(stream_key, 6), axis_at), (shards_of,), jnp.float32, low / len(cuts), high / len(cuts))
        level = level * jnp.repeat(jnp.exp(heights), dims[axis_at] // shards_of).reshape((-1,) + (1,) * (len(dims) - 1 - axis_at))
    return level


def normal_values(stream_key, dims, deviation, limit, cuts=(), kind=jnp.bfloat16):
    factor_of = block_scale(stream_key, dims, cuts, -0.22, 0.18) if cuts else 1.0
    drawn = jax.random.normal(stream_key, dims, jnp.float32) * deviation * factor_of
    return jnp.minimum(jnp.maximum(drawn, -limit), limit).astype(kind)


def setup_inputs(seed: int = 0) -> dict:
    key_of = jax.random.split(jax.random.key(seed), 16)
    return {
        "layer_input": normal_values(key_of[0], (MICRO, SEQS, LEN, D), 1.0, 6.0, ((1, 4), (2, 8))),
        "lengths": draw_lengths(jax.random.fold_in(key_of[15], 71), 0),
        "attn_gain": jnp.clip(1.0 + 0.18 * jax.random.normal(key_of[2], (D,), jnp.float32), 0.099609375, 1.8984375).astype(jnp.bfloat16),
        "query_proj": normal_values(key_of[3], (D, H * HD), D ** -0.5, 0.15625, ((0, 32),)),
        "query_bias": normal_values(key_of[4], (H * HD,), 0.5, 3.0, ((0, 32),)),
        "key_proj": normal_values(key_of[5], (D, KV * HD), D ** -0.5, 0.15625, ((0, 32),)),
        "key_bias": normal_values(key_of[6], (KV * HD,), 0.5, 3.0, ((0, 32),)),
        "value_proj": normal_values(key_of[7], (D, KV * HD), D ** -0.5, 0.15625, ((0, 32),)),
        "value_bias": normal_values(key_of[8], (KV * HD,), 0.5, 3.0, ((0, 32),)),
        "out_proj": normal_values(key_of[9], (H * HD, D), (max(1, H * HD * 8 // LEN)) ** -0.5, 2.0, ((0, 32),)),
        "mlp_gain": jnp.clip(1.0 + 0.18 * jax.random.normal(key_of[10], (D,), jnp.float32), 0.099609375, 1.8984375).astype(jnp.bfloat16),
        "gate_proj": normal_values(key_of[11], (D, FF), D ** -0.5, 0.15625, ((1, 8),)),
        "up_proj": normal_values(key_of[12], (D, FF), D ** -0.5, 0.15625, ((1, 8),)),
        "down_proj": normal_values(key_of[13], (FF, D), FF ** -0.5, 0.0625, ((0, 8),)),
        "cotangent": normal_values(key_of[14], (MICRO, SEQS, LEN, D), 1.0, 6.0, ((1, 4), (2, 8))),
    }


ROPE_BASE = 1000000.0
EPS = 1e-06

@jax.custom_vjp
def low(v):
    return lax.optimization_barrier(v.astype(jnp.bfloat16)).astype(jnp.float32)

@jax.custom_vjp
def low_back(v):
    return v

def low_keep(v):
    return (low(v), None)

def low_pass(kept, grad):
    return (grad,)

def back_keep(v):
    return (v, None)

def back_low(kept, grad):
    return (low(grad),)
low.defvjp(low_keep, low_pass)
low_back.defvjp(back_keep, back_low)

def matmul(left, right):
    return jnp.dot(left, right, precision=lax.Precision.HIGHEST, preferred_element_type=jnp.float32)

def rope_tables(positions):
    half = HD // 2
    freqs = ROPE_BASE ** (-(jnp.arange(half, dtype=jnp.float32) * 2.0 / HD))
    angles = positions.astype(jnp.float32)[:, None] * freqs[None, :]
    angles = jnp.concatenate([angles, angles], axis=1)
    return (jnp.cos(angles)[:, None, :], jnp.sin(angles)[:, None, :])

def rotate(values, cosine, sine):
    half = values.shape[-1] // 2
    turned = jnp.concatenate([-values[..., half:], values[..., :half]], axis=-1)
    return values * cosine + turned * sine

def normalize(rows, gain):
    return rows * lax.rsqrt(lax.optimization_barrier(jnp.mean(rows * rows, axis=-1, keepdims=True)) + EPS) * gain

def seq_layer(params, rows, length):
    attn_gain, query_proj, query_bias, key_proj, key_bias, value_proj, value_bias, out_proj, mlp_gain, gate_proj, up_proj, down_proj = params
    positions = jnp.arange(LEN, dtype=jnp.int32)
    cosine, sine = rope_tables(positions)
    hidden = low(normalize(rows, attn_gain))
    queries = low_back(matmul(hidden, query_proj) + query_bias).reshape(LEN, H, HD)
    keys = low_back(matmul(hidden, key_proj) + key_bias).reshape(LEN, KV, HD)
    values = low(low_back(matmul(hidden, value_proj) + value_bias)).reshape(LEN, KV, HD)
    queries = low(rotate(queries, cosine, sine)).reshape(LEN, KV, H // KV, HD)
    keys = low(rotate(keys, cosine, sine))
    block = min(512, LEN)
    key_ok = positions < length

    def attend(start):
        grouped = lax.dynamic_slice_in_dim(queries, start, block, 0)
        place = start + jnp.arange(block, dtype=jnp.int32)
        scores = jnp.einsum('tkgd,ukd->kgtu', grouped, keys, precision=lax.Precision.HIGHEST) * HD ** (-0.5)
        scores = low_back(scores)
        allowed = (positions[None, :] <= place[:, None]) & key_ok[None, :]
        scores = jnp.where(allowed[None, None], scores, -1e+30)
        top = lax.optimization_barrier(jnp.max(scores, axis=-1, keepdims=True))
        expd = jnp.exp(scores - top)
        probs = expd / lax.optimization_barrier(jnp.sum(expd, axis=-1, keepdims=True))
        return jnp.einsum('kgtu,ukd->tkgd', low(probs), values, precision=lax.Precision.HIGHEST).reshape(block, H * HD)
    starts = jnp.arange(LEN // block, dtype=jnp.int32) * block
    attended = lax.map(jax.checkpoint(attend), starts).reshape(LEN, H * HD)
    attended = low(low_back(attended))
    mixed = rows + low_back(matmul(attended, out_proj))
    hidden_two = low(normalize(mixed, mlp_gain))
    gate = low_back(matmul(hidden_two, gate_proj))
    up = low_back(matmul(hidden_two, up_proj))
    activ = low(gate / (1.0 + jnp.exp(-gate)) * up)
    return mixed + low_back(matmul(activ, down_proj))

def reference(layer_input, lengths, attn_gain, query_proj, query_bias, key_proj, key_bias, value_proj, value_bias, out_proj, mlp_gain, gate_proj, up_proj, down_proj, cotangent):
    params = tuple((item.astype(jnp.float32) for item in (attn_gain, query_proj, query_bias, key_proj, key_bias, value_proj, value_bias, out_proj, mlp_gain, gate_proj, up_proj, down_proj)))
    sequences = layer_input.reshape(MICRO * SEQS, LEN, D).astype(jnp.float32)
    flat_lengths = lengths.reshape(MICRO * SEQS).astype(jnp.int32)
    layer = jax.checkpoint(seq_layer)

    def forward(weights, inputs):

        def one(item):
            return layer(weights, item[0], item[1])
        return lax.map(one, (inputs, flat_lengths))
    outputs, pullback = jax.vjp(forward, params, sequences)
    valid = (jnp.arange(LEN, dtype=jnp.int32)[None, :] < flat_lengths[:, None]).astype(jnp.float32)
    grads_out = cotangent.reshape(MICRO * SEQS, LEN, D).astype(jnp.float32) * valid[:, :, None]
    weight_grads, input_grads = pullback(grads_out)
    shape = layer_input.shape
    return (outputs.reshape(shape).astype(jnp.bfloat16), input_grads.reshape(shape), weight_grads[0], weight_grads[1], weight_grads[2], weight_grads[3], weight_grads[4], weight_grads[5], weight_grads[6], weight_grads[7], weight_grads[8], weight_grads[9], weight_grads[10], weight_grads[11])
```

```python
import functools

import jax
import jax.numpy as jnp
from jax import lax
from jax.experimental import pallas as pl
from jax.experimental.pallas import tpu as pltpu
from jax.sharding import PartitionSpec as P

H = 12
KV = 2
HD = 128
GROUPS = H // KV
QW = H * HD
KW = KV * HD
QKV = QW + 2 * KW
EXTRA = 128

ROPE_BASE = 1000000.0
EPS = 1e-06
MASKED = -1e30
F32 = jnp.float32
B16 = jnp.bfloat16
VMEM_LIMIT = 56 * 1024 * 1024


def dot(a, b):
    return jnp.dot(a, b, preferred_element_type=F32)


def dot_t(a, b):
    return lax.dot_general(a, b, (((1,), (1,)), ((), ())), preferred_element_type=F32)


def t_dot(a, b):
    return lax.dot_general(a, b, (((0,), (0,)), ((), ())), preferred_element_type=F32)


def rope_tables(positions):
    half = HD // 2
    freqs = ROPE_BASE ** (-(jnp.arange(half, dtype=F32) * 2.0 / HD))
    angles = positions.astype(F32)[:, None] * freqs[None, :]
    cosine = jnp.cos(angles)
    sine = jnp.sin(angles)
    return (
        jnp.concatenate([cosine, cosine], axis=1),
        jnp.concatenate([-sine, sine], axis=1),
    )


def swap(value, axis, bit):
    count = lax.axis_size(axis)
    return lax.ppermute(value, axis, [(i, i ^ bit) for i in range(count)])


def pick(value, index, axis=0):
    return lax.dynamic_index_in_dim(value, index, axis, keepdims=False)


def ordered(mine, other, index):
    first = index == 0
    return jnp.stack([jnp.where(first, mine, other), jnp.where(first, other, mine)])


def line_gather(block, chips, place):
    count = 2 * chips
    from_left, from_right = [], []
    left = right = block
    for step in range(1, chips):
        left = lax.ppermute(left, "tensor", [(i, i + 2) for i in range(count - 2)])
        right = lax.ppermute(right, "tensor", [(i + 2, i) for i in range(count - 2)])
        from_left.append(left)
        from_right.append(right)
    window = jnp.stack(from_left[::-1] + [block] + from_right)
    return lax.dynamic_slice_in_dim(window, chips - 1 - place, chips, 0)


def line_scatter(part, chips, place):
    count = 2 * chips
    left = right = None
    for step in range(1, chips):
        ahead = part(jnp.minimum(place + chips - step, chips - 1))
        behind = part(jnp.maximum(place - chips + step, 0))
        if left is not None:
            ahead = ahead + left.astype(F32)
            behind = behind + right.astype(F32)
        left = lax.ppermute(
            ahead.astype(B16), "tensor", [(i, i + 2) for i in range(2 * step)]
        )
        right = lax.ppermute(
            behind.astype(B16),
            "tensor",
            [(count - 1 - i, count - 3 - i) for i in range(2 * step)],
        )
    return part(place) + left.astype(F32) + right.astype(F32)


def rows_scatter(partial, rows):
    chips = lax.axis_size("tensor") // 2
    place = lax.axis_index("tensor")
    chip, core = place // 2, place % 2
    width = partial.shape[-1]
    blocks = partial.reshape(chips, 2, rows, width)
    got = swap(pick(blocks, 1 - core, 1), "tensor", 1)

    def part(index):
        own = lax.dynamic_slice(blocks, (index, core, 0, 0), (1, 1, rows, width))
        return own[0, 0].astype(F32) + pick(got, index).astype(F32)

    return line_scatter(part, chips, chip)


def gather_weights(block):
    size, width = block.shape
    devices = lax.axis_size(("dp", "tensor"))
    if lax.axis_size("dp") != 4:
        return lax.all_gather(block, ("dp", "tensor"), axis=0, tiled=True)
    tensor = lax.axis_index("tensor")
    core = tensor % 2
    chips = lax.axis_size("tensor") // 2
    line = line_gather(block, chips, tensor // 2)
    row, col = lax.axis_index("dp") // 2, lax.axis_index("dp") % 2
    cut = chips // 2
    one, two = line[:cut], line[cut:]
    one = ordered(one, swap(one, "dp", 1), col)
    two = ordered(two, swap(two, "dp", 2), row)
    one = ordered(one, swap(one, "dp", 2), row)
    two = ordered(two, swap(two, "dp", 1), col)
    plane = jnp.concatenate([one, two.swapaxes(0, 1)], axis=2)
    whole = ordered(plane, swap(plane, "tensor", 1), core)
    whole = jnp.moveaxis(whole, 0, 3)
    return whole.reshape(devices * size, width)


def scatter_weights(grads):
    total, width = grads.shape
    devices = lax.axis_size(("dp", "tensor"))
    size = total // devices
    if lax.axis_size("dp") != 4:
        return lax.psum_scatter(grads, ("dp", "tensor"), scatter_dimension=0, tiled=True).astype(F32)
    tensor = lax.axis_index("tensor")
    core = tensor % 2
    chips = lax.axis_size("tensor") // 2
    row, col = lax.axis_index("dp") // 2, lax.axis_index("dp") % 2
    blocks = grads.reshape(2, 2, chips, 2, size, width)
    cut = chips // 2

    def halve(value, index, axis, mesh_axis, bit):
        got = swap(pick(value, 1 - index, axis), mesh_axis, bit)
        return (pick(value, index, axis).astype(F32) + got.astype(F32)).astype(B16)

    plane = halve(blocks, core, 3, "tensor", 1)
    one, two = plane[:, :, :cut], plane[:, :, cut:]
    one = halve(one, col, 1, "dp", 1)
    two = halve(two, row, 0, "dp", 2)
    one = halve(one, row, 0, "dp", 2)
    two = halve(two, col, 0, "dp", 1)
    line = jnp.concatenate([one, two], axis=0)
    return line_scatter(lambda index: pick(line, index).astype(F32), chips, tensor // 2)


def project_kernel(hidden_ref, weight_ref, bias_ref, cos_ref, sin_ref, out_ref):
    chunk = pl.program_id(0)
    turned = chunk < (QW + KW) // 256
    lin = dot(hidden_ref[...], weight_ref[...]) + bias_ref[...]
    for head in range(2):
        cut = pl.ds(head * HD, HD)
        one = lin[:, head * HD : (head + 1) * HD]
        rot = one * cos_ref[...] + pltpu.roll(one, HD // 2, 1) * sin_ref[...]
        out_ref[:, cut] = jnp.where(turned, rot, one).astype(B16)


def project(hidden, weights, bias, cosine, sine):
    rows, depth = hidden.shape
    return pl.pallas_call(
        project_kernel,
        grid=(QKV // 256,),
        in_specs=[
            pl.BlockSpec((rows, depth), lambda j: (0, 0)),
            pl.BlockSpec((depth, 256), lambda j: (0, j)),
            pl.BlockSpec((1, 256), lambda j: (0, j)),
            pl.BlockSpec((rows, HD), lambda j: (0, 0)),
            pl.BlockSpec((rows, HD), lambda j: (0, 0)),
        ],
        out_specs=pl.BlockSpec((rows, 256), lambda j: (0, j)),
        out_shape=jax.ShapeDtypeStruct((rows, QKV), B16),
        compiler_params=pltpu.CompilerParams(vmem_limit_bytes=VMEM_LIMIT),
        cost_estimate=pl.CostEstimate(
            flops=2 * rows * depth * QKV,
            bytes_accessed=2 * (depth * QKV + rows * depth + rows * QKV),
            transcendentals=0,
        ),
    )(hidden, weights, bias, cosine, sine)


def fill_bias(info_ref, bias):
    shape = bias.shape
    place = info_ref[1] + lax.broadcasted_iota(jnp.int32, shape, 0)
    keys = lax.broadcasted_iota(jnp.int32, shape, 1)
    bias[...] = jnp.where((keys <= place) & (keys < info_ref[0]), 0.0, MASKED)


def attend_kernel(info_ref, q_ref, k_ref, v_ref, out_ref, log_ref, bias):
    @pl.when(pl.program_id(0) == 0)
    def _():
        fill_bias(info_ref, bias)

    scores = dot_t(q_ref[...], k_ref[...]) * (HD**-0.5) + bias[...]
    top = jnp.max(scores, axis=-1, keepdims=True)
    expd = jnp.exp(scores - top)
    summed = jnp.sum(expd, axis=-1, keepdims=True)
    probs = (expd * (1.0 / summed)).astype(B16)
    out_ref[...] = dot(probs, v_ref[...]).astype(B16)
    log_ref[...] = jnp.broadcast_to(top + jnp.log(summed), log_ref.shape)


def attend(info, micro, qkv, keys_values, rows):
    total = keys_values.shape[0]
    return pl.pallas_call(
        attend_kernel,
        grid_spec=pltpu.PrefetchScalarGridSpec(
            num_scalar_prefetch=1,
            grid=(H,),
            in_specs=[
                pl.BlockSpec((rows, HD), lambda h, info: (micro, h)),
                pl.BlockSpec((total, HD), lambda h, info: (0, h // GROUPS)),
                pl.BlockSpec((total, HD), lambda h, info: (0, KV + h // GROUPS)),
            ],
            out_specs=[
                pl.BlockSpec((rows, HD), lambda h, info: (0, h)),
                pl.BlockSpec((rows, HD), lambda h, info: (0, h)),
            ],
            scratch_shapes=[pltpu.VMEM((rows, total), F32)],
        ),
        out_shape=[
            jax.ShapeDtypeStruct((rows, QW), B16),
            jax.ShapeDtypeStruct((rows, QW), F32),
        ],
        compiler_params=pltpu.CompilerParams(vmem_limit_bytes=VMEM_LIMIT),
        cost_estimate=pl.CostEstimate(
            flops=8 * rows * total * QW,
            bytes_accessed=4 * total * KW + 8 * rows * QW,
            transcendentals=H * rows * total,
        ),
    )(info, qkv, keys_values, keys_values)


def attend_back_kernel(
    info_ref, q_ref, k_ref, v_ref, g_ref, log_ref, cos_ref, sin_ref, dq_ref, dk_ref, dv_ref, bias, dk_acc, dv_acc
):
    head = pl.program_id(0)

    @pl.when(head == 0)
    def _():
        fill_bias(info_ref, bias)

    scale = HD**-0.5
    queries, keys, values, grads = q_ref[...], k_ref[...], v_ref[...], g_ref[...]
    scores = dot_t(queries, keys) * scale + bias[...]
    probs = jnp.exp(scores - log_ref[:, :1])
    grad_probs = dot_t(grads, values)
    inner = jnp.sum(grad_probs * probs, axis=-1, keepdims=True)
    grad_scores = (probs * (grad_probs - inner)).astype(B16)
    grad_q = dot(grad_scores, keys) * scale
    turned = grad_q * cos_ref[...] - pltpu.roll(grad_q, HD // 2, 1) * sin_ref[...]
    dq_ref[...] = turned.astype(B16)
    grad_k = t_dot(grad_scores, queries) * scale
    grad_v = t_dot(probs.astype(B16), grads)
    first = lax.rem(head, GROUPS) == 0

    @pl.when(first)
    def _():
        dk_acc[...] = grad_k
        dv_acc[...] = grad_v

    @pl.when(jnp.logical_not(first))
    def _():
        dk_acc[...] += grad_k
        dv_acc[...] += grad_v

    @pl.when(lax.rem(head, GROUPS) == GROUPS - 1)
    def _():
        dk_ref[...] = dk_acc[...].astype(B16)
        dv_ref[...] = dv_acc[...].astype(B16)


def attend_back(info, micro, qkv, keys_values, grads, logs, cosine, sine, rows):
    total = keys_values.shape[0]
    return pl.pallas_call(
        attend_back_kernel,
        grid_spec=pltpu.PrefetchScalarGridSpec(
            num_scalar_prefetch=1,
            grid=(H,),
            in_specs=[
                pl.BlockSpec((rows, HD), lambda h, info: (micro, h)),
                pl.BlockSpec((total, HD), lambda h, info: (0, h // GROUPS)),
                pl.BlockSpec((total, HD), lambda h, info: (0, KV + h // GROUPS)),
                pl.BlockSpec((rows, HD), lambda h, info: (0, h)),
                pl.BlockSpec((rows, HD), lambda h, info: (0, h)),
                pl.BlockSpec((rows, HD), lambda h, info: (0, 0)),
                pl.BlockSpec((rows, HD), lambda h, info: (0, 0)),
            ],
            out_specs=[
                pl.BlockSpec((rows, HD), lambda h, info: (0, h)),
                pl.BlockSpec((total, HD), lambda h, info: (0, h // GROUPS)),
                pl.BlockSpec((total, HD), lambda h, info: (0, h // GROUPS)),
            ],
            scratch_shapes=[
                pltpu.VMEM((rows, total), F32),
                pltpu.VMEM((total, HD), F32),
                pltpu.VMEM((total, HD), F32),
            ],
        ),
        out_shape=[
            jax.ShapeDtypeStruct((rows, QW), B16),
            jax.ShapeDtypeStruct((total, KW), B16),
            jax.ShapeDtypeStruct((total, KW), B16),
        ],
        compiler_params=pltpu.CompilerParams(vmem_limit_bytes=VMEM_LIMIT),
        cost_estimate=pl.CostEstimate(
            flops=20 * rows * total * QW,
            bytes_accessed=8 * total * KW + 12 * rows * QW,
            transcendentals=H * rows * total,
        ),
    )(info, qkv, keys_values, keys_values, grads, logs, cosine, sine)


def norm_back(grad_out, normed, factor, gain):
    inner = grad_out * gain
    grad_rows = factor * (inner - normed * jnp.mean(inner * normed, axis=-1, keepdims=True))
    return (grad_rows, jnp.sum(grad_out * normed, axis=0))


def normalize(rows, gain):
    factor = lax.rsqrt(jnp.mean(rows * rows, axis=-1, keepdims=True) + EPS)
    normed = rows * factor
    return (normed, factor, (normed * gain).astype(B16))


def on_device(
    layer_input,
    lengths,
    attn_gain,
    query_proj,
    query_bias,
    key_proj,
    key_bias,
    value_proj,
    value_bias,
    out_proj,
    mlp_gain,
    gate_proj,
    up_proj,
    down_proj,
    cotangent,
):
    micros = layer_input.shape[0]
    rows = layer_input.shape[2]
    depth = layer_input.shape[3]
    tensor = lax.axis_index("tensor")
    total = rows * lax.axis_size("tensor")
    devices = lax.axis_size(("dp", "tensor"))
    size = query_proj.shape[0]
    small = key_bias.shape[0]
    offset = tensor * rows
    positions = offset + jnp.arange(rows, dtype=jnp.int32)
    cosine, sine = rope_tables(positions)

    extra = jnp.zeros((size, EXTRA), B16)
    extra = extra.at[:, 0].set(attn_gain).at[:, 1].set(query_bias).at[:, 2].set(mlp_gain)
    extra = extra.at[:small, 3].set(key_bias).at[small : 2 * small, 3].set(value_bias)
    packed = gather_weights(jnp.concatenate([query_proj, key_proj, value_proj, extra], axis=1))
    wout = gather_weights(out_proj)
    vectors = packed[:, QKV : QKV + 4].astype(F32)
    gain_one, gain_two = vectors[:, 0], vectors[:, 2]
    tails = vectors[:, 3].reshape(devices, size)
    bias = jnp.concatenate(
        [vectors[:, 1], tails[:, :small].reshape(-1), tails[:, small : 2 * small].reshape(-1)]
    )[None, :]
    wqkv = packed[:, :QKV]

    valid = (positions[None, :] < lengths).astype(F32)[:, :, None]
    grad_rows = cotangent[:, 0].astype(F32) * valid
    full_grads = [
        lax.all_gather(grad_rows[m].astype(B16), "tensor", axis=0, tiled=True) for m in range(micros)
    ]

    inputs = layer_input[:, 0].astype(F32).reshape(micros * rows, depth)
    normed_one, factor_one, hidden = normalize(inputs, gain_one)
    qkv = project(
        hidden, packed, bias, jnp.tile(cosine, (micros, 1)), jnp.tile(sine, (micros, 1))
    )
    infos = [jnp.stack([lengths[m, 0], offset]) for m in range(micros)]

    all_kv, attended, logs, mixed, norm_two, full_hidden = [], [], [], [], [], []
    for m in range(micros):
        all_kv.append(
            lax.all_gather(qkv[m * rows : (m + 1) * rows, QW:], "tensor", axis=0, tiled=True)
        )
    for m in range(micros):
        out, log = attend(infos[m], m, qkv, all_kv[m], rows)
        attended.append(out)
        logs.append(log)
        mixed.append(inputs[m * rows : (m + 1) * rows] + dot(out, wout))
        normed, factor, hidden_two = normalize(mixed[m], gain_two)
        norm_two.append((normed, factor))
        full_hidden.append(lax.all_gather(hidden_two, "tensor", axis=0, tiled=True))

    acc_gate = acc_up = acc_down = 0.0
    out_parts, grad_mixed, gain_two_grads = [], [], []
    for m in range(micros):
        full = full_hidden[m]
        gate = dot(full, gate_proj)
        up = dot(full, up_proj)
        grad_activ = dot_t(full_grads[m], down_proj)
        sigma = jax.nn.sigmoid(gate)
        silu_gate = gate * sigma
        activ = (silu_gate * up).astype(B16)
        grad_gate = (grad_activ * up * sigma * (1.0 + gate * (1.0 - sigma))).astype(B16)
        grad_up = (grad_activ * silu_gate).astype(B16)
        grad_two = (dot_t(grad_gate, gate_proj) + dot_t(grad_up, up_proj)).astype(B16)
        grad_two = rows_scatter(grad_two, rows)
        out_parts.append(dot(activ, down_proj).astype(B16))
        acc_down = acc_down + t_dot(activ, full_grads[m])
        acc_gate = acc_gate + t_dot(full, grad_gate)
        acc_up = acc_up + t_dot(full, grad_up)
        normed, factor = norm_two[m]
        grad, gain_grad = norm_back(grad_two, normed, factor, gain_two)
        gain_two_grads.append(gain_grad)
        grad_mixed.append(grad + grad_rows[m])

    down_total = lax.psum(acc_down.astype(B16), "dp").astype(F32)
    gate_total = lax.psum(acc_gate.astype(B16), "dp").astype(F32)
    up_total = lax.psum(acc_up.astype(B16), "dp").astype(F32)

    grad_low = jnp.concatenate(grad_mixed, axis=0).astype(B16)
    acc_out = t_dot(jnp.concatenate(attended, axis=0), grad_low).astype(B16)
    grad_q, grad_kv = [], []
    for m in range(micros):
        grad_attended = dot_t(grad_low[m * rows : (m + 1) * rows], wout).astype(B16)
        dq, dk, dv = attend_back(
            infos[m], m, qkv, all_kv[m], grad_attended, logs[m], cosine, sine, rows
        )
        grad_q.append(dq)
        summed = rows_scatter(jnp.concatenate([dk, dv], axis=1), rows)
        heads = summed[:, :KW].reshape(rows, KV, HD)
        turned = jnp.concatenate([heads[..., HD // 2 :], heads[..., : HD // 2]], axis=-1)
        heads = heads * cosine[:, None, :] - turned * sine[:, None, :]
        grad_kv.append(
            jnp.concatenate([heads.reshape(rows, KW), summed[:, KW:]], axis=1).astype(B16)
        )
    grad_qkv = jnp.concatenate(
        [jnp.concatenate(grad_q, axis=0), jnp.concatenate(grad_kv, axis=0)], axis=1
    )
    grad_hidden = dot_t(grad_qkv, wqkv)
    grad_in, gain_one_grad = norm_back(grad_hidden, normed_one, factor_one, gain_one)
    grad_bias = jnp.sum(grad_qkv.astype(F32), axis=0)
    acc_qkv = t_dot(hidden, grad_qkv).astype(B16)
    tails = jnp.concatenate(
        [
            grad_bias[QW : QW + KW].reshape(devices, small),
            grad_bias[QW + KW :].reshape(devices, small),
            jnp.zeros((devices, size - 2 * small), F32),
        ],
        axis=1,
    ).reshape(-1)
    columns = jnp.stack([gain_one_grad, grad_bias[:QW], sum(gain_two_grads), tails], axis=1)
    columns = jnp.pad(columns.astype(B16), ((0, 0), (0, EXTRA - 4)))
    grad_out = scatter_weights(acc_out)
    grad_packed = scatter_weights(jnp.concatenate([acc_qkv, columns], axis=1))

    layer_output = jnp.stack(
        [
            (mixed[m] + rows_scatter(out_parts[m], rows)).astype(B16)
            for m in range(micros)
        ]
    )[:, None]
    grad_input = (grad_in + jnp.concatenate(grad_mixed, axis=0)).reshape(micros, 1, rows, depth)
    return (
        layer_output,
        grad_input,
        grad_packed[:, QKV],
        grad_packed[:, :QW],
        grad_packed[:, QKV + 1],
        grad_packed[:, QW : QW + KW],
        grad_packed[:small, QKV + 3],
        grad_packed[:, QW + KW : QKV],
        grad_packed[small : 2 * small, QKV + 3],
        grad_out,
        grad_packed[:, QKV + 2],
        gate_total,
        up_total,
        down_total,
    )


def solution(mesh):
    rows = P(None, "dp", "tensor", None)
    both = P(("dp", "tensor"))
    wide = P(("dp", "tensor"), None)
    placed = (
        rows,
        P(None, "dp"),
        both,
        wide,
        both,
        wide,
        both,
        wide,
        both,
        wide,
        both,
        P(None, "tensor"),
        P(None, "tensor"),
        P("tensor", None),
        rows,
    )
    return jax.shard_map(
        on_device,
        mesh=mesh,
        in_specs=placed,
        out_specs=(
            rows,
            rows,
            both,
            wide,
            both,
            wide,
            both,
            wide,
            both,
            wide,
            both,
            P(None, "tensor"),
            P(None, "tensor"),
            P("tensor", None),
        ),
        check_vma=False,
    )
```

```python
import functools

import jax
import jax.numpy as jnp
from jax import lax
from jax.experimental import pallas as pl
from jax.experimental.pallas import tpu as pltpu
from jax.sharding import PartitionSpec as P

H = 12
KV = 2
HD = 128
GROUPS = H // KV
QW = H * HD
KW = KV * HD
QKV = QW + 2 * KW
EXTRA = 128

ROPE_BASE = 1000000.0
EPS = 1e-06
MASKED = -1e30
F32 = jnp.float32
B16 = jnp.bfloat16
VMEM_LIMIT = 56 * 1024 * 1024
MESH = pl.DeviceIdType.MESH


def dot(a, b):
    return jnp.dot(a, b, preferred_element_type=F32)


def dot_t(a, b):
    return lax.dot_general(a, b, (((1,), (1,)), ((), ())), preferred_element_type=F32)


def t_dot(a, b):
    return lax.dot_general(a, b, (((0,), (0,)), ((), ())), preferred_element_type=F32)


def rope_tables(positions):
    half = HD // 2
    freqs = ROPE_BASE ** (-(jnp.arange(half, dtype=F32) * 2.0 / HD))
    angles = positions.astype(F32)[:, None] * freqs[None, :]
    cosine = jnp.cos(angles)
    sine = jnp.sin(angles)
    return (
        jnp.concatenate([cosine, cosine], axis=1),
        jnp.concatenate([-sine, sine], axis=1),
    )


def swap(value, axis, bit):
    count = lax.axis_size(axis)
    return lax.ppermute(value, axis, [(i, i ^ bit) for i in range(count)])


def pick(value, index, axis=0):
    return lax.dynamic_index_in_dim(value, index, axis, keepdims=False)


def line_scatter(part, chips, place):
    count = 2 * chips
    left = right = None
    for step in range(1, chips):
        ahead = part(jnp.minimum(place + chips - step, chips - 1))
        behind = part(jnp.maximum(place - chips + step, 0))
        if left is not None:
            ahead = ahead + left.astype(F32)
            behind = behind + right.astype(F32)
        left = lax.ppermute(
            ahead.astype(B16), "tensor", [(i, i + 2) for i in range(2 * step)]
        )
        right = lax.ppermute(
            behind.astype(B16),
            "tensor",
            [(count - 1 - i, count - 3 - i) for i in range(2 * step)],
        )
    return part(place) + left.astype(F32) + right.astype(F32)


def rows_scatter(partial, rows):
    chips = lax.axis_size("tensor") // 2
    place = lax.axis_index("tensor")
    chip, core = place // 2, place % 2
    width = partial.shape[-1]
    blocks = partial.reshape(chips, 2, rows, width)
    got = swap(pick(blocks, 1 - core, 1), "tensor", 1)

    def part(index):
        own = lax.dynamic_slice(blocks, (index, core, 0, 0), (1, 1, rows, width))
        return own[0, 0].astype(F32) + pick(got, index).astype(F32)

    return line_scatter(part, chips, chip)


def nearest(chips, place, step):
    found = 0
    for here in range(chips):
        order = sorted(range(chips), key=lambda there: abs(there - here))
        found = found + jnp.where(place == here, order[step], 0)
    return found


class Spot:
    def __init__(self):
        self.chips = lax.axis_size("tensor") // 2
        dp, tensor = lax.axis_index("dp"), lax.axis_index("tensor")
        self.dp, self.tensor = dp, tensor
        self.row, self.col = dp // 2, dp % 2
        self.chip, self.core = tensor // 2, tensor % 2
        self.over_x = (self.row * 2 + 1 - self.col, tensor)
        self.over_y = ((1 - self.row) * 2 + self.col, tensor)
        self.beside = (dp, self.chip * 2 + 1 - self.core)
        self.left = (dp, jnp.maximum(tensor - 2, 0))
        self.right = (dp, jnp.minimum(tensor + 2, 2 * self.chips - 1))

    def on_line(self, chip):
        return (self.dp, chip * 2 + self.core)

    def index(self, row, col, chip, core):
        return ((row * 2 + col) * self.chips + chip) * 2 + core


def greet(spot, plane, line):
    barrier = pltpu.get_barrier_semaphore()
    peers = [spot.beside] + ([spot.over_x, spot.over_y] if plane else [])
    for peer in peers:
        pl.semaphore_signal(barrier, inc=1, device_id=peer, device_id_type=MESH)
    count = len(peers)
    if line == "all":
        for chip in range(spot.chips):

            @pl.when(spot.chip != chip)
            def _():
                pl.semaphore_signal(barrier, inc=1, device_id=spot.on_line(chip), device_id_type=MESH)

        count = count + spot.chips - 1
    else:
        has_left, has_right = spot.chip > 0, spot.chip < spot.chips - 1

        @pl.when(has_left)
        def _():
            pl.semaphore_signal(barrier, inc=1, device_id=spot.left, device_id_type=MESH)

        @pl.when(has_right)
        def _():
            pl.semaphore_signal(barrier, inc=1, device_id=spot.right, device_id_type=MESH)

        count = count + jnp.where(has_left, 1, 0) + jnp.where(has_right, 1, 0)
    pl.semaphore_wait(barrier, count)


def remote(src, dst, send_sem, recv_sem, device):
    return pltpu.make_async_remote_copy(
        src_ref=src,
        dst_ref=dst,
        send_sem=send_sem,
        recv_sem=recv_sem,
        device_id=device,
        device_id_type=MESH,
    )


def gather_kernel(block_ref, whole_ref, local_sem, send_sem, recv_sem):
    spot = Spot()
    chips, chip, core, row, col = spot.chips, spot.chip, spot.core, spot.row, spot.col
    cut = chips // 2
    own = spot.index(row, col, chip, core)
    local = pltpu.make_async_copy(block_ref, whole_ref.at[own], local_sem)
    local.start()
    greet(spot, True, "near")
    local.wait()
    sent = []

    def send(index, device, when=None):
        copy = remote(
            whole_ref.at[index], whole_ref.at[index], send_sem.at[len(sent)], recv_sem.at[index], device
        )
        sent.append((copy, when))
        if when is None:
            copy.start()
        else:
            pl.when(when)(copy.start)

    def arrive(index):
        remote(
            whole_ref.at[index], whole_ref.at[index], send_sem.at[0], recv_sem.at[index], spot.beside
        ).wait_recv()

    order = [nearest(chips, chip, step) for step in range(chips)]
    for step, there in enumerate(order):
        index = spot.index(row, col, there, core)
        if step:
            arrive(index)
        send(index, spot.right, (there <= chip) & (chip < chips - 1))
        send(index, spot.left, (there >= chip) & (chip > 0))
        send(index, spot.over_x)
        send(index, spot.over_y)
        send(index, spot.beside)
    for there in order:
        index = spot.index(row, 1 - col, there, core)
        arrive(index)
        send(index, spot.over_y, there < cut)
        send(index, spot.beside)
        index = spot.index(1 - row, col, there, core)
        arrive(index)
        send(index, spot.over_x, there >= cut)
        send(index, spot.beside)
    for there in order:
        index = spot.index(1 - row, 1 - col, there, core)
        arrive(index)
        send(index, spot.beside)
    for plane in range(4):
        for there in range(chips):
            arrive(spot.index(plane // 2, plane % 2, there, 1 - core))
    for copy, when in sent:
        if when is None:
            copy.wait_send()
        else:
            pl.when(when)(copy.wait_send)


def gather_weights(block, collective_id):
    size, width = block.shape
    devices = lax.axis_size(("dp", "tensor"))
    if lax.axis_size("dp") != 4:
        return lax.all_gather(block, ("dp", "tensor"), axis=0, tiled=True)
    chips = lax.axis_size("tensor") // 2
    whole = pl.pallas_call(
        gather_kernel,
        in_specs=[pl.BlockSpec(memory_space=pl.ANY)],
        out_specs=pl.BlockSpec(memory_space=pl.ANY),
        out_shape=jax.ShapeDtypeStruct((devices, size, width), B16),
        scratch_shapes=[
            pltpu.SemaphoreType.DMA,
            pltpu.SemaphoreType.DMA((10 * chips,)),
            pltpu.SemaphoreType.DMA((devices,)),
        ],
        compiler_params=pltpu.CompilerParams(
            collective_id=collective_id, has_side_effects=True, vmem_limit_bytes=VMEM_LIMIT
        ),
        cost_estimate=pl.CostEstimate(flops=0, bytes_accessed=devices * size * width * 8, transcendentals=0),
    )(block)
    return whole.reshape(devices * size, width)


def scatter_kernel(
    grads_ref, out_ref, mine, got, over_x, over_y, across_x, across_y, line, load_sem, send_sem, recv_sem
):
    spot = Spot()
    chips, chip, core, row, col = spot.chips, spot.chip, spot.core, spot.row, spot.col
    cut = chips // 2
    load = pltpu.make_async_copy(grads_ref.at[:, core], mine, load_sem)
    load.start()
    greet(spot, True, "all")
    swap_copy = remote(grads_ref.at[:, 1 - core], got, send_sem.at[0], recv_sem.at[0], spot.beside)
    swap_copy.start()
    load.wait()
    swap_copy.wait()

    def add(target, start, source, first, count):
        def body(step, _):
            target[start + step] = (
                target[start + step].astype(F32) + source[first + step].astype(F32)
            ).astype(B16)
            return 0

        lax.fori_loop(0, count, body, 0)

    add(mine, 0, got, 0, 4 * chips)

    def at(r, c, z):
        return (r * 2 + c) * chips + z

    copies = []
    for side in range(2):
        copies.append(
            remote(
                mine.at[pl.ds(at(side, 1 - col, 0), cut)],
                over_x.at[pl.ds(side * cut, cut)],
                send_sem.at[1 + side],
                recv_sem.at[1 + side],
                spot.over_x,
            )
        )
        copies.append(
            remote(
                mine.at[pl.ds(at(1 - row, side, cut), chips - cut)],
                over_y.at[pl.ds(side * (chips - cut), chips - cut)],
                send_sem.at[3 + side],
                recv_sem.at[3 + side],
                spot.over_y,
            )
        )
    for copy in copies:
        copy.start()
    for copy in copies:
        copy.wait()
    for side in range(2):
        add(mine, at(side, col, 0), over_x, side * cut, cut)
        add(mine, at(row, side, cut), over_y, side * (chips - cut), chips - cut)
    copies = [
        remote(
            mine.at[pl.ds(at(1 - row, col, 0), cut)], across_y, send_sem.at[5], recv_sem.at[5], spot.over_y
        ),
        remote(
            mine.at[pl.ds(at(row, 1 - col, cut), chips - cut)],
            across_x,
            send_sem.at[6],
            recv_sem.at[6],
            spot.over_x,
        ),
    ]
    for copy in copies:
        copy.start()
    for copy in copies:
        copy.wait()
    add(mine, at(row, col, 0), across_y, 0, cut)
    add(mine, at(row, col, cut), across_x, 0, chips - cut)

    def to(other):
        return remote(
            mine.at[at(row, col, other)],
            line.at[chip],
            send_sem.at[7 + other],
            recv_sem.at[7 + chip],
            spot.on_line(other),
        )

    for other in range(chips):
        pl.when(chip != other)(to(other).start)
    total = mine[at(row, col, chip)].astype(F32)
    line[chip] = jnp.zeros(line.shape[1:], B16)
    for other in range(chips):

        @pl.when(chip != other)
        def _():
            remote(
                line.at[other], line.at[other], send_sem.at[7 + other], recv_sem.at[7 + other], spot.on_line(other)
            ).wait_recv()

        total = total + line[other].astype(F32)
    out_ref[...] = total
    for other in range(chips):
        pl.when(chip != other)(to(other).wait_send)


def scatter_weights(grads, collective_id):
    total, width = grads.shape
    devices = lax.axis_size(("dp", "tensor"))
    size = total // devices
    if lax.axis_size("dp") != 4:
        return lax.psum_scatter(grads, ("dp", "tensor"), scatter_dimension=0, tiled=True).astype(F32)
    chips = lax.axis_size("tensor") // 2
    cut = chips // 2
    return pl.pallas_call(
        scatter_kernel,
        in_specs=[pl.BlockSpec(memory_space=pl.ANY)],
        out_specs=pl.BlockSpec(memory_space=pltpu.VMEM),
        out_shape=jax.ShapeDtypeStruct((size, width), F32),
        scratch_shapes=[
            pltpu.VMEM((4 * chips, size, width), B16),
            pltpu.VMEM((4 * chips, size, width), B16),
            pltpu.VMEM((2 * cut, size, width), B16),
            pltpu.VMEM((2 * (chips - cut), size, width), B16),
            pltpu.VMEM((chips - cut, size, width), B16),
            pltpu.VMEM((cut, size, width), B16),
            pltpu.VMEM((chips, size, width), B16),
            pltpu.SemaphoreType.DMA,
            pltpu.SemaphoreType.DMA((7 + chips,)),
            pltpu.SemaphoreType.DMA((7 + chips,)),
        ],
        compiler_params=pltpu.CompilerParams(
            collective_id=collective_id, has_side_effects=True, vmem_limit_bytes=VMEM_LIMIT
        ),
        cost_estimate=pl.CostEstimate(flops=0, bytes_accessed=devices * size * width * 8, transcendentals=0),
    )(grads.reshape(devices // 2, 2, size, width))


def project_kernel(hidden_ref, weight_ref, bias_ref, cos_ref, sin_ref, out_ref):
    chunk = pl.program_id(0)
    turned = chunk < (QW + KW) // 256
    lin = dot(hidden_ref[...], weight_ref[...]) + bias_ref[...]
    for head in range(2):
        cut = pl.ds(head * HD, HD)
        one = lin[:, head * HD : (head + 1) * HD]
        rot = one * cos_ref[...] + pltpu.roll(one, HD // 2, 1) * sin_ref[...]
        out_ref[:, cut] = jnp.where(turned, rot, one).astype(B16)


def project(hidden, weights, bias, cosine, sine):
    rows, depth = hidden.shape
    return pl.pallas_call(
        project_kernel,
        grid=(QKV // 256,),
        in_specs=[
            pl.BlockSpec((rows, depth), lambda j: (0, 0)),
            pl.BlockSpec((depth, 256), lambda j: (0, j)),
            pl.BlockSpec((1, 256), lambda j: (0, j)),
            pl.BlockSpec((rows, HD), lambda j: (0, 0)),
            pl.BlockSpec((rows, HD), lambda j: (0, 0)),
        ],
        out_specs=pl.BlockSpec((rows, 256), lambda j: (0, j)),
        out_shape=jax.ShapeDtypeStruct((rows, QKV), B16),
        compiler_params=pltpu.CompilerParams(vmem_limit_bytes=VMEM_LIMIT),
        cost_estimate=pl.CostEstimate(
            flops=2 * rows * depth * QKV,
            bytes_accessed=2 * (depth * QKV + rows * depth + rows * QKV),
            transcendentals=0,
        ),
    )(hidden, weights, bias, cosine, sine)


def fill_bias(info_ref, bias):
    shape = bias.shape
    place = info_ref[1] + lax.broadcasted_iota(jnp.int32, shape, 0)
    keys = lax.broadcasted_iota(jnp.int32, shape, 1)
    bias[...] = jnp.where((keys <= place) & (keys < info_ref[0]), 0.0, MASKED)


def attend_kernel(info_ref, q_ref, k_ref, v_ref, out_ref, log_ref, bias):
    @pl.when(pl.program_id(0) == 0)
    def _():
        fill_bias(info_ref, bias)

    scores = dot_t(q_ref[...], k_ref[...]) * (HD**-0.5) + bias[...]
    top = jnp.max(scores, axis=-1, keepdims=True)
    expd = jnp.exp(scores - top)
    summed = jnp.sum(expd, axis=-1, keepdims=True)
    probs = (expd * (1.0 / summed)).astype(B16)
    out_ref[...] = dot(probs, v_ref[...]).astype(B16)
    log_ref[...] = jnp.broadcast_to(top + jnp.log(summed), log_ref.shape)


def attend(info, micro, qkv, keys_values, rows):
    total = keys_values.shape[0]
    return pl.pallas_call(
        attend_kernel,
        grid_spec=pltpu.PrefetchScalarGridSpec(
            num_scalar_prefetch=1,
            grid=(H,),
            in_specs=[
                pl.BlockSpec((rows, HD), lambda h, info: (micro, h)),
                pl.BlockSpec((total, HD), lambda h, info: (0, h // GROUPS)),
                pl.BlockSpec((total, HD), lambda h, info: (0, KV + h // GROUPS)),
            ],
            out_specs=[
                pl.BlockSpec((rows, HD), lambda h, info: (0, h)),
                pl.BlockSpec((rows, HD), lambda h, info: (0, h)),
            ],
            scratch_shapes=[pltpu.VMEM((rows, total), F32)],
        ),
        out_shape=[
            jax.ShapeDtypeStruct((rows, QW), B16),
            jax.ShapeDtypeStruct((rows, QW), F32),
        ],
        compiler_params=pltpu.CompilerParams(vmem_limit_bytes=VMEM_LIMIT),
        cost_estimate=pl.CostEstimate(
            flops=8 * rows * total * QW,
            bytes_accessed=4 * total * KW + 8 * rows * QW,
            transcendentals=H * rows * total,
        ),
    )(info, qkv, keys_values, keys_values)


def attend_back_kernel(
    info_ref, q_ref, k_ref, v_ref, g_ref, log_ref, cos_ref, sin_ref, dq_ref, dk_ref, dv_ref, bias, dk_acc, dv_acc
):
    head = pl.program_id(0)

    @pl.when(head == 0)
    def _():
        fill_bias(info_ref, bias)

    scale = HD**-0.5
    queries, keys, values, grads = q_ref[...], k_ref[...], v_ref[...], g_ref[...]
    scores = dot_t(queries, keys) * scale + bias[...]
    probs = jnp.exp(scores - log_ref[:, :1])
    grad_probs = dot_t(grads, values)
    inner = jnp.sum(grad_probs * probs, axis=-1, keepdims=True)
    grad_scores = (probs * (grad_probs - inner)).astype(B16)
    grad_q = dot(grad_scores, keys) * scale
    turned = grad_q * cos_ref[...] - pltpu.roll(grad_q, HD // 2, 1) * sin_ref[...]
    dq_ref[...] = turned.astype(B16)
    grad_k = t_dot(grad_scores, queries) * scale
    grad_v = t_dot(probs.astype(B16), grads)
    first = lax.rem(head, GROUPS) == 0

    @pl.when(first)
    def _():
        dk_acc[...] = grad_k
        dv_acc[...] = grad_v

    @pl.when(jnp.logical_not(first))
    def _():
        dk_acc[...] += grad_k
        dv_acc[...] += grad_v

    @pl.when(lax.rem(head, GROUPS) == GROUPS - 1)
    def _():
        dk_ref[...] = dk_acc[...].astype(B16)
        dv_ref[...] = dv_acc[...].astype(B16)


def attend_back(info, micro, qkv, keys_values, grads, logs, cosine, sine, rows):
    total = keys_values.shape[0]
    return pl.pallas_call(
        attend_back_kernel,
        grid_spec=pltpu.PrefetchScalarGridSpec(
            num_scalar_prefetch=1,
            grid=(H,),
            in_specs=[
                pl.BlockSpec((rows, HD), lambda h, info: (micro, h)),
                pl.BlockSpec((total, HD), lambda h, info: (0, h // GROUPS)),
                pl.BlockSpec((total, HD), lambda h, info: (0, KV + h // GROUPS)),
                pl.BlockSpec((rows, HD), lambda h, info: (0, h)),
                pl.BlockSpec((rows, HD), lambda h, info: (0, h)),
                pl.BlockSpec((rows, HD), lambda h, info: (0, 0)),
                pl.BlockSpec((rows, HD), lambda h, info: (0, 0)),
            ],
            out_specs=[
                pl.BlockSpec((rows, HD), lambda h, info: (0, h)),
                pl.BlockSpec((total, HD), lambda h, info: (0, h // GROUPS)),
                pl.BlockSpec((total, HD), lambda h, info: (0, h // GROUPS)),
            ],
            scratch_shapes=[
                pltpu.VMEM((rows, total), F32),
                pltpu.VMEM((total, HD), F32),
                pltpu.VMEM((total, HD), F32),
            ],
        ),
        out_shape=[
            jax.ShapeDtypeStruct((rows, QW), B16),
            jax.ShapeDtypeStruct((total, KW), B16),
            jax.ShapeDtypeStruct((total, KW), B16),
        ],
        compiler_params=pltpu.CompilerParams(vmem_limit_bytes=VMEM_LIMIT),
        cost_estimate=pl.CostEstimate(
            flops=20 * rows * total * QW,
            bytes_accessed=8 * total * KW + 12 * rows * QW,
            transcendentals=H * rows * total,
        ),
    )(info, qkv, keys_values, keys_values, grads, logs, cosine, sine)


def norm_back(grad_out, normed, factor, gain):
    inner = grad_out * gain
    grad_rows = factor * (inner - normed * jnp.mean(inner * normed, axis=-1, keepdims=True))
    return (grad_rows, jnp.sum(grad_out * normed, axis=0))


def normalize(rows, gain):
    factor = lax.rsqrt(jnp.mean(rows * rows, axis=-1, keepdims=True) + EPS)
    normed = rows * factor
    return (normed, factor, (normed * gain).astype(B16))


def on_device(
    layer_input,
    lengths,
    attn_gain,
    query_proj,
    query_bias,
    key_proj,
    key_bias,
    value_proj,
    value_bias,
    out_proj,
    mlp_gain,
    gate_proj,
    up_proj,
    down_proj,
    cotangent,
):
    micros = layer_input.shape[0]
    rows = layer_input.shape[2]
    depth = layer_input.shape[3]
    tensor = lax.axis_index("tensor")
    total = rows * lax.axis_size("tensor")
    devices = lax.axis_size(("dp", "tensor"))
    size = query_proj.shape[0]
    small = key_bias.shape[0]
    offset = tensor * rows
    positions = offset + jnp.arange(rows, dtype=jnp.int32)
    cosine, sine = rope_tables(positions)

    extra = jnp.zeros((size, EXTRA), B16)
    extra = extra.at[:, 0].set(attn_gain).at[:, 1].set(query_bias).at[:, 2].set(mlp_gain)
    extra = extra.at[:small, 3].set(key_bias).at[small : 2 * small, 3].set(value_bias)
    packed = gather_weights(
        jnp.concatenate([query_proj, key_proj, value_proj, extra], axis=1), 0
    )
    wout = gather_weights(out_proj, 1)
    vectors = packed[:, QKV : QKV + 4].astype(F32)
    gain_one, gain_two = vectors[:, 0], vectors[:, 2]
    tails = vectors[:, 3].reshape(devices, size)
    bias = jnp.concatenate(
        [vectors[:, 1], tails[:, :small].reshape(-1), tails[:, small : 2 * small].reshape(-1)]
    )[None, :]
    wqkv = packed[:, :QKV]

    valid = (positions[None, :] < lengths).astype(F32)[:, :, None]
    grad_rows = cotangent[:, 0].astype(F32) * valid
    full_grads = [
        lax.all_gather(grad_rows[m].astype(B16), "tensor", axis=0, tiled=True) for m in range(micros)
    ]

    inputs = layer_input[:, 0].astype(F32).reshape(micros * rows, depth)
    normed_one, factor_one, hidden = normalize(inputs, gain_one)
    qkv = project(
        hidden, packed, bias, jnp.tile(cosine, (micros, 1)), jnp.tile(sine, (micros, 1))
    )
    infos = [jnp.stack([lengths[m, 0], offset]) for m in range(micros)]

    all_kv, attended, logs, mixed, norm_two, full_hidden = [], [], [], [], [], []
    for m in range(micros):
        all_kv.append(
            lax.all_gather(qkv[m * rows : (m + 1) * rows, QW:], "tensor", axis=0, tiled=True)
        )
    for m in range(micros):
        out, log = attend(infos[m], m, qkv, all_kv[m], rows)
        attended.append(out)
        logs.append(log)
        mixed.append(inputs[m * rows : (m + 1) * rows] + dot(out, wout))
        normed, factor, hidden_two = normalize(mixed[m], gain_two)
        norm_two.append((normed, factor))
        full_hidden.append(lax.all_gather(hidden_two, "tensor", axis=0, tiled=True))

    acc_gate = acc_up = acc_down = 0.0
    out_parts, grad_mixed, gain_two_grads = [], [], []
    for m in range(micros):
        full = full_hidden[m]
        gate = dot(full, gate_proj)
        up = dot(full, up_proj)
        grad_activ = dot_t(full_grads[m], down_proj)
        sigma = jax.nn.sigmoid(gate)
        silu_gate = gate * sigma
        activ = (silu_gate * up).astype(B16)
        grad_gate = (grad_activ * up * sigma * (1.0 + gate * (1.0 - sigma))).astype(B16)
        grad_up = (grad_activ * silu_gate).astype(B16)
        grad_two = (dot_t(grad_gate, gate_proj) + dot_t(grad_up, up_proj)).astype(B16)
        grad_two = rows_scatter(grad_two, rows)
        out_parts.append(dot(activ, down_proj).astype(B16))
        acc_down = acc_down + t_dot(activ, full_grads[m])
        acc_gate = acc_gate + t_dot(full, grad_gate)
        acc_up = acc_up + t_dot(full, grad_up)
        normed, factor = norm_two[m]
        grad, gain_grad = norm_back(grad_two, normed, factor, gain_two)
        gain_two_grads.append(gain_grad)
        grad_mixed.append(grad + grad_rows[m])

    down_total = lax.psum(acc_down.astype(B16), "dp").astype(F32)
    gate_total = lax.psum(acc_gate.astype(B16), "dp").astype(F32)
    up_total = lax.psum(acc_up.astype(B16), "dp").astype(F32)

    grad_low = jnp.concatenate(grad_mixed, axis=0).astype(B16)
    acc_out = t_dot(jnp.concatenate(attended, axis=0), grad_low).astype(B16)
    grad_q, grad_kv = [], []
    for m in range(micros):
        grad_attended = dot_t(grad_low[m * rows : (m + 1) * rows], wout).astype(B16)
        dq, dk, dv = attend_back(
            infos[m], m, qkv, all_kv[m], grad_attended, logs[m], cosine, sine, rows
        )
        grad_q.append(dq)
        summed = rows_scatter(jnp.concatenate([dk, dv], axis=1), rows)
        heads = summed[:, :KW].reshape(rows, KV, HD)
        turned = jnp.concatenate([heads[..., HD // 2 :], heads[..., : HD // 2]], axis=-1)
        heads = heads * cosine[:, None, :] - turned * sine[:, None, :]
        grad_kv.append(
            jnp.concatenate([heads.reshape(rows, KW), summed[:, KW:]], axis=1).astype(B16)
        )
    grad_qkv = jnp.concatenate(
        [jnp.concatenate(grad_q, axis=0), jnp.concatenate(grad_kv, axis=0)], axis=1
    )
    grad_hidden = dot_t(grad_qkv, wqkv)
    grad_in, gain_one_grad = norm_back(grad_hidden, normed_one, factor_one, gain_one)
    grad_bias = jnp.sum(grad_qkv.astype(F32), axis=0)
    acc_qkv = t_dot(hidden, grad_qkv).astype(B16)
    tails = jnp.concatenate(
        [
            grad_bias[QW : QW + KW].reshape(devices, small),
            grad_bias[QW + KW :].reshape(devices, small),
            jnp.zeros((devices, size - 2 * small), F32),
        ],
        axis=1,
    ).reshape(-1)
    columns = jnp.stack([gain_one_grad, grad_bias[:QW], sum(gain_two_grads), tails], axis=1)
    columns = jnp.pad(columns.astype(B16), ((0, 0), (0, EXTRA - 4)))
    grad_out = scatter_weights(acc_out, 2)
    grad_packed = scatter_weights(jnp.concatenate([acc_qkv, columns], axis=1), 3)

    layer_output = jnp.stack(
        [
            (mixed[m] + rows_scatter(out_parts[m], rows)).astype(B16)
            for m in range(micros)
        ]
    )[:, None]
    grad_input = (grad_in + jnp.concatenate(grad_mixed, axis=0)).reshape(micros, 1, rows, depth)
    return (
        layer_output,
        grad_input,
        grad_packed[:, QKV],
        grad_packed[:, :QW],
        grad_packed[:, QKV + 1],
        grad_packed[:, QW : QW + KW],
        grad_packed[:small, QKV + 3],
        grad_packed[:, QW + KW : QKV],
        grad_packed[small : 2 * small, QKV + 3],
        grad_out,
        grad_packed[:, QKV + 2],
        gate_total,
        up_total,
        down_total,
    )


def solution(mesh):
    rows = P(None, "dp", "tensor", None)
    both = P(("dp", "tensor"))
    wide = P(("dp", "tensor"), None)
    placed = (
        rows,
        P(None, "dp"),
        both,
        wide,
        both,
        wide,
        both,
        wide,
        both,
        wide,
        both,
        P(None, "tensor"),
        P(None, "tensor"),
        P("tensor", None),
        rows,
    )
    return jax.shard_map(
        on_device,
        mesh=mesh,
        in_specs=placed,
        out_specs=(
            rows,
            rows,
            both,
            wide,
            both,
            wide,
            both,
            wide,
            both,
            wide,
            both,
            P(None, "tensor"),
            P(None, "tensor"),
            P("tensor", None),
        ),
        check_vma=False,
    )
```

```python
import functools

import jax
import jax.numpy as jnp
from jax import lax
from jax.experimental import pallas as pl
from jax.experimental.pallas import tpu as pltpu
from jax.sharding import PartitionSpec as P

H = 12
KV = 2
HD = 128
GROUPS = H // KV
QW = H * HD
KW = KV * HD
QKV = QW + 2 * KW
EXTRA = 128

ROPE_BASE = 1000000.0
EPS = 1e-06
MASKED = -1e30
F32 = jnp.float32
B16 = jnp.bfloat16
VMEM_LIMIT = 56 * 1024 * 1024
VMEM_MOST = 60 * 1024 * 1024
CHUNK = 256
SCATTER_LANES = 1024
MESH = pl.DeviceIdType.MESH


def dot(a, b):
    return jnp.dot(a, b, preferred_element_type=F32)


def dot_t(a, b):
    return lax.dot_general(a, b, (((1,), (1,)), ((), ())), preferred_element_type=F32)


def t_dot(a, b):
    return lax.dot_general(a, b, (((0,), (0,)), ((), ())), preferred_element_type=F32)


def rope_tables(positions):
    half = HD // 2
    freqs = ROPE_BASE ** (-(jnp.arange(half, dtype=F32) * 2.0 / HD))
    angles = positions.astype(F32)[:, None] * freqs[None, :]
    cosine = jnp.cos(angles)
    sine = jnp.sin(angles)
    return (
        jnp.concatenate([cosine, cosine], axis=1),
        jnp.concatenate([-sine, sine], axis=1),
    )


def swap(value, axis, bit):
    count = lax.axis_size(axis)
    return lax.ppermute(value, axis, [(i, i ^ bit) for i in range(count)])


def nearest(chips, place, step):
    found = 0
    for here in range(chips):
        for at, there in enumerate(sorted(range(chips), key=lambda there: abs(there - here))):
            found = found + jnp.where((place == here) & (step == at), there, 0)
    return found


class Spot:
    def __init__(self):
        self.chips = lax.axis_size("tensor") // 2
        dp, tensor = lax.axis_index("dp"), lax.axis_index("tensor")
        self.dp, self.tensor = dp, tensor
        self.row, self.col = dp // 2, dp % 2
        self.chip, self.core = tensor // 2, tensor % 2
        self.over_x = (self.row * 2 + 1 - self.col, tensor)
        self.over_y = ((1 - self.row) * 2 + self.col, tensor)
        self.beside = (dp, self.chip * 2 + 1 - self.core)
        self.left = (dp, jnp.maximum(tensor - 2, 0))
        self.right = (dp, jnp.minimum(tensor + 2, 2 * self.chips - 1))

    def on_line(self, chip):
        return (self.dp, chip * 2 + self.core)

    def index(self, row, col, chip, core):
        return ((row * 2 + col) * self.chips + chip) * 2 + core


def greet(spot, plane, line):
    barrier = pltpu.get_barrier_semaphore()
    peers = [spot.beside] + ([spot.over_x, spot.over_y] if plane else [])
    for peer in peers:
        pl.semaphore_signal(barrier, inc=1, device_id=peer, device_id_type=MESH)
    count = len(peers)
    if line == "all":
        for chip in range(spot.chips):

            @pl.when(spot.chip != chip)
            def _():
                pl.semaphore_signal(barrier, inc=1, device_id=spot.on_line(chip), device_id_type=MESH)

        count = count + spot.chips - 1
    elif line == "near":
        has_left, has_right = spot.chip > 0, spot.chip < spot.chips - 1

        @pl.when(has_left)
        def _():
            pl.semaphore_signal(barrier, inc=1, device_id=spot.left, device_id_type=MESH)

        @pl.when(has_right)
        def _():
            pl.semaphore_signal(barrier, inc=1, device_id=spot.right, device_id_type=MESH)

        count = count + jnp.where(has_left, 1, 0) + jnp.where(has_right, 1, 0)
    pl.semaphore_wait(barrier, count)


def remote(src, dst, send_sem, recv_sem, device):
    return pltpu.make_async_remote_copy(
        src_ref=src,
        dst_ref=dst,
        send_sem=send_sem,
        recv_sem=recv_sem,
        device_id=device,
        device_id_type=MESH,
    )


class Line:
    def __init__(self, spot, block_ref, line_ref, local_sem, send_sem, recv_sem):
        self.spot, self.line = spot, line_ref
        self.send_sem, self.recv_sem = send_sem, recv_sem
        self.local = pltpu.make_async_copy(block_ref, line_ref.at[spot.chip], local_sem)

    def copy(self, there, way):
        here = self.line.at[there]
        peer = (self.spot.left, self.spot.right)[way]
        return remote(here, here, self.send_sem.at[way, there], self.recv_sem.at[there], peer)

    def ways(self, there):
        chip, chips = self.spot.chip, self.spot.chips
        return ((chip > 0) & (there >= chip), (chip < chips - 1) & (there <= chip))

    def send(self, there):
        for way, when in enumerate(self.ways(there)):
            pl.when(when)(self.copy(there, way).start)

    def start(self):
        self.local.wait()
        self.send(self.spot.chip)

    def forward(self, step):
        for there in (self.spot.chip - step, self.spot.chip + step):

            @pl.when((there >= 0) & (there < self.spot.chips))
            def _():
                here = self.line.at[there]
                remote(here, here, self.send_sem.at[0, there], self.recv_sem.at[there], self.spot.beside).wait_recv()
                self.send(there)

    def end(self):
        for there in range(self.spot.chips):
            for way, when in enumerate(self.ways(there)):
                pl.when(when)(self.copy(there, way).wait_send)


def line_kernel(block_ref, line_ref, local_sem, send_sem, recv_sem):
    spot = Spot()
    line = Line(spot, block_ref, line_ref, local_sem, send_sem, recv_sem)
    line.local.start()
    greet(spot, False, "near")
    line.start()
    for step in range(1, spot.chips):
        line.forward(step)
    line.end()


def plane_kernel(more, line_ref, *refs):
    spot = Spot()
    if more:
        block_ref, whole_ref, next_ref, local_sem, send_sem, recv_sem, *sems = refs
        line = Line(spot, block_ref, next_ref, *sems)
        line.local.start()
    else:
        whole_ref, local_sem, send_sem, recv_sem = refs
    chips, chip, core, row, col = spot.chips, spot.chip, spot.core, spot.row, spot.col
    cut = chips // 2

    def local(there):
        return pltpu.make_async_copy(
            line_ref.at[there], whole_ref.at[spot.index(row, col, there, core)], local_sem.at[there]
        )

    for there in range(chips):
        local(there).start()
    greet(spot, True, "near" if more else None)
    if more:
        line.start()
    sent = []

    def send(index, device, source=None):
        source = whole_ref.at[index] if source is None else source
        copy = remote(source, whole_ref.at[index], send_sem.at[len(sent)], recv_sem.at[index], device)
        sent.append(copy)
        copy.start()

    def arrive(index):
        remote(
            whole_ref.at[index], whole_ref.at[index], send_sem.at[0], recv_sem.at[index], spot.beside
        ).wait_recv()

    for there in range(chips):
        index = spot.index(row, col, there, core)
        for peer in (spot.over_x, spot.over_y, spot.beside):
            send(index, peer, line_ref.at[there])
    for there in range(chips):
        across_x = spot.index(row, 1 - col, there, core)
        arrive(across_x)
        if there < cut:
            send(across_x, spot.over_y)
        send(across_x, spot.beside)
        across_y = spot.index(1 - row, col, there, core)
        arrive(across_y)
        if there >= cut:
            send(across_y, spot.over_x)
        send(across_y, spot.beside)
        if more and 0 < there:
            line.forward(there)
    for there in range(chips):
        index = spot.index(1 - row, 1 - col, there, core)
        arrive(index)
        send(index, spot.beside)
    for plane in range(4):
        for there in range(chips):
            arrive(spot.index(plane // 2, plane % 2, there, 1 - core))
    for there in range(chips):
        local(there).wait()
    for copy in sent:
        copy.wait_send()
    if more:
        line.end()


def gather_line(block, collective_id):
    chips = lax.axis_size("tensor") // 2
    dma = pltpu.SemaphoreType.DMA
    return pl.pallas_call(
        line_kernel,
        in_specs=[pl.BlockSpec(memory_space=pl.ANY)],
        out_specs=pl.BlockSpec(memory_space=pl.ANY),
        out_shape=jax.ShapeDtypeStruct((chips,) + block.shape, B16),
        scratch_shapes=[dma, dma((2, chips)), dma((chips,))],
        compiler_params=pltpu.CompilerParams(
            collective_id=collective_id, has_side_effects=True, vmem_limit_bytes=VMEM_LIMIT
        ),
        cost_estimate=pl.CostEstimate(flops=0, bytes_accessed=block.size * 100, transcendentals=0),
    )(block)


def gather_plane(line, collective_id, more=None):
    chips, size, width = line.shape
    dma = pltpu.SemaphoreType.DMA
    anywhere = pl.BlockSpec(memory_space=pl.ANY)
    shapes = [jax.ShapeDtypeStruct((8 * chips, size, width), B16)]
    sems = [dma((chips,)), dma((10 * chips,)), dma((8 * chips,))]
    if more is not None:
        shapes.append(jax.ShapeDtypeStruct((chips,) + more.shape, B16))
        sems += [dma, dma((2, chips)), dma((chips,))]
    out = pl.pallas_call(
        functools.partial(plane_kernel, more is not None),
        in_specs=[anywhere] * len(shapes),
        out_specs=[anywhere] * len(shapes),
        out_shape=shapes,
        scratch_shapes=sems,
        compiler_params=pltpu.CompilerParams(
            collective_id=collective_id, has_side_effects=True, vmem_limit_bytes=VMEM_LIMIT
        ),
        cost_estimate=pl.CostEstimate(flops=0, bytes_accessed=line.size * 60, transcendentals=0),
    )(line, *([] if more is None else [more]))
    return (out[0].reshape(8 * chips * size, width), *out[1:])


def scatter_kernel(parts, arrays, *refs):
    grads, outs = refs[:arrays], refs[arrays : 2 * arrays]
    mine, got, over_x, over_y, across_x, across_y, line, load_sem, send_sem, recv_sem = refs[2 * arrays :]
    spot = Spot()
    chips, chip, core, row, col = spot.chips, spot.chip, spot.core, spot.row, spot.col
    cut = chips // 2

    def at(r, c, z):
        return (r * 2 + c) * chips + z

    def lanes(p):
        return pl.ds(parts[p][0], parts[p][1])

    def source(p, which):
        _, width, array, start = parts[p]
        return grads[array].at[:, which, :, pl.ds(start, width)]

    def load(p):
        return pltpu.make_async_copy(source(p, core), mine.at[:, :, lanes(p)], load_sem.at[p])

    def swapped(p):
        return remote(
            source(p, 1 - core), got.at[:, :, lanes(p)], send_sem.at[p, 0], recv_sem.at[p, 0], spot.beside
        )

    def first(p):
        cols = lanes(p)
        copies = []
        for side in range(2):
            copies.append(
                remote(
                    mine.at[pl.ds(at(side, 1 - col, 0), cut), :, cols],
                    over_x.at[pl.ds(side * cut, cut), :, cols],
                    send_sem.at[p, 1 + side],
                    recv_sem.at[p, 1 + side],
                    spot.over_x,
                )
            )
            copies.append(
                remote(
                    mine.at[pl.ds(at(1 - row, side, cut), chips - cut), :, cols],
                    over_y.at[pl.ds(side * (chips - cut), chips - cut), :, cols],
                    send_sem.at[p, 3 + side],
                    recv_sem.at[p, 3 + side],
                    spot.over_y,
                )
            )
        return copies

    def second(p):
        cols = lanes(p)
        return [
            remote(
                mine.at[pl.ds(at(1 - row, col, 0), cut), :, cols],
                across_y.at[:, :, cols],
                send_sem.at[p, 5],
                recv_sem.at[p, 5],
                spot.over_y,
            ),
            remote(
                mine.at[pl.ds(at(row, 1 - col, cut), chips - cut), :, cols],
                across_x.at[:, :, cols],
                send_sem.at[p, 6],
                recv_sem.at[p, 6],
                spot.over_x,
            ),
        ]

    def third(p, other):
        cols = lanes(p)
        return remote(
            mine.at[at(row, col, other), :, cols],
            line.at[chip, :, cols],
            send_sem.at[p, 7 + other],
            recv_sem.at[p, 7 + chip],
            spot.on_line(other),
        )

    def add(p, target, start, source, begin, count):
        cols = lanes(p)

        def body(step, _):
            target[start + step, :, cols] = (
                target[start + step, :, cols].astype(F32) + source[begin + step, :, cols].astype(F32)
            ).astype(B16)
            return 0

        lax.fori_loop(0, count, body, 0)

    def stage_one(p):
        load(p).wait()
        swapped(p).wait()
        add(p, mine, 0, got, 0, 4 * chips)
        for copy in first(p):
            copy.start()

    def stage_two(p):
        for copy in first(p):
            copy.wait()
        for side in range(2):
            add(p, mine, at(side, col, 0), over_x, side * cut, cut)
            add(p, mine, at(row, side, cut), over_y, side * (chips - cut), chips - cut)
        for copy in second(p):
            copy.start()

    def stage_three(p):
        for copy in second(p):
            copy.wait()
        add(p, mine, at(row, col, 0), across_y, 0, cut)
        add(p, mine, at(row, col, cut), across_x, 0, chips - cut)
        for other in range(chips):
            pl.when(chip != other)(third(p, other).start)

    def stage_four(p):
        cols = lanes(p)
        total = mine[at(row, col, chip), :, cols].astype(F32)
        for other in range(chips):

            @pl.when(chip != other)
            def _():
                here = line.at[other, :, cols]
                remote(here, here, send_sem.at[p, 7 + other], recv_sem.at[p, 7 + other], spot.beside).wait_recv()

            total = total + line[other, :, cols].astype(F32)
        _, width, array, start = parts[p]
        outs[array][:, start : start + width] = total
        for other in range(chips):
            pl.when(chip != other)(third(p, other).wait_send)

    for p in range(len(parts)):
        load(p).start()
    line[chip] = jnp.zeros(line.shape[1:], B16)
    greet(spot, True, "all")
    for p in range(len(parts)):
        swapped(p).start()
    stages = (stage_one, stage_two, stage_three, stage_four)
    for step in range(len(parts) + len(stages) - 1):
        for late, stage in enumerate(stages):
            if 0 <= step - late < len(parts):
                stage(step - late)


def scatter_weights(grads, collective_id):
    total = grads[0].shape[0]
    devices = lax.axis_size(("dp", "tensor"))
    size = total // devices
    if lax.axis_size("dp") != 4:
        return [
            lax.psum_scatter(array, ("dp", "tensor"), scatter_dimension=0, tiled=True).astype(F32)
            for array in grads
        ]
    chips = lax.axis_size("tensor") // 2
    cut = chips // 2
    parts, width = [], 0
    for at, array in enumerate(grads):
        count = pl.cdiv(array.shape[1], SCATTER_LANES)
        tiles = array.shape[1] // 128
        ends = [tiles * p // count * 128 for p in range(count + 1)]
        for start, end in zip(ends, ends[1:]):
            parts.append((width + start, end - start, at, start))
        width += array.shape[1]
    dma = pltpu.SemaphoreType.DMA
    return pl.pallas_call(
        functools.partial(scatter_kernel, parts, len(grads)),
        in_specs=[pl.BlockSpec(memory_space=pl.ANY)] * len(grads),
        out_specs=[pl.BlockSpec(memory_space=pltpu.VMEM)] * len(grads),
        out_shape=[jax.ShapeDtypeStruct((size, array.shape[1]), F32) for array in grads],
        scratch_shapes=[
            pltpu.VMEM((4 * chips, size, width), B16),
            pltpu.VMEM((4 * chips, size, width), B16),
            pltpu.VMEM((2 * cut, size, width), B16),
            pltpu.VMEM((2 * (chips - cut), size, width), B16),
            pltpu.VMEM((chips - cut, size, width), B16),
            pltpu.VMEM((cut, size, width), B16),
            pltpu.VMEM((chips, size, width), B16),
            dma((len(parts),)),
            dma((len(parts), 7 + chips)),
            dma((len(parts), 7 + chips)),
        ],
        compiler_params=pltpu.CompilerParams(
            collective_id=collective_id, has_side_effects=True, vmem_limit_bytes=VMEM_LIMIT
        ),
        cost_estimate=pl.CostEstimate(flops=0, bytes_accessed=devices * size * width * 8, transcendentals=0),
    )(*[array.reshape(devices // 2, 2, size, array.shape[1]) for array in grads])


class Named:
    def __init__(self, names, refs):
        for name, ref in zip(names, refs, strict=True):
            setattr(self, name, ref)


def project_kernel(hidden_ref, weight_ref, bias_ref, cos_ref, sin_ref, out_ref):
    chunk = pl.program_id(0)
    turned = chunk < (QW + KW) // 256
    lin = dot(hidden_ref[...], weight_ref[...]) + bias_ref[...]
    for head in range(2):
        cut = pl.ds(head * HD, HD)
        one = lin[:, head * HD : (head + 1) * HD]
        rot = one * cos_ref[...] + pltpu.roll(one, HD // 2, 1) * sin_ref[...]
        out_ref[:, cut] = jnp.where(turned, rot, one).astype(B16)


def project(hidden, weights, bias, cosine, sine):
    rows, depth = hidden.shape
    return pl.pallas_call(
        project_kernel,
        grid=(QKV // 256,),
        in_specs=[
            pl.BlockSpec((rows, depth), lambda j: (0, 0)),
            pl.BlockSpec((depth, 256), lambda j: (0, j)),
            pl.BlockSpec((1, 256), lambda j: (0, j)),
            pl.BlockSpec((rows, HD), lambda j: (0, 0)),
            pl.BlockSpec((rows, HD), lambda j: (0, 0)),
        ],
        out_specs=pl.BlockSpec((rows, 256), lambda j: (0, j)),
        out_shape=jax.ShapeDtypeStruct((rows, QKV), B16),
        compiler_params=pltpu.CompilerParams(vmem_limit_bytes=VMEM_LIMIT),
        cost_estimate=pl.CostEstimate(
            flops=2 * rows * depth * QKV,
            bytes_accessed=2 * (depth * QKV + rows * depth + rows * QKV),
            transcendentals=0,
        ),
    )(hidden, weights, bias, cosine, sine)


def fill_bias(info_ref, bias):
    shape = bias.shape
    place = info_ref[1] + lax.broadcasted_iota(jnp.int32, shape, 0)
    keys = lax.broadcasted_iota(jnp.int32, shape, 1)
    bias[...] = jnp.where((keys <= place) & (keys < info_ref[0]), 0.0, MASKED)


def flat(ref):
    return ref[...].reshape(ref.shape[0] * ref.shape[2], ref.shape[3])


def attend_kernel(info_ref, q_ref, k_ref, v_ref, out_ref, log_ref, bias):
    @pl.when(pl.program_id(0) == 0)
    def _():
        fill_bias(info_ref, bias)

    keys, values = flat(k_ref), flat(v_ref)
    scores = dot_t(q_ref[...], keys) * (HD**-0.5) + bias[...]
    top = jnp.max(scores, axis=-1, keepdims=True)
    expd = jnp.exp(scores - top)
    summed = jnp.sum(expd, axis=-1, keepdims=True)
    probs = (expd * (1.0 / summed)).astype(B16)
    out_ref[...] = dot(probs, values).astype(B16)
    log_ref[...] = jnp.broadcast_to(top + jnp.log(summed), log_ref.shape)


def attend(info, micro, qkv, keys_values, rows):
    parts = keys_values.shape[0]
    total = parts * rows
    return pl.pallas_call(
        attend_kernel,
        grid_spec=pltpu.PrefetchScalarGridSpec(
            num_scalar_prefetch=1,
            grid=(H,),
            in_specs=[
                pl.BlockSpec((rows, HD), lambda h, info: (micro, h)),
                pl.BlockSpec((parts, 1, rows, HD), lambda h, info: (0, micro, 0, h // GROUPS)),
                pl.BlockSpec((parts, 1, rows, HD), lambda h, info: (0, micro, 0, KV + h // GROUPS)),
            ],
            out_specs=[
                pl.BlockSpec((rows, HD), lambda h, info: (0, h)),
                pl.BlockSpec((rows, HD), lambda h, info: (0, h)),
            ],
            scratch_shapes=[pltpu.VMEM((rows, total), F32)],
        ),
        out_shape=[
            jax.ShapeDtypeStruct((rows, QW), B16),
            jax.ShapeDtypeStruct((rows, QW), F32),
        ],
        compiler_params=pltpu.CompilerParams(vmem_limit_bytes=VMEM_LIMIT),
        cost_estimate=pl.CostEstimate(
            flops=8 * rows * total * QW,
            bytes_accessed=4 * total * KW + 8 * rows * QW,
            transcendentals=H * rows * total,
        ),
    )(info, qkv, keys_values, keys_values)


def attend_back_kernel(names, parts, *refs):
    r = Named(names, refs)
    spot = Spot()
    chips, chip, core = spot.chips, spot.chip, spot.core
    rows = r.q.shape[0]
    step = pl.program_id(0)
    micros = r.sums.shape[0]
    micro, head = step // H, lax.rem(step, H)
    pieces = micros * KV
    scale = HD**-0.5

    def rows_of(block, which):
        return pl.ds(pl.multiple_of((2 * block + which) * rows, rows), rows)

    def swapped(piece):
        mine = r.part.at[piece, :, 1 - core]
        return remote(mine, r.xrecv.at[piece], r.xsend.at[piece], r.xrecv_sem.at[piece], spot.beside)

    def along(piece, block):
        return remote(
            r.part.at[piece, block, core],
            r.zrecv.at[piece, chip],
            r.zsend.at[piece, block],
            r.zrecv_sem.at[piece, chip],
            spot.on_line(block),
        )

    def spread(piece):
        swapped(piece).wait_recv()
        for block in range(chips):
            total = r.part[piece, block, core].astype(F32) + r.xrecv[piece, block].astype(F32)
            r.part[piece, block, core] = total.astype(B16)
            pl.when(chip != block)(along(piece, block).start)

    @pl.when(step == 0)
    def _():
        greet(spot, False, "all")

    @pl.when(head == 0)
    def _():
        shape = r.bias.shape
        place = spot.tensor * rows + lax.broadcasted_iota(jnp.int32, shape, 0)
        keys_at = lax.broadcasted_iota(jnp.int32, shape, 1)
        r.bias[...] = jnp.where((keys_at <= place) & (keys_at < r.length[micro]), 0.0, MASKED)

    queries, keys, values, grads = r.q[...], flat(r.k), flat(r.v), r.g[...]
    scores = dot_t(queries, keys) * scale + r.bias[...]
    probs = jnp.exp(scores - r.log[:, :1])
    grad_probs = dot_t(grads, values)
    inner = jnp.sum(grad_probs * probs, axis=-1, keepdims=True)
    grad_scores = (probs * (grad_probs - inner)).astype(B16)
    grad_q = dot(grad_scores, keys) * scale
    turned = grad_q * r.cos[...] - pltpu.roll(grad_q, HD // 2, 1) * r.sin[...]
    r.dq[...] = turned.astype(B16)
    grad_k = t_dot(grad_scores, queries) * scale
    grad_v = t_dot(probs.astype(B16), grads)
    first = lax.rem(head, GROUPS) == 0

    @pl.when(first)
    def _():
        r.dk_acc[...] = grad_k
        r.dv_acc[...] = grad_v

    @pl.when(jnp.logical_not(first))
    def _():
        r.dk_acc[...] += grad_k
        r.dv_acc[...] += grad_v

    for piece in range(pieces):

        @pl.when(step == (piece + 1) * GROUPS - 1)
        def _():
            shape = (chips, 2, rows, HD)
            r.part[piece, :, :, :, :HD] = r.dk_acc[...].reshape(shape).astype(B16)
            r.part[piece, :, :, :, HD:] = r.dv_acc[...].reshape(shape).astype(B16)
            swapped(piece).start()

        if piece + 1 < pieces:

            @pl.when(step == (piece + 1) * GROUPS)
            def _():
                spread(piece)

    @pl.when(step == pieces * GROUPS - 1)
    def _():
        spread(pieces - 1)
        for piece in range(pieces):
            total = r.part[piece, chip, core].astype(F32)
            for other in range(chips):

                @pl.when(chip != other)
                def _():
                    here = r.zrecv.at[piece, other]
                    remote(
                        here, here, r.zsend.at[piece, other], r.zrecv_sem.at[piece, other], spot.beside
                    ).wait_recv()

                got = jnp.where(chip != other, r.zrecv[piece, other], jnp.zeros((rows, 2 * HD), B16))
                total = total + got.astype(F32)
            at, group = piece // KV, piece % KV
            grad = total[:, :HD]
            grad = grad * r.cos[...] - pltpu.roll(grad, HD // 2, 1) * r.sin[...]
            r.sums[at, :, group * HD : (group + 1) * HD] = grad.astype(B16)
            r.sums[at, :, KW + group * HD : KW + (group + 1) * HD] = total[:, HD:].astype(B16)
        for piece in range(pieces):
            swapped(piece).wait_send()
            for block in range(chips):
                pl.when(chip != block)(along(piece, block).wait_send)


def attend_back(lengths, qkv, keys_values, grads, logs, cosine, sine, rows, collective_id):
    parts, micros = keys_values.shape[:2]
    chips = parts // 2
    total = parts * rows
    pieces = micros * KV
    dma = pltpu.SemaphoreType.DMA
    vmem = pltpu.VMEM

    def heads(step):
        return (step // H, step % H)

    inputs = {
        "length": (pl.BlockSpec(memory_space=pltpu.SMEM), lengths),
        "q": (pl.BlockSpec((rows, HD), heads), qkv),
        "k": (
            pl.BlockSpec((parts, 1, rows, HD), lambda s: (0, s // H, 0, s % H // GROUPS)),
            keys_values,
        ),
        "v": (
            pl.BlockSpec((parts, 1, rows, HD), lambda s: (0, s // H, 0, KV + s % H // GROUPS)),
            keys_values,
        ),
        "g": (pl.BlockSpec((rows, HD), heads), grads),
        "log": (pl.BlockSpec((rows, HD), heads), logs),
        "cos": (pl.BlockSpec((rows, HD), lambda s: (0, 0)), cosine),
        "sin": (pl.BlockSpec((rows, HD), lambda s: (0, 0)), sine),
    }
    outputs = {
        "dq": (pl.BlockSpec((rows, HD), heads), jax.ShapeDtypeStruct((micros * rows, QW), B16)),
        "sums": (
            pl.BlockSpec((micros, rows, 2 * KW), lambda s: (0, 0, 0)),
            jax.ShapeDtypeStruct((micros, rows, 2 * KW), B16),
        ),
    }
    scratch = {
        "bias": vmem((rows, total), F32),
        "dk_acc": vmem((total, HD), F32),
        "dv_acc": vmem((total, HD), F32),
        "part": vmem((pieces, chips, 2, rows, 2 * HD), B16),
        "xrecv": vmem((pieces, chips, rows, 2 * HD), B16),
        "zrecv": vmem((pieces, chips, rows, 2 * HD), B16),
        "xsend": dma((pieces,)),
        "xrecv_sem": dma((pieces,)),
        "zsend": dma((pieces, chips)),
        "zrecv_sem": dma((pieces, chips)),
    }
    return pl.pallas_call(
        functools.partial(attend_back_kernel, [*inputs, *outputs, *scratch], parts),
        grid=(micros * H,),
        in_specs=[spec for spec, _ in inputs.values()],
        out_specs=[spec for spec, _ in outputs.values()],
        out_shape=[shape for _, shape in outputs.values()],
        scratch_shapes=list(scratch.values()),
        compiler_params=pltpu.CompilerParams(
            collective_id=collective_id, has_side_effects=True, vmem_limit_bytes=VMEM_LIMIT
        ),
        cost_estimate=pl.CostEstimate(
            flops=20 * micros * rows * total * QW,
            bytes_accessed=micros * (8 * total * KW + 12 * rows * QW),
            transcendentals=micros * H * rows * total,
        ),
    )(*[value for _, value in inputs.values()])


def mlp_kernel(names, reduced, *refs):
    r = Named(names, refs)
    has_next, has_prior = "own" in names, "prior" in names
    spot = Spot()
    chips, chip, core, row, col = spot.chips, spot.chip, spot.core, spot.row, spot.col
    units, depth = r.wg.shape
    rows = r.grad.shape[0]
    pair = 2 * rows
    quarter = depth // 4
    chunks = [(i * CHUNK, min(CHUNK, units - i * CHUNK)) for i in range(pl.cdiv(units, CHUNK))]
    whole_chunks, rest = units // CHUNK, units % CHUNK
    wide = depth // 2

    def block_at(step):
        return nearest(chips, chip, chips - 1 - step)

    def span(block):
        return pl.ds(pl.multiple_of(block * pair, pair), pair)

    def rows_of(block, which):
        return pl.ds(pl.multiple_of(block * pair + which * rows, rows), rows)

    def columns(index, width=CHUNK):
        return pl.ds(pl.multiple_of(index * width, width), width)

    def weight_load(index):
        cut = pl.ds(*chunks[index])
        return [
            pltpu.make_async_copy(src.at[cut], dst.at[cut], r.weight_sem.at[i, index])
            for i, (src, dst) in enumerate(((r.wg_hbm, r.wg), (r.wu_hbm, r.wu), (r.wd_hbm, r.wd)))
        ]

    def weights_here(index, width=CHUNK):
        for i, dst in enumerate((r.wg, r.wu, r.wd)):
            cut = dst.at[pl.ds(index * CHUNK, width)]
            pltpu.make_async_copy(cut, cut, r.weight_sem.at[i, index]).wait()

    def h_load(block):
        return pltpu.make_async_copy(r.h_hbm.at[span(block)], r.h.at[span(block)], r.load_sem.at[0, block])

    def g_load(block):
        return pltpu.make_async_copy(r.cot.at[span(block)], r.g.at[span(block)], r.load_sem.at[1, block])

    def gather_send(block, way):
        here = r.whole.at[rows_of(block, core)]
        peer = (spot.left, spot.right, spot.beside)[way]
        return remote(here, here, r.gather_send.at[way, block], r.gather_recv.at[block, core], peer)

    def gather_first(way):
        peer = (spot.left, spot.right, spot.beside)[way]
        here = r.whole.at[rows_of(chip, core)]
        return remote(r.own, here, r.gather_send.at[way, chip], r.gather_recv.at[chip, core], peer)

    def gathered(block, which):
        here = r.whole.at[rows_of(block, which)]
        remote(here, here, r.gather_send.at[2, block], r.gather_recv.at[block, which], spot.beside).wait_recv()

    def own_copy():
        return pltpu.make_async_copy(r.own, r.whole.at[rows_of(chip, core)], r.local_sem)

    def gather_start():
        own_copy().start()
        pl.when(chip > 0)(gather_first(0).start)
        pl.when(chip < chips - 1)(gather_first(1).start)
        gather_first(2).start()

    def gather_forward(step):
        block = chip - step

        @pl.when(block >= 0)
        def _():
            gathered(block, core)
            pl.when(chip < chips - 1)(gather_send(block, 1).start)
            gather_send(block, 2).start()

        after = chip + step

        @pl.when(after < chips)
        def _():
            gathered(after, core)
            pl.when(chip > 0)(gather_send(after, 0).start)
            gather_send(after, 2).start()

    def gather_end():
        own_copy().wait()
        for block in range(chips):
            gathered(block, 1 - core)
        for block in range(chips):
            away = block != chip
            pl.when((chip > 0) & (block >= chip) & away)(gather_send(block, 0).wait_send)
            pl.when((chip < chips - 1) & (block <= chip) & away)(gather_send(block, 1).wait_send)
            pl.when(away)(gather_send(block, 2).wait_send)
        pl.when(chip > 0)(gather_first(0).wait_send)
        pl.when(chip < chips - 1)(gather_first(1).wait_send)
        gather_first(2).wait_send()

    def swapped(block):
        return remote(
            r.part.at[rows_of(block, 1 - core)],
            r.xrecv.at[block],
            r.xsend.at[block],
            r.xrecv_sem.at[block],
            spot.beside,
        )

    def along(block, ahead):
        slot = chips - 1 - block if ahead else chips - block
        return remote(
            r.part.at[rows_of(block, core)],
            r.zrecv.at[slot],
            r.zsend.at[block],
            r.zrecv_sem.at[slot],
            spot.right if ahead else spot.left,
        )

    def finish(block):
        swapped(block).wait_recv()
        total = r.part[rows_of(block, core), :].astype(F32) + r.xrecv[block].astype(F32)

        @pl.when(block == chip)
        def _():
            r.grad[...] = total

        @pl.when(block != chip)
        def _():
            r.part[rows_of(block, core), :] = total.astype(B16)
            pl.when(chip == 0)(along(block, True).start)
            pl.when(chip == chips - 1)(along(block, False).start)

    def relay_one(block, ahead):
        slot = chips - 1 - block if ahead else chips - block
        remote(
            r.zrecv.at[slot], r.zrecv.at[slot], r.zsend.at[block], r.zrecv_sem.at[slot], spot.beside
        ).wait_recv()

        @pl.when(block == chip)
        def _():
            r.grad[...] = r.grad[...] + r.zrecv[slot].astype(F32)

        @pl.when(block != chip)
        def _():
            here = rows_of(block, core)
            r.part[here, :] = (r.part[here, :].astype(F32) + r.zrecv[slot].astype(F32)).astype(B16)
            along(block, ahead).start()

    def relay(point):
        step = point - (chip - 1)

        @pl.when((chip > 0) & (step >= 0) & (step < chips - chip))
        def _():
            relay_one(chips - 1 - step, True)

        back_step = point - (chips - 2 - chip)

        @pl.when((chip < chips - 1) & (back_step >= 0) & (back_step <= chip))
        def _():
            relay_one(back_step, False)

    def gates(step, block):
        here = span(block)

        def one(start, width):
            cut = pl.ds(start, width)
            gate = dot_t(r.h[here, :], r.wg[cut, :])
            up = dot_t(r.h[here, :], r.wu[cut, :])
            grad = dot_t(r.g[here, :], r.wd[cut, :])
            sigma = jax.nn.sigmoid(gate)
            silu = gate * sigma
            r.act[here, cut] = (silu * up).astype(B16)
            r.dg[here, cut] = (grad * up * sigma * (1.0 + gate * (1.0 - sigma))).astype(B16)
            r.du[here, cut] = (grad * silu).astype(B16)

        def chunk(index, _):
            pl.when(step == 0)(functools.partial(weights_here, index))
            one(pl.multiple_of(index * CHUNK, CHUNK), CHUNK)
            return 0

        lax.fori_loop(0, whole_chunks, chunk, 0)
        if rest:
            pl.when(step == 0)(functools.partial(weights_here, whole_chunks, rest))
            one(whole_chunks * CHUNK, rest)

    def back(block):
        here = span(block)

        def chunk(index, _):
            cut = columns(index, wide)
            grad = dot(r.dg[here, :], r.wg[:, cut]) + dot(r.du[here, :], r.wu[:, cut])
            r.part[here, cut] = grad.astype(B16)
            return 0

        lax.fori_loop(0, depth // wide, chunk, 0)
        swapped(block).start()

    def put_out(block, index):
        cut = pl.ds(index * wide, wide)
        return pltpu.make_async_copy(
            r.stage_out.at[:, cut], r.out.at[span(block), cut], r.out_sem.at[index]
        )

    def out_block(block):
        for index in range(2):
            pl.when(block > 0)(put_out(block, index).wait)
            cut = slice(index * wide, (index + 1) * wide)
            r.stage_out[:, cut] = dot(r.act[span(block), :], r.wd[:, cut]).astype(B16)
            put_out(block, index).start()

    def place(matrix, start, width):
        return pl.ds(pl.multiple_of(matrix * units + start, 16), width)

    def exchanged(matrix, index, start, width, over_x):
        here = place(matrix, start, width)
        at = matrix * len(chunks) + index
        source = r.sums.at[:, 1 - col, here] if over_x else r.sums.at[1 - row, :, here]
        peer = spot.over_x if over_x else spot.over_y
        return remote(source, r.landing.at[:, here], r.one_send.at[at], r.one_recv.at[at], peer)

    def exchange_start(matrix, index, start, width):
        first = lax.rem(matrix + index, 2) == 0
        pl.when(first)(exchanged(matrix, index, start, width, True).start)
        pl.when(jnp.logical_not(first))(exchanged(matrix, index, start, width, False).start)

    def exchange_copies(matrix, index, slot):
        start, width = chunks[index]
        here = place(matrix, start, width)
        cut = pl.ds(0, width)
        own = r.sums.at[:, col, here] if (matrix + index) % 2 == 0 else r.sums.at[row, :, here]
        return [
            pltpu.make_async_copy(own, r.held_own.at[slot, :, cut], r.held_sem.at[slot, 0]),
            pltpu.make_async_copy(r.landing.at[:, here], r.held_got.at[slot, :, cut], r.held_sem.at[slot, 1]),
        ]

    def exchange_load(matrix, index, slot):
        exchanged(matrix, index, *chunks[index], (matrix + index) % 2 == 0).wait_recv()
        for copy in exchange_copies(matrix, index, slot):
            copy.start()

    def exchange(matrix, index, slot):
        start, width = chunks[index]
        for copy in exchange_copies(matrix, index, slot):
            copy.wait()
        mine = row if (matrix + index) % 2 == 0 else col
        r.shard[place(matrix, start, width), :] = (
            r.held_own[slot, mine, :width].astype(F32) + r.held_got[slot, mine, :width].astype(F32)
        ).astype(B16)
        at = reduced[matrix, index]
        r.rest[at : at + width, :] = (
            r.held_own[slot, 1 - mine, :width].astype(F32) + r.held_got[slot, 1 - mine, :width].astype(F32)
        ).astype(B16)

    def weight_grads(matrix, left, right):
        def put(start, width, slot):
            return pltpu.make_async_copy(
                r.stage.at[slot, :, :, pl.ds(0, width)],
                r.sums.at[:, :, place(matrix, start, width)],
                r.stage_sem.at[slot],
            )

        def one(index, start, width, slot):
            if has_prior:
                fetch = pltpu.make_async_copy(
                    r.prior.at[:, :, place(matrix, start, width)],
                    r.before.at[:, :, pl.ds(0, width)],
                    r.before_sem,
                )
                fetch.start()
            value = t_dot(left[:, pl.ds(start, width)], right[...])
            if has_prior:
                fetch.wait()
            for at in range(4):
                piece = value[:, at * quarter : (at + 1) * quarter]
                if has_prior:
                    piece = piece + r.before[at // 2, at % 2, :width].astype(F32)
                r.stage[slot, at // 2, at % 2, :width] = piece.astype(B16)
            put(start, width, slot).start()

        def sent(index, start, width, slot):
            put(start, width, slot).wait()
            if reduced:
                exchange_start(matrix, index, start, width)

        def body(index, _):
            slot = lax.rem(index, 2)
            start = pl.multiple_of(index * CHUNK, CHUNK)
            one(index, start, CHUNK, slot)

            @pl.when(index > 0)
            def _():
                sent(index - 1, start - CHUNK, CHUNK, 1 - slot)

            return 0

        lax.fori_loop(0, whole_chunks, body, 0)
        index = whole_chunks
        if rest:
            one(index, index * CHUNK, rest, index % 2)
            if index:
                sent(index - 1, (index - 1) * CHUNK, CHUNK, (index - 1) % 2)
            sent(index, index * CHUNK, rest, index % 2)
        else:
            sent(index - 1, (index - 1) * CHUNK, CHUNK, (index - 1) % 2)

    for step in range(chips):
        h_load(block_at(step)).start()
        g_load(block_at(step)).start()
        if step == 0:
            for index in range(len(chunks)):
                for copy in weight_load(index):
                    copy.start()
    greet(spot, bool(reduced), "near")
    if has_next:
        gather_start()

    def loaded(block):
        h_load(block).wait()
        g_load(block).wait()

    todo = [(matrix, index) for matrix in (2, 0, 1) for index in range(len(chunks))] if reduced else []
    share = pl.cdiv(len(todo), chips)
    loading = []

    def some():
        for _ in range(share):
            if loading:
                exchange(*loading.pop(0))
            if todo:
                loading.append((*todo.pop(0), len(todo) % 2))
                exchange_load(*loading[-1])

    if has_next:

        def unit(step, _):
            block = block_at(step)
            loaded(block)
            gates(step, block)

            @pl.when(step > 0)
            def _():
                finish(block_at(step - 1))

            back(block)
            pl.when(step == 0)(functools.partial(gather_forward, 1))
            return 0

        lax.fori_loop(0, chips, unit, 0)
        finish(block_at(chips - 1))
        gather_forward(2)
        relay(0)
        weight_grads(2, r.act, r.g)
        for step in range(3, chips):
            gather_forward(step)
        weight_grads(0, r.dg, r.h)
        relay(1)
        weight_grads(1, r.du, r.h)
        for point in range(2, chips - 2):
            relay(point)
    else:

        def unit(step, _):
            block = block_at(step)
            loaded(block)
            gates(step, block)
            return 0

        def unit_back(step, _):
            back(block_at(step))

            @pl.when(step > 0)
            def _():
                finish(block_at(step - 1))

            return 0

        lax.fori_loop(0, chips, unit, 0)
        weight_grads(2, r.act, r.g)
        lax.fori_loop(0, chips, unit_back, 0)
        finish(block_at(chips - 1))
        weight_grads(0, r.dg, r.h)
        relay(0)
        weight_grads(1, r.du, r.h)
        for point in range(1, chips - 2):
            relay(point)
    for block in range(chips):
        out_block(jnp.int32(block))
        some()
    relay(chips - 2)
    some()
    for index in range(2):
        put_out(0, index).wait()
    if reduced:
        for matrix in range(3):
            for index, (start, width) in enumerate(chunks):
                exchanged(matrix, index, start, width, (matrix + index) % 2 == 0).wait_send()
    for block in range(chips):
        swapped(block).wait_send()
        pl.when(chip < block)(along(block, True).wait_send)
        pl.when(chip > block)(along(block, False).wait_send)
    if has_next:
        gather_end()


def exchange_rows(units):
    chunks = [min(CHUNK, units - start) for start in range(0, units, CHUNK)]
    keys = [(matrix, index) for matrix in range(3) for index in range(len(chunks))]
    places, at = {}, 0
    for odd in range(2):
        for matrix, index in keys:
            if (matrix + index) % 2 == odd:
                places[matrix, index] = at
                at += chunks[index]
    border = sum(chunks[index] for matrix, index in keys if (matrix + index) % 2 == 0)
    return places, border, [(places[key], chunks[key[1]]) for key in keys]


def mlp(cot, hidden, wg, wu, wd, own, prior, rows, collective_id):
    total, depth = hidden.shape
    units = wg.shape[0]
    chips = total // (2 * rows)
    reduced = exchange_rows(units)[0] if own is None and lax.axis_size("dp") == 4 else {}
    quarter = depth // 4
    count = pl.cdiv(units, CHUNK)
    anywhere = pl.BlockSpec(memory_space=pl.ANY)
    local = pl.BlockSpec(memory_space=pltpu.VMEM)
    dma = pltpu.SemaphoreType.DMA
    vmem = pltpu.VMEM
    held = jax.ShapeDtypeStruct((3 * units, quarter), B16)

    inputs = {"cot": cot, "h_hbm": hidden, "wg_hbm": wg, "wu_hbm": wu, "wd_hbm": wd}
    if own is not None:
        inputs["own"] = own
    if prior is not None:
        inputs["prior"] = prior
    outputs = {
        "out": (anywhere, jax.ShapeDtypeStruct((total, depth), B16)),
        "grad": (local, jax.ShapeDtypeStruct((rows, depth), F32)),
        "sums": (anywhere, jax.ShapeDtypeStruct((2, 2, 3 * units, quarter), B16)),
    }
    if own is not None:
        outputs["whole"] = (anywhere, jax.ShapeDtypeStruct((total, depth), B16))
    if reduced:
        outputs["shard"] = (local, held)
        outputs["rest"] = (local, held)
        outputs["landing"] = (anywhere, jax.ShapeDtypeStruct((2, 3 * units, quarter), B16))
    scratch = {
        "wg": vmem((units, depth), B16),
        "wu": vmem((units, depth), B16),
        "wd": vmem((units, depth), B16),
        "h": vmem((total, depth), B16),
        "g": vmem((total, depth), B16),
        "act": vmem((total, units), B16),
        "dg": vmem((total, units), B16),
        "du": vmem((total, units), B16),
        "part": vmem((total, depth), B16),
        "xrecv": vmem((chips, rows, depth), B16),
        "zrecv": vmem((chips + 1, rows, depth), B16),
        "stage_out": vmem((2 * rows, depth), B16),
        "stage": vmem((2, 2, 2, CHUNK, quarter), B16),
        "weight_sem": dma((3, count)),
        "load_sem": dma((2, chips)),
        "xsend": dma((chips,)),
        "xrecv_sem": dma((chips,)),
        "zsend": dma((chips,)),
        "zrecv_sem": dma((chips + 1,)),
        "out_sem": dma((2,)),
        "stage_sem": dma((2,)),
    }
    if own is not None:
        scratch["local_sem"] = dma
        scratch["gather_send"] = dma((3, chips))
        scratch["gather_recv"] = dma((chips, 2))
    if prior is not None:
        scratch["before"] = vmem((2, 2, CHUNK, quarter), B16)
        scratch["before_sem"] = dma
    if reduced:
        scratch["held_own"] = vmem((2, 2, CHUNK, quarter), B16)
        scratch["held_got"] = vmem((2, 2, CHUNK, quarter), B16)
        scratch["held_sem"] = dma((2, 2))
        scratch["one_send"] = dma((3 * count,))
        scratch["one_recv"] = dma((3 * count,))
    names = [*inputs, *outputs, *scratch]
    out = pl.pallas_call(
        functools.partial(mlp_kernel, names, reduced),
        in_specs=[anywhere] * len(inputs),
        out_specs=[spec for spec, _ in outputs.values()],
        out_shape=[shape for _, shape in outputs.values()],
        scratch_shapes=list(scratch.values()),
        compiler_params=pltpu.CompilerParams(
            collective_id=collective_id, has_side_effects=True, vmem_limit_bytes=VMEM_MOST
        ),
        cost_estimate=pl.CostEstimate(
            flops=18 * total * depth * units, bytes_accessed=40 * total * depth, transcendentals=total * units
        ),
    )(*inputs.values())
    return dict(zip(outputs, out))


def widen_kernel(first_ref, second_ref, third_ref, *outs):
    for source, out in zip((first_ref, second_ref, third_ref), outs):
        quarter = source.shape[2]
        for at in range(4):
            out[:, at * quarter : (at + 1) * quarter] = source[at].astype(F32)


def widen(quarters, units):
    quarter = quarters.shape[2]
    steps = next(n for n in range(4, units) if units % (16 * n) == 0)
    size = units // steps
    return pl.pallas_call(
        widen_kernel,
        grid=(steps,),
        in_specs=[
            pl.BlockSpec((4, size, quarter), functools.partial(lambda base, i: (0, base + i, 0), at * steps))
            for at in range(3)
        ],
        out_specs=[pl.BlockSpec((size, 4 * quarter), lambda i: (i, 0))] * 3,
        out_shape=[jax.ShapeDtypeStruct((units, 4 * quarter), F32)] * 3,
        compiler_params=pltpu.CompilerParams(vmem_limit_bytes=VMEM_LIMIT),
        cost_estimate=pl.CostEstimate(flops=0, bytes_accessed=72 * units * quarter, transcendentals=0),
    )(quarters, quarters, quarters)


def norm_back(grad_out, normed, factor, gain):
    inner = grad_out * gain
    grad_rows = factor * (inner - normed * jnp.mean(inner * normed, axis=-1, keepdims=True))
    return (grad_rows, jnp.sum(grad_out * normed, axis=0))


def normalize(rows, gain):
    factor = lax.rsqrt(jnp.mean(rows * rows, axis=-1, keepdims=True) + EPS)
    normed = rows * factor
    return (normed, factor, (normed * gain).astype(B16))


def on_device(
    layer_input,
    lengths,
    attn_gain,
    query_proj,
    query_bias,
    key_proj,
    key_bias,
    value_proj,
    value_bias,
    out_proj,
    mlp_gain,
    gate_proj,
    up_proj,
    down_proj,
    cotangent,
):
    micros = layer_input.shape[0]
    rows = layer_input.shape[2]
    depth = layer_input.shape[3]
    tensor = lax.axis_index("tensor")
    total = rows * lax.axis_size("tensor")
    devices = lax.axis_size(("dp", "tensor"))
    size = query_proj.shape[0]
    small = key_bias.shape[0]
    offset = tensor * rows
    positions = offset + jnp.arange(rows, dtype=jnp.int32)
    cosine, sine = rope_tables(positions)

    valid = (positions[None, :] < lengths).astype(F32).reshape(micros, rows, 1)
    grad_rows = cotangent[:, 0].astype(F32) * valid
    low_rows = [grad_rows[m].astype(B16) for m in range(micros)]

    tail = jnp.concatenate([key_bias, value_bias, jnp.zeros((size - 2 * small,), B16)])
    extra = jnp.stack([attn_gain, query_bias, mlp_gain, tail], axis=1)
    extra = jnp.pad(extra, ((0, 0), (0, EXTRA - 4)))
    block = jnp.concatenate([query_proj, key_proj, value_proj, extra], axis=1)
    square = lax.axis_size("dp") == 4
    low = low_rows[0]
    if square:
        line = gather_line(block, 0)
        line, low = lax.optimization_barrier((line, low))
    cots = [lax.all_gather(low, "tensor", axis=0, tiled=True)]
    if square:
        packed, wout_line = gather_plane(line, 1, out_proj)
    else:
        packed = lax.all_gather(block, ("dp", "tensor"), axis=0, tiled=True)
    vectors = packed[:, QKV : QKV + 4].astype(F32)
    gain_one, gain_two = vectors[:, 0], vectors[:, 2]
    tails = vectors[:, 3].reshape(devices, size)
    bias = jnp.concatenate(
        [vectors[:, 1], tails[:, :small].reshape(-1), tails[:, small : 2 * small].reshape(-1)]
    )[None, :]

    inputs = layer_input[:, 0].astype(F32).reshape(micros * rows, depth)
    normed_one, factor_one, hidden = normalize(inputs, gain_one)
    qkv = project(
        hidden, packed, bias, jnp.tile(cosine, (micros, 1)), jnp.tile(sine, (micros, 1))
    )
    infos = [jnp.stack([lengths[m, 0], offset]) for m in range(micros)]

    own_kv = qkv[:, QW:].reshape(micros, rows, 2 * KW)
    own_kv, *cots = lax.optimization_barrier((own_kv, *cots))
    all_kv = lax.all_gather(own_kv, "tensor", axis=0)
    if square:
        wout_line, own_kv = lax.optimization_barrier((wout_line, own_kv))
        (wout,) = gather_plane(wout_line, 6)
    else:
        wout = lax.all_gather(out_proj, ("dp", "tensor"), axis=0, tiled=True)
    attended, logs, mixed, norm_two, hidden_two = [], [], [], [], []
    for m in range(micros):
        out, log = attend(infos[m], m, qkv, all_kv, rows)
        attended.append(out)
        logs.append(log)
        mixed.append(inputs[m * rows : (m + 1) * rows] + dot(out, wout))
        normed, factor, low = normalize(mixed[m], gain_two)
        norm_two.append((normed, factor))
        hidden_two.append(low)
        if m == 0:
            low, all_kv = lax.optimization_barrier((low, all_kv))
            whole = lax.all_gather(low, "tensor", axis=0, tiled=True)
    units = down_proj.shape[0]
    prior, grad_two, out_sums = None, [], []
    for m in range(1, micros):
        low, whole, *hidden_two = lax.optimization_barrier((low_rows[m], whole, *hidden_two))
        cots.append(lax.all_gather(low, "tensor", axis=0, tiled=True))
    for m in range(micros):
        own = hidden_two[m + 1] if m + 1 < micros else None
        done = mlp(cots[m], whole, gate_proj.T, up_proj.T, down_proj, own, prior, rows, 7 + m)
        whole, prior = done.get("whole"), done["sums"]
        grad_two.append(done["grad"])
        out_sums.append(lax.psum_scatter(done["out"], "tensor", scatter_dimension=0, tiled=True))
    if square:
        _, border, spans = exchange_rows(units)
        rest = done["rest"]
        got = jnp.concatenate([swap(rest[:border], "dp", 2), swap(rest[border:], "dp", 1)], axis=0)
    grad_mixed, gain_two_grads = [], []
    for m in range(micros):
        normed, factor = norm_two[m]
        grad, gain_grad = norm_back(grad_two[m], normed, factor, gain_two)
        gain_two_grads.append(gain_grad)
        grad_mixed.append(grad + grad_rows[m])

    grad_low = jnp.concatenate(grad_mixed, axis=0).astype(B16)
    acc_out = t_dot(jnp.concatenate(attended, axis=0), grad_low).astype(B16)
    grad_attended = dot_t(grad_low, wout).astype(B16)
    if square:
        got, grad_attended, acc_out = lax.optimization_barrier((got, grad_attended, acc_out))
        got = jnp.concatenate([got[at : at + width] for at, width in spans], axis=0)
        shard = (done["shard"].astype(F32) + got.astype(F32)).astype(B16)
        shard, grad_attended = lax.optimization_barrier((shard, grad_attended))
        weight_grads = lax.all_gather(shard, "dp", axis=0)
    else:
        weight_grads = lax.psum(prior, "dp").reshape(4, 3 * units, depth // 4)
    grad_q, grad_kv = attend_back(
        lengths[:, 0], qkv, all_kv, grad_attended, jnp.concatenate(logs, axis=0), cosine, sine, rows, 3
    )
    grad_kv = grad_kv.reshape(micros * rows, 2 * KW)
    grad_hidden = dot_t(grad_q, packed[:, :QW]) + dot_t(grad_kv, packed[:, QW:QKV])
    grad_in, gain_one_grad = norm_back(grad_hidden, normed_one, factor_one, gain_one)
    grad_bias = jnp.concatenate(
        [jnp.sum(grad_q.astype(F32), axis=0), jnp.sum(grad_kv.astype(F32), axis=0)]
    )
    acc_q = t_dot(hidden, grad_q).astype(B16)
    acc_kv = t_dot(hidden, grad_kv).astype(B16)
    tails = jnp.concatenate(
        [
            grad_bias[QW : QW + KW].reshape(devices, small),
            grad_bias[QW + KW :].reshape(devices, small),
            jnp.zeros((devices, size - 2 * small), F32),
        ],
        axis=1,
    ).reshape(-1)
    columns = jnp.stack([gain_one_grad, grad_bias[:QW], sum(gain_two_grads), tails], axis=1)
    columns = jnp.pad(columns.astype(B16), ((0, 0), (0, EXTRA - 4)))
    summed = scatter_weights([acc_out, acc_q, jnp.concatenate([acc_kv, columns], axis=1)], 2)
    out_sums, weight_grads, summed = lax.optimization_barrier((out_sums, weight_grads, summed))
    gate_total, up_total, down_total = widen(weight_grads, units)
    grad_out, grad_query, grad_rest = summed
    layer_output = jnp.stack(
        [(mixed[m] + out_sums[m].astype(F32)).astype(B16) for m in range(micros)]
    )[:, None]
    grad_input = (grad_in + jnp.concatenate(grad_mixed, axis=0)).reshape(micros, 1, rows, depth)
    return (
        layer_output,
        grad_input,
        grad_rest[:, 2 * KW],
        grad_query,
        grad_rest[:, 2 * KW + 1],
        grad_rest[:, :KW],
        grad_rest[:small, 2 * KW + 3],
        grad_rest[:, KW : 2 * KW],
        grad_rest[small : 2 * small, 2 * KW + 3],
        grad_out,
        grad_rest[:, 2 * KW + 2],
        gate_total.T,
        up_total.T,
        down_total,
    )


def solution(mesh):
    rows = P(None, "dp", "tensor", None)
    both = P(("dp", "tensor"))
    wide = P(("dp", "tensor"), None)
    placed = (
        rows,
        P(None, "dp"),
        both,
        wide,
        both,
        wide,
        both,
        wide,
        both,
        wide,
        both,
        P(None, "tensor"),
        P(None, "tensor"),
        P("tensor", None),
        rows,
    )
    return jax.shard_map(
        on_device,
        mesh=mesh,
        in_specs=placed,
        out_specs=(
            rows,
            rows,
            both,
            wide,
            both,
            wide,
            both,
            wide,
            both,
            wide,
            both,
            P(None, "tensor"),
            P(None, "tensor"),
            P("tensor", None),
        ),
        check_vma=False,
    )
```

```python
import functools

import jax
import jax.numpy as jnp
from jax import lax
from jax.experimental import pallas as pl
from jax.experimental.pallas import tpu as pltpu
from jax.sharding import PartitionSpec as P

H = 12
KV = 2
HD = 128
GROUPS = H // KV
QW = H * HD
KW = KV * HD
QKV = QW + 2 * KW
EXTRA = 128

ROPE_BASE = 1000000.0
EPS = 1e-06
MASKED = -1e30
LOG2E = 1.4426950408889634
HEADS = 3
F32 = jnp.float32
B16 = jnp.bfloat16
VMEM_LIMIT = 56 * 1024 * 1024
VMEM_MOST = 60 * 1024 * 1024
CHUNK = 256
SCATTER_LANES = 1024
MESH = pl.DeviceIdType.MESH


def dot(a, b):
    return jnp.dot(a, b, preferred_element_type=F32)


def dot_t(a, b):
    return lax.dot_general(a, b, (((1,), (1,)), ((), ())), preferred_element_type=F32)


def t_dot(a, b):
    return lax.dot_general(a, b, (((0,), (0,)), ((), ())), preferred_element_type=F32)


def rope_tables(positions):
    half = HD // 2
    freqs = ROPE_BASE ** (-(jnp.arange(half, dtype=F32) * 2.0 / HD))
    angles = positions.astype(F32)[:, None] * freqs[None, :]
    cosine = jnp.cos(angles)
    sine = jnp.sin(angles)
    return (
        jnp.concatenate([cosine, cosine], axis=1),
        jnp.concatenate([-sine, sine], axis=1),
    )


def swap(value, axis, bit):
    count = lax.axis_size(axis)
    return lax.ppermute(value, axis, [(i, i ^ bit) for i in range(count)])


def nearest(chips, place, step):
    found = 0
    for here in range(chips):
        for at, there in enumerate(sorted(range(chips), key=lambda there: abs(there - here))):
            found = found + jnp.where((place == here) & (step == at), there, 0)
    return found


class Spot:
    def __init__(self):
        self.chips = lax.axis_size("tensor") // 2
        dp, tensor = lax.axis_index("dp"), lax.axis_index("tensor")
        self.dp, self.tensor = dp, tensor
        self.row, self.col = dp // 2, dp % 2
        self.chip, self.core = tensor // 2, tensor % 2
        self.over_x = (self.row * 2 + 1 - self.col, tensor)
        self.over_y = ((1 - self.row) * 2 + self.col, tensor)
        self.beside = (dp, self.chip * 2 + 1 - self.core)
        self.left = (dp, jnp.maximum(tensor - 2, 0))
        self.right = (dp, jnp.minimum(tensor + 2, 2 * self.chips - 1))

    def on_line(self, chip):
        return (self.dp, chip * 2 + self.core)

    def index(self, row, col, chip, core):
        return ((row * 2 + col) * self.chips + chip) * 2 + core


def greet(spot, plane, line):
    barrier = pltpu.get_barrier_semaphore()
    peers = [spot.beside] + ([spot.over_x, spot.over_y] if plane else [])
    for peer in peers:
        pl.semaphore_signal(barrier, inc=1, device_id=peer, device_id_type=MESH)
    count = len(peers)
    if line == "all":
        for chip in range(spot.chips):

            @pl.when(spot.chip != chip)
            def _():
                pl.semaphore_signal(barrier, inc=1, device_id=spot.on_line(chip), device_id_type=MESH)

        count = count + spot.chips - 1
    elif line == "near":
        has_left, has_right = spot.chip > 0, spot.chip < spot.chips - 1

        @pl.when(has_left)
        def _():
            pl.semaphore_signal(barrier, inc=1, device_id=spot.left, device_id_type=MESH)

        @pl.when(has_right)
        def _():
            pl.semaphore_signal(barrier, inc=1, device_id=spot.right, device_id_type=MESH)

        count = count + jnp.where(has_left, 1, 0) + jnp.where(has_right, 1, 0)
    pl.semaphore_wait(barrier, count)


def remote(src, dst, send_sem, recv_sem, device):
    return pltpu.make_async_remote_copy(
        src_ref=src,
        dst_ref=dst,
        send_sem=send_sem,
        recv_sem=recv_sem,
        device_id=device,
        device_id_type=MESH,
    )


class Line:
    def __init__(self, spot, block_ref, line_ref, local_sem, send_sem, recv_sem):
        self.spot, self.line = spot, line_ref
        self.send_sem, self.recv_sem = send_sem, recv_sem
        self.local = pltpu.make_async_copy(block_ref, line_ref.at[spot.chip], local_sem)

    def copy(self, there, way):
        here = self.line.at[there]
        peer = (self.spot.left, self.spot.right)[way]
        return remote(here, here, self.send_sem.at[way, there], self.recv_sem.at[there], peer)

    def ways(self, there):
        chip, chips = self.spot.chip, self.spot.chips
        return ((chip > 0) & (there >= chip), (chip < chips - 1) & (there <= chip))

    def send(self, there):
        for way, when in enumerate(self.ways(there)):
            pl.when(when)(self.copy(there, way).start)

    def start(self):
        self.local.wait()
        self.send(self.spot.chip)

    def forward(self, step):
        for there in (self.spot.chip - step, self.spot.chip + step):

            @pl.when((there >= 0) & (there < self.spot.chips))
            def _():
                here = self.line.at[there]
                remote(here, here, self.send_sem.at[0, there], self.recv_sem.at[there], self.spot.beside).wait_recv()
                self.send(there)

    def end(self):
        for there in range(self.spot.chips):
            for way, when in enumerate(self.ways(there)):
                pl.when(when)(self.copy(there, way).wait_send)


def line_kernel(block_ref, line_ref, local_sem, send_sem, recv_sem):
    spot = Spot()
    line = Line(spot, block_ref, line_ref, local_sem, send_sem, recv_sem)
    line.local.start()
    greet(spot, False, "near")
    line.start()
    for step in range(1, spot.chips):
        line.forward(step)
    line.end()


def plane_kernel(more, line_ref, *refs):
    spot = Spot()
    if more:
        block_ref, whole_ref, next_ref, local_sem, send_sem, recv_sem, *sems = refs
        line = Line(spot, block_ref, next_ref, *sems)
        line.local.start()
    else:
        whole_ref, local_sem, send_sem, recv_sem = refs
    chips, chip, core, row, col = spot.chips, spot.chip, spot.core, spot.row, spot.col
    cut = chips // 2

    def local(there):
        return pltpu.make_async_copy(
            line_ref.at[there], whole_ref.at[spot.index(row, col, there, core)], local_sem.at[there]
        )

    for there in range(chips):
        local(there).start()
    greet(spot, True, "near" if more else None)
    if more:
        line.start()
    sent = []

    def send(index, device, source=None):
        source = whole_ref.at[index] if source is None else source
        copy = remote(source, whole_ref.at[index], send_sem.at[len(sent)], recv_sem.at[index], device)
        sent.append(copy)
        copy.start()

    def arrive(index):
        remote(
            whole_ref.at[index], whole_ref.at[index], send_sem.at[0], recv_sem.at[index], spot.beside
        ).wait_recv()

    for there in range(chips):
        index = spot.index(row, col, there, core)
        for peer in (spot.over_x, spot.over_y, spot.beside):
            send(index, peer, line_ref.at[there])
    for there in range(chips):
        across_x = spot.index(row, 1 - col, there, core)
        arrive(across_x)
        if there < cut:
            send(across_x, spot.over_y)
        send(across_x, spot.beside)
        across_y = spot.index(1 - row, col, there, core)
        arrive(across_y)
        if there >= cut:
            send(across_y, spot.over_x)
        send(across_y, spot.beside)
        if more and 0 < there:
            line.forward(there)
    for there in range(chips):
        index = spot.index(1 - row, 1 - col, there, core)
        arrive(index)
        send(index, spot.beside)
    for plane in range(4):
        for there in range(chips):
            arrive(spot.index(plane // 2, plane % 2, there, 1 - core))
    for there in range(chips):
        local(there).wait()
    for copy in sent:
        copy.wait_send()
    if more:
        line.end()


def gather_line(block, collective_id):
    chips = lax.axis_size("tensor") // 2
    dma = pltpu.SemaphoreType.DMA
    return pl.pallas_call(
        line_kernel,
        in_specs=[pl.BlockSpec(memory_space=pl.ANY)],
        out_specs=pl.BlockSpec(memory_space=pl.ANY),
        out_shape=jax.ShapeDtypeStruct((chips,) + block.shape, B16),
        scratch_shapes=[dma, dma((2, chips)), dma((chips,))],
        compiler_params=pltpu.CompilerParams(
            collective_id=collective_id, has_side_effects=True, vmem_limit_bytes=VMEM_LIMIT
        ),
        cost_estimate=pl.CostEstimate(flops=0, bytes_accessed=block.size * 100, transcendentals=0),
    )(block)


def gather_plane(line, collective_id, more=None):
    chips, size, width = line.shape
    dma = pltpu.SemaphoreType.DMA
    anywhere = pl.BlockSpec(memory_space=pl.ANY)
    shapes = [jax.ShapeDtypeStruct((8 * chips, size, width), B16)]
    sems = [dma((chips,)), dma((10 * chips,)), dma((8 * chips,))]
    if more is not None:
        shapes.append(jax.ShapeDtypeStruct((chips,) + more.shape, B16))
        sems += [dma, dma((2, chips)), dma((chips,))]
    out = pl.pallas_call(
        functools.partial(plane_kernel, more is not None),
        in_specs=[anywhere] * len(shapes),
        out_specs=[anywhere] * len(shapes),
        out_shape=shapes,
        scratch_shapes=sems,
        compiler_params=pltpu.CompilerParams(
            collective_id=collective_id, has_side_effects=True, vmem_limit_bytes=VMEM_LIMIT
        ),
        cost_estimate=pl.CostEstimate(flops=0, bytes_accessed=line.size * 60, transcendentals=0),
    )(line, *([] if more is None else [more]))
    return (out[0].reshape(8 * chips * size, width), *out[1:])


def scatter_kernel(parts, arrays, *refs):
    grads, outs = refs[:arrays], refs[arrays : 2 * arrays]
    mine, got, over_x, over_y, across_x, across_y, line, load_sem, send_sem, recv_sem = refs[2 * arrays :]
    spot = Spot()
    chips, chip, core, row, col = spot.chips, spot.chip, spot.core, spot.row, spot.col
    cut = chips // 2

    def at(r, c, z):
        return (r * 2 + c) * chips + z

    def lanes(p):
        return pl.ds(parts[p][0], parts[p][1])

    def source(p, which):
        _, width, array, start = parts[p]
        return grads[array].at[:, which, :, pl.ds(start, width)]

    def load(p):
        return pltpu.make_async_copy(source(p, core), mine.at[:, :, lanes(p)], load_sem.at[p])

    def swapped(p):
        return remote(
            source(p, 1 - core), got.at[:, :, lanes(p)], send_sem.at[p, 0], recv_sem.at[p, 0], spot.beside
        )

    def first(p):
        cols = lanes(p)
        copies = []
        for side in range(2):
            copies.append(
                remote(
                    mine.at[pl.ds(at(side, 1 - col, 0), cut), :, cols],
                    over_x.at[pl.ds(side * cut, cut), :, cols],
                    send_sem.at[p, 1 + side],
                    recv_sem.at[p, 1 + side],
                    spot.over_x,
                )
            )
            copies.append(
                remote(
                    mine.at[pl.ds(at(1 - row, side, cut), chips - cut), :, cols],
                    over_y.at[pl.ds(side * (chips - cut), chips - cut), :, cols],
                    send_sem.at[p, 3 + side],
                    recv_sem.at[p, 3 + side],
                    spot.over_y,
                )
            )
        return copies

    def second(p):
        cols = lanes(p)
        return [
            remote(
                mine.at[pl.ds(at(1 - row, col, 0), cut), :, cols],
                across_y.at[:, :, cols],
                send_sem.at[p, 5],
                recv_sem.at[p, 5],
                spot.over_y,
            ),
            remote(
                mine.at[pl.ds(at(row, 1 - col, cut), chips - cut), :, cols],
                across_x.at[:, :, cols],
                send_sem.at[p, 6],
                recv_sem.at[p, 6],
                spot.over_x,
            ),
        ]

    def third(p, other):
        cols = lanes(p)
        return remote(
            mine.at[at(row, col, other), :, cols],
            line.at[chip, :, cols],
            send_sem.at[p, 7 + other],
            recv_sem.at[p, 7 + chip],
            spot.on_line(other),
        )

    def add(p, target, start, source, begin, count):
        cols = lanes(p)

        def body(step, _):
            target[start + step, :, cols] = (
                target[start + step, :, cols].astype(F32) + source[begin + step, :, cols].astype(F32)
            ).astype(B16)
            return 0

        lax.fori_loop(0, count, body, 0)

    def stage_one(p):
        load(p).wait()
        swapped(p).wait()
        add(p, mine, 0, got, 0, 4 * chips)
        for copy in first(p):
            copy.start()

    def stage_two(p):
        for copy in first(p):
            copy.wait()
        for side in range(2):
            add(p, mine, at(side, col, 0), over_x, side * cut, cut)
            add(p, mine, at(row, side, cut), over_y, side * (chips - cut), chips - cut)
        for copy in second(p):
            copy.start()

    def stage_three(p):
        for copy in second(p):
            copy.wait()
        add(p, mine, at(row, col, 0), across_y, 0, cut)
        add(p, mine, at(row, col, cut), across_x, 0, chips - cut)
        for other in range(chips):
            pl.when(chip != other)(third(p, other).start)

    def stage_four(p):
        cols = lanes(p)
        total = mine[at(row, col, chip), :, cols].astype(F32)
        for other in range(chips):

            @pl.when(chip != other)
            def _():
                here = line.at[other, :, cols]
                remote(here, here, send_sem.at[p, 7 + other], recv_sem.at[p, 7 + other], spot.beside).wait_recv()

            total = total + line[other, :, cols].astype(F32)
        _, width, array, start = parts[p]
        outs[array][:, start : start + width] = total
        for other in range(chips):
            pl.when(chip != other)(third(p, other).wait_send)

    for p in range(len(parts)):
        load(p).start()
    line[chip] = jnp.zeros(line.shape[1:], B16)
    greet(spot, True, "all")
    for p in range(len(parts)):
        swapped(p).start()
    stages = (stage_one, stage_two, stage_three, stage_four)
    for step in range(len(parts) + len(stages) - 1):
        for late, stage in enumerate(stages):
            if 0 <= step - late < len(parts):
                stage(step - late)


def scatter_weights(grads, collective_id):
    total = grads[0].shape[0]
    devices = lax.axis_size(("dp", "tensor"))
    size = total // devices
    if lax.axis_size("dp") != 4:
        return [
            lax.psum_scatter(array, ("dp", "tensor"), scatter_dimension=0, tiled=True).astype(F32)
            for array in grads
        ]
    chips = lax.axis_size("tensor") // 2
    cut = chips // 2
    parts, width = [], 0
    for at, array in enumerate(grads):
        count = pl.cdiv(array.shape[1], SCATTER_LANES)
        tiles = array.shape[1] // 128
        ends = [tiles * p // count * 128 for p in range(count + 1)]
        for start, end in zip(ends, ends[1:]):
            parts.append((width + start, end - start, at, start))
        width += array.shape[1]
    dma = pltpu.SemaphoreType.DMA
    return pl.pallas_call(
        functools.partial(scatter_kernel, parts, len(grads)),
        in_specs=[pl.BlockSpec(memory_space=pl.ANY)] * len(grads),
        out_specs=[pl.BlockSpec(memory_space=pltpu.VMEM)] * len(grads),
        out_shape=[jax.ShapeDtypeStruct((size, array.shape[1]), F32) for array in grads],
        scratch_shapes=[
            pltpu.VMEM((4 * chips, size, width), B16),
            pltpu.VMEM((4 * chips, size, width), B16),
            pltpu.VMEM((2 * cut, size, width), B16),
            pltpu.VMEM((2 * (chips - cut), size, width), B16),
            pltpu.VMEM((chips - cut, size, width), B16),
            pltpu.VMEM((cut, size, width), B16),
            pltpu.VMEM((chips, size, width), B16),
            dma((len(parts),)),
            dma((len(parts), 7 + chips)),
            dma((len(parts), 7 + chips)),
        ],
        compiler_params=pltpu.CompilerParams(
            collective_id=collective_id, has_side_effects=True, vmem_limit_bytes=VMEM_LIMIT
        ),
        cost_estimate=pl.CostEstimate(flops=0, bytes_accessed=devices * size * width * 8, transcendentals=0),
    )(*[array.reshape(devices // 2, 2, size, array.shape[1]) for array in grads])


class Named:
    def __init__(self, names, refs):
        for name, ref in zip(names, refs, strict=True):
            setattr(self, name, ref)


def project_kernel(hidden_ref, weight_ref, bias_ref, cos_ref, sin_ref, out_ref):
    chunk = pl.program_id(0)
    turned = chunk < (QW + KW) // 256
    lin = dot(hidden_ref[...], weight_ref[...]) + bias_ref[...]
    for head in range(2):
        cut = pl.ds(head * HD, HD)
        one = lin[:, head * HD : (head + 1) * HD]
        rot = one * cos_ref[...] + pltpu.roll(one, HD // 2, 1) * sin_ref[...]
        out_ref[:, cut] = jnp.where(turned, rot, one).astype(B16)


def project(hidden, weights, bias, cosine, sine):
    rows, depth = hidden.shape
    return pl.pallas_call(
        project_kernel,
        grid=(QKV // 256,),
        in_specs=[
            pl.BlockSpec((rows, depth), lambda j: (0, 0)),
            pl.BlockSpec((depth, 256), lambda j: (0, j)),
            pl.BlockSpec((1, 256), lambda j: (0, j)),
            pl.BlockSpec((rows, HD), lambda j: (0, 0)),
            pl.BlockSpec((rows, HD), lambda j: (0, 0)),
        ],
        out_specs=pl.BlockSpec((rows, 256), lambda j: (0, j)),
        out_shape=jax.ShapeDtypeStruct((rows, QKV), B16),
        compiler_params=pltpu.CompilerParams(vmem_limit_bytes=VMEM_LIMIT),
        cost_estimate=pl.CostEstimate(
            flops=2 * rows * depth * QKV,
            bytes_accessed=2 * (depth * QKV + rows * depth + rows * QKV),
            transcendentals=0,
        ),
    )(hidden, weights, bias, cosine, sine)


def fill_bias(info_ref, bias):
    shape = bias.shape
    place = info_ref[1] + lax.broadcasted_iota(jnp.int32, shape, 0)
    keys = lax.broadcasted_iota(jnp.int32, shape, 1)
    bias[...] = jnp.where((keys <= place) & (keys < info_ref[0]), 0.0, MASKED)


def flat(ref):
    return ref[...].reshape(ref.shape[0] * ref.shape[2], ref.shape[3])


def attend_kernel(info_ref, q_ref, k_ref, v_ref, out_ref, log_ref, bias):
    @pl.when(pl.program_id(0) == 0)
    def _():
        fill_bias(info_ref, bias)

    keys, values = flat(k_ref), flat(v_ref)
    for head in range(HEADS):
        cut = slice(head * HD, (head + 1) * HD)
        scores = dot_t(q_ref[:, cut], keys) * (HD**-0.5 * LOG2E) + bias[...]
        top = jnp.max(scores, axis=-1, keepdims=True)
        expd = jnp.exp2(scores - top)
        summed = jnp.sum(expd, axis=-1, keepdims=True)
        out_ref[:, cut] = (dot(expd.astype(B16), values) * (1.0 / summed)).astype(B16)
        log_ref[:, cut] = jnp.broadcast_to(top + jnp.log2(summed), (q_ref.shape[0], HD))


def attend(info, micro, qkv, keys_values, rows):
    parts = keys_values.shape[0]
    total = parts * rows
    return pl.pallas_call(
        attend_kernel,
        grid_spec=pltpu.PrefetchScalarGridSpec(
            num_scalar_prefetch=1,
            grid=(H // HEADS,),
            in_specs=[
                pl.BlockSpec((rows, HEADS * HD), lambda h, info: (micro, h)),
                pl.BlockSpec((parts, 1, rows, HD), lambda h, info: (0, micro, 0, h * HEADS // GROUPS)),
                pl.BlockSpec((parts, 1, rows, HD), lambda h, info: (0, micro, 0, KV + h * HEADS // GROUPS)),
            ],
            out_specs=[
                pl.BlockSpec((rows, HEADS * HD), lambda h, info: (0, h)),
                pl.BlockSpec((rows, HEADS * HD), lambda h, info: (0, h)),
            ],
            scratch_shapes=[pltpu.VMEM((rows, total), F32)],
        ),
        out_shape=[
            jax.ShapeDtypeStruct((rows, QW), B16),
            jax.ShapeDtypeStruct((rows, QW), F32),
        ],
        compiler_params=pltpu.CompilerParams(vmem_limit_bytes=VMEM_LIMIT),
        cost_estimate=pl.CostEstimate(
            flops=8 * rows * total * QW,
            bytes_accessed=4 * total * KW + 8 * rows * QW,
            transcendentals=H * rows * total,
        ),
    )(info, qkv, keys_values, keys_values)


def attend_back_kernel(names, parts, *refs):
    r = Named(names, refs)
    spot = Spot()
    chips, chip, core = spot.chips, spot.chip, spot.core
    rows = r.q.shape[0]
    step = pl.program_id(0)
    micros = r.sums.shape[0]
    turns = H // HEADS
    micro, turn = step // turns, lax.rem(step, turns)
    span = GROUPS // HEADS
    pieces = micros * KV
    scale = HD**-0.5

    def rows_of(block, which):
        return pl.ds(pl.multiple_of((2 * block + which) * rows, rows), rows)

    def swapped(piece):
        mine = r.part.at[piece, :, 1 - core]
        return remote(mine, r.xrecv.at[piece], r.xsend.at[piece], r.xrecv_sem.at[piece], spot.beside)

    def along(piece, block):
        return remote(
            r.part.at[piece, block, core],
            r.zrecv.at[piece, chip],
            r.zsend.at[piece, block],
            r.zrecv_sem.at[piece, chip],
            spot.on_line(block),
        )

    def spread(piece):
        swapped(piece).wait_recv()
        for block in range(chips):
            total = r.part[piece, block, core].astype(F32) + r.xrecv[piece, block].astype(F32)
            r.part[piece, block, core] = total.astype(B16)
            pl.when(chip != block)(along(piece, block).start)

    @pl.when(step == 0)
    def _():
        greet(spot, False, "all")

    @pl.when(turn == 0)
    def _():
        shape = r.bias.shape
        place = spot.tensor * rows + lax.broadcasted_iota(jnp.int32, shape, 0)
        keys_at = lax.broadcasted_iota(jnp.int32, shape, 1)
        r.bias[...] = jnp.where((keys_at <= place) & (keys_at < r.length[micro]), 0.0, MASKED)

    keys, values = flat(r.k), flat(r.v)
    grad_k = grad_v = 0.0
    for head in range(HEADS):
        cut = slice(head * HD, (head + 1) * HD)
        queries, grads = r.q[:, cut], r.g[:, cut]
        scores = dot_t(queries, keys) * (scale * LOG2E) + r.bias[...]
        probs = jnp.exp2(scores - r.log[:, head * HD : head * HD + 1])
        grad_probs = dot_t(grads, values)
        inner = jnp.sum(grad_probs * probs, axis=-1, keepdims=True)
        grad_scores = (probs * (grad_probs - inner)).astype(B16)
        grad_q = dot(grad_scores, keys) * scale
        turned = grad_q * r.cos[...] - pltpu.roll(grad_q, HD // 2, 1) * r.sin[...]
        r.dq[:, cut] = turned.astype(B16)
        grad_k = grad_k + t_dot(grad_scores, queries)
        grad_v = grad_v + t_dot(probs.astype(B16), grads)
    first = lax.rem(turn, span) == 0

    @pl.when(first)
    def _():
        r.dk_acc[...] = grad_k
        r.dv_acc[...] = grad_v

    @pl.when(jnp.logical_not(first))
    def _():
        r.dk_acc[...] += grad_k
        r.dv_acc[...] += grad_v

    for piece in range(pieces):

        @pl.when(step == (piece + 1) * span - 1)
        def _():
            shape = (chips, 2, rows, HD)
            r.part[piece, :, :, :, :HD] = (r.dk_acc[...] * scale).reshape(shape).astype(B16)
            r.part[piece, :, :, :, HD:] = r.dv_acc[...].reshape(shape).astype(B16)
            swapped(piece).start()

        if piece + 1 < pieces:

            @pl.when(step == (piece + 1) * span)
            def _():
                spread(piece)

    @pl.when(step == pieces * span - 1)
    def _():
        spread(pieces - 1)
        for piece in range(pieces):
            total = r.part[piece, chip, core].astype(F32)
            for other in range(chips):

                @pl.when(chip != other)
                def _():
                    here = r.zrecv.at[piece, other]
                    remote(
                        here, here, r.zsend.at[piece, other], r.zrecv_sem.at[piece, other], spot.beside
                    ).wait_recv()

                got = jnp.where(chip != other, r.zrecv[piece, other], jnp.zeros((rows, 2 * HD), B16))
                total = total + got.astype(F32)
            at, group = piece // KV, piece % KV
            grad = total[:, :HD]
            grad = grad * r.cos[...] - pltpu.roll(grad, HD // 2, 1) * r.sin[...]
            r.sums[at, :, group * HD : (group + 1) * HD] = grad.astype(B16)
            r.sums[at, :, KW + group * HD : KW + (group + 1) * HD] = total[:, HD:].astype(B16)
        for piece in range(pieces):
            swapped(piece).wait_send()
            for block in range(chips):
                pl.when(chip != block)(along(piece, block).wait_send)


def attend_back(lengths, qkv, keys_values, grads, logs, cosine, sine, rows, collective_id):
    parts, micros = keys_values.shape[:2]
    chips = parts // 2
    total = parts * rows
    pieces = micros * KV
    turns = H // HEADS
    dma = pltpu.SemaphoreType.DMA
    vmem = pltpu.VMEM

    def heads(step):
        return (step // turns, step % turns)

    inputs = {
        "length": (pl.BlockSpec(memory_space=pltpu.SMEM), lengths),
        "q": (pl.BlockSpec((rows, HEADS * HD), heads), qkv),
        "k": (
            pl.BlockSpec((parts, 1, rows, HD), lambda s: (0, s // turns, 0, s % turns * HEADS // GROUPS)),
            keys_values,
        ),
        "v": (
            pl.BlockSpec((parts, 1, rows, HD), lambda s: (0, s // turns, 0, KV + s % turns * HEADS // GROUPS)),
            keys_values,
        ),
        "g": (pl.BlockSpec((rows, HEADS * HD), heads), grads),
        "log": (pl.BlockSpec((rows, HEADS * HD), heads), logs),
        "cos": (pl.BlockSpec((rows, HD), lambda s: (0, 0)), cosine),
        "sin": (pl.BlockSpec((rows, HD), lambda s: (0, 0)), sine),
    }
    outputs = {
        "dq": (pl.BlockSpec((rows, HEADS * HD), heads), jax.ShapeDtypeStruct((micros * rows, QW), B16)),
        "sums": (
            pl.BlockSpec((micros, rows, 2 * KW), lambda s: (0, 0, 0)),
            jax.ShapeDtypeStruct((micros, rows, 2 * KW), B16),
        ),
    }
    scratch = {
        "bias": vmem((rows, total), F32),
        "dk_acc": vmem((total, HD), F32),
        "dv_acc": vmem((total, HD), F32),
        "part": vmem((pieces, chips, 2, rows, 2 * HD), B16),
        "xrecv": vmem((pieces, chips, rows, 2 * HD), B16),
        "zrecv": vmem((pieces, chips, rows, 2 * HD), B16),
        "xsend": dma((pieces,)),
        "xrecv_sem": dma((pieces,)),
        "zsend": dma((pieces, chips)),
        "zrecv_sem": dma((pieces, chips)),
    }
    return pl.pallas_call(
        functools.partial(attend_back_kernel, [*inputs, *outputs, *scratch], parts),
        grid=(micros * turns,),
        in_specs=[spec for spec, _ in inputs.values()],
        out_specs=[spec for spec, _ in outputs.values()],
        out_shape=[shape for _, shape in outputs.values()],
        scratch_shapes=list(scratch.values()),
        compiler_params=pltpu.CompilerParams(
            collective_id=collective_id, has_side_effects=True, vmem_limit_bytes=VMEM_LIMIT
        ),
        cost_estimate=pl.CostEstimate(
            flops=20 * micros * rows * total * QW,
            bytes_accessed=micros * (8 * total * KW + 12 * rows * QW),
            transcendentals=micros * H * rows * total,
        ),
    )(*[value for _, value in inputs.values()])


def mlp_kernel(names, reduced, *refs):
    r = Named(names, refs)
    has_next, has_prior = "own" in names, "prior" in names
    spot = Spot()
    chips, chip, core, row, col = spot.chips, spot.chip, spot.core, spot.row, spot.col
    units, depth = r.wg.shape
    rows = r.grad.shape[0]
    pair = 2 * rows
    quarter = depth // 4
    chunks = [(i * CHUNK, min(CHUNK, units - i * CHUNK)) for i in range(pl.cdiv(units, CHUNK))]
    whole_chunks, rest = units // CHUNK, units % CHUNK
    wide = depth // 2

    def block_at(step):
        return nearest(chips, chip, chips - 1 - step)

    def span(block):
        return pl.ds(pl.multiple_of(block * pair, pair), pair)

    def rows_of(block, which):
        return pl.ds(pl.multiple_of(block * pair + which * rows, rows), rows)

    def columns(index, width=CHUNK):
        return pl.ds(pl.multiple_of(index * width, width), width)

    def weight_load(index):
        cut = pl.ds(*chunks[index])
        return [
            pltpu.make_async_copy(src.at[cut], dst.at[cut], r.weight_sem.at[i, index])
            for i, (src, dst) in enumerate(((r.wg_hbm, r.wg), (r.wu_hbm, r.wu), (r.wd_hbm, r.wd)))
        ]

    def weights_here(index, width=CHUNK):
        for i, dst in enumerate((r.wg, r.wu, r.wd)):
            cut = dst.at[pl.ds(index * CHUNK, width)]
            pltpu.make_async_copy(cut, cut, r.weight_sem.at[i, index]).wait()

    def h_load(block):
        return pltpu.make_async_copy(r.h_hbm.at[span(block)], r.h.at[span(block)], r.load_sem.at[0, block])

    def g_load(block):
        return pltpu.make_async_copy(r.cot.at[span(block)], r.g.at[span(block)], r.load_sem.at[1, block])

    def gather_send(block, way):
        here = r.whole.at[rows_of(block, core)]
        peer = (spot.left, spot.right, spot.beside)[way]
        return remote(here, here, r.gather_send.at[way, block], r.gather_recv.at[block, core], peer)

    def gather_first(way):
        peer = (spot.left, spot.right, spot.beside)[way]
        here = r.whole.at[rows_of(chip, core)]
        return remote(r.own, here, r.gather_send.at[way, chip], r.gather_recv.at[chip, core], peer)

    def gathered(block, which):
        here = r.whole.at[rows_of(block, which)]
        remote(here, here, r.gather_send.at[2, block], r.gather_recv.at[block, which], spot.beside).wait_recv()

    def own_copy():
        return pltpu.make_async_copy(r.own, r.whole.at[rows_of(chip, core)], r.local_sem)

    def gather_start():
        own_copy().start()
        pl.when(chip > 0)(gather_first(0).start)
        pl.when(chip < chips - 1)(gather_first(1).start)
        gather_first(2).start()

    def gather_forward(step):
        block = chip - step

        @pl.when(block >= 0)
        def _():
            gathered(block, core)
            pl.when(chip < chips - 1)(gather_send(block, 1).start)
            gather_send(block, 2).start()

        after = chip + step

        @pl.when(after < chips)
        def _():
            gathered(after, core)
            pl.when(chip > 0)(gather_send(after, 0).start)
            gather_send(after, 2).start()

    def gather_end():
        own_copy().wait()
        for block in range(chips):
            gathered(block, 1 - core)
        for block in range(chips):
            away = block != chip
            pl.when((chip > 0) & (block >= chip) & away)(gather_send(block, 0).wait_send)
            pl.when((chip < chips - 1) & (block <= chip) & away)(gather_send(block, 1).wait_send)
            pl.when(away)(gather_send(block, 2).wait_send)
        pl.when(chip > 0)(gather_first(0).wait_send)
        pl.when(chip < chips - 1)(gather_first(1).wait_send)
        gather_first(2).wait_send()

    def swapped(block):
        return remote(
            r.part.at[rows_of(block, 1 - core)],
            r.xrecv.at[block],
            r.xsend.at[block],
            r.xrecv_sem.at[block],
            spot.beside,
        )

    def along(block, ahead):
        slot = chips - 1 - block if ahead else chips - block
        return remote(
            r.part.at[rows_of(block, core)],
            r.zrecv.at[slot],
            r.zsend.at[block],
            r.zrecv_sem.at[slot],
            spot.right if ahead else spot.left,
        )

    def finish(block):
        swapped(block).wait_recv()
        total = r.part[rows_of(block, core), :].astype(F32) + r.xrecv[block].astype(F32)

        @pl.when(block == chip)
        def _():
            r.grad[...] = total

        @pl.when(block != chip)
        def _():
            r.part[rows_of(block, core), :] = total.astype(B16)
            pl.when(chip == 0)(along(block, True).start)
            pl.when(chip == chips - 1)(along(block, False).start)

    def relay_one(block, ahead):
        slot = chips - 1 - block if ahead else chips - block
        remote(
            r.zrecv.at[slot], r.zrecv.at[slot], r.zsend.at[block], r.zrecv_sem.at[slot], spot.beside
        ).wait_recv()

        @pl.when(block == chip)
        def _():
            r.grad[...] = r.grad[...] + r.zrecv[slot].astype(F32)

        @pl.when(block != chip)
        def _():
            here = rows_of(block, core)
            r.part[here, :] = (r.part[here, :].astype(F32) + r.zrecv[slot].astype(F32)).astype(B16)
            along(block, ahead).start()

    def relay(point):
        step = point - (chip - 1)

        @pl.when((chip > 0) & (step >= 0) & (step < chips - chip))
        def _():
            relay_one(chips - 1 - step, True)

        back_step = point - (chips - 2 - chip)

        @pl.when((chip < chips - 1) & (back_step >= 0) & (back_step <= chip))
        def _():
            relay_one(back_step, False)

    def gates(step, block):
        here = span(block)

        def one(start, width):
            cut = pl.ds(start, width)
            gate = dot_t(r.h[here, :], r.wg[cut, :])
            up = dot_t(r.h[here, :], r.wu[cut, :])
            grad = dot_t(r.g[here, :], r.wd[cut, :])
            sigma = jax.nn.sigmoid(gate)
            silu = gate * sigma
            r.act[here, cut] = (silu * up).astype(B16)
            r.dg[here, cut] = (grad * up * sigma * (1.0 + gate * (1.0 - sigma))).astype(B16)
            r.du[here, cut] = (grad * silu).astype(B16)

        def chunk(index, _):
            pl.when(step == 0)(functools.partial(weights_here, index))
            one(pl.multiple_of(index * CHUNK, CHUNK), CHUNK)
            return 0

        lax.fori_loop(0, whole_chunks, chunk, 0)
        if rest:
            pl.when(step == 0)(functools.partial(weights_here, whole_chunks, rest))
            one(whole_chunks * CHUNK, rest)

    def back(block):
        here = span(block)

        def chunk(index, _):
            cut = columns(index, wide)
            grad = dot(r.dg[here, :], r.wg[:, cut]) + dot(r.du[here, :], r.wu[:, cut])
            r.part[here, cut] = grad.astype(B16)
            return 0

        lax.fori_loop(0, depth // wide, chunk, 0)
        swapped(block).start()

    def put_out(block, index):
        cut = pl.ds(index * wide, wide)
        return pltpu.make_async_copy(
            r.stage_out.at[:, cut], r.out.at[span(block), cut], r.out_sem.at[index]
        )

    def out_block(block):
        for index in range(2):
            pl.when(block > 0)(put_out(block, index).wait)
            cut = slice(index * wide, (index + 1) * wide)
            r.stage_out[:, cut] = dot(r.act[span(block), :], r.wd[:, cut]).astype(B16)
            put_out(block, index).start()

    def place(matrix, start, width):
        return pl.ds(pl.multiple_of(matrix * units + start, 16), width)

    def exchanged(matrix, index, start, width, over_x):
        here = place(matrix, start, width)
        at = matrix * len(chunks) + index
        source = r.sums.at[:, 1 - col, here] if over_x else r.sums.at[1 - row, :, here]
        peer = spot.over_x if over_x else spot.over_y
        return remote(source, r.landing.at[:, here], r.one_send.at[at], r.one_recv.at[at], peer)

    def exchange_start(matrix, index, start, width):
        first = lax.rem(matrix + index, 2) == 0
        pl.when(first)(exchanged(matrix, index, start, width, True).start)
        pl.when(jnp.logical_not(first))(exchanged(matrix, index, start, width, False).start)

    def exchange_copies(matrix, index, slot):
        start, width = chunks[index]
        here = place(matrix, start, width)
        cut = pl.ds(0, width)
        own = r.sums.at[:, col, here] if (matrix + index) % 2 == 0 else r.sums.at[row, :, here]
        return [
            pltpu.make_async_copy(own, r.held_own.at[slot, :, cut], r.held_sem.at[slot, 0]),
            pltpu.make_async_copy(r.landing.at[:, here], r.held_got.at[slot, :, cut], r.held_sem.at[slot, 1]),
        ]

    def exchange_load(matrix, index, slot):
        exchanged(matrix, index, *chunks[index], (matrix + index) % 2 == 0).wait_recv()
        for copy in exchange_copies(matrix, index, slot):
            copy.start()

    def exchange(matrix, index, slot):
        start, width = chunks[index]
        for copy in exchange_copies(matrix, index, slot):
            copy.wait()
        mine = row if (matrix + index) % 2 == 0 else col
        r.shard[place(matrix, start, width), :] = (
            r.held_own[slot, mine, :width].astype(F32) + r.held_got[slot, mine, :width].astype(F32)
        ).astype(B16)
        r.rest[place(matrix, start, width), :] = (
            r.held_own[slot, 1 - mine, :width].astype(F32) + r.held_got[slot, 1 - mine, :width].astype(F32)
        ).astype(B16)
        passed(matrix, index).start()

    def passed(matrix, index):
        start, width = chunks[index]
        here = place(matrix, start, width)
        at = matrix * len(chunks) + index
        peer = spot.over_y if (matrix + index) % 2 == 0 else spot.over_x
        return remote(r.rest.at[here], r.got_rest.at[here], r.two_send.at[at], r.two_recv.at[at], peer)

    def weight_grads(matrix, left, right):
        def put(start, width, slot):
            return pltpu.make_async_copy(
                r.stage.at[slot, :, :, pl.ds(0, width)],
                r.sums.at[:, :, place(matrix, start, width)],
                r.stage_sem.at[slot],
            )

        def one(index, start, width, slot):
            if has_prior:
                fetch = pltpu.make_async_copy(
                    r.prior.at[:, :, place(matrix, start, width)],
                    r.before.at[:, :, pl.ds(0, width)],
                    r.before_sem,
                )
                fetch.start()
            value = t_dot(left[:, pl.ds(start, width)], right[...])
            if has_prior:
                fetch.wait()
            for at in range(4):
                piece = value[:, at * quarter : (at + 1) * quarter]
                if has_prior:
                    piece = piece + r.before[at // 2, at % 2, :width].astype(F32)
                r.stage[slot, at // 2, at % 2, :width] = piece.astype(B16)
            put(start, width, slot).start()

        def sent(index, start, width, slot):
            put(start, width, slot).wait()
            if reduced:
                exchange_start(matrix, index, start, width)

        def body(index, _):
            slot = lax.rem(index, 2)
            start = pl.multiple_of(index * CHUNK, CHUNK)
            one(index, start, CHUNK, slot)

            @pl.when(index > 0)
            def _():
                sent(index - 1, start - CHUNK, CHUNK, 1 - slot)

            return 0

        lax.fori_loop(0, whole_chunks, body, 0)
        index = whole_chunks
        if rest:
            one(index, index * CHUNK, rest, index % 2)
            if index:
                sent(index - 1, (index - 1) * CHUNK, CHUNK, (index - 1) % 2)
            sent(index, index * CHUNK, rest, index % 2)
        else:
            sent(index - 1, (index - 1) * CHUNK, CHUNK, (index - 1) % 2)

    for step in range(chips):
        h_load(block_at(step)).start()
        g_load(block_at(step)).start()
        if step == 0:
            for index in range(len(chunks)):
                for copy in weight_load(index):
                    copy.start()
    greet(spot, reduced, "near")
    if has_next:
        gather_start()

    def loaded(block):
        h_load(block).wait()
        g_load(block).wait()

    todo = [(matrix, index) for matrix in (2, 0, 1) for index in range(len(chunks))] if reduced else []
    share = pl.cdiv(len(todo), chips + 2)
    loading = []

    def some():
        for _ in range(share):
            if loading:
                exchange(*loading.pop(0))
            if todo:
                loading.append((*todo.pop(0), len(todo) % 2))
                exchange_load(*loading[-1])

    if has_next:

        def unit(step, _):
            block = block_at(step)
            loaded(block)
            gates(step, block)

            @pl.when(step > 0)
            def _():
                finish(block_at(step - 1))

            back(block)
            pl.when(step == 0)(functools.partial(gather_forward, 1))
            return 0

        lax.fori_loop(0, chips, unit, 0)
        finish(block_at(chips - 1))
        gather_forward(2)
        relay(0)
        weight_grads(2, r.act, r.g)
        for step in range(3, chips):
            gather_forward(step)
        weight_grads(0, r.dg, r.h)
        relay(1)
        weight_grads(1, r.du, r.h)
        for point in range(2, chips - 2):
            relay(point)
    else:

        def unit(step, _):
            block = block_at(step)
            loaded(block)
            gates(step, block)
            return 0

        def unit_back(step, _):
            back(block_at(step))

            @pl.when(step > 0)
            def _():
                finish(block_at(step - 1))

            return 0

        lax.fori_loop(0, chips, unit, 0)
        weight_grads(2, r.act, r.g)
        lax.fori_loop(0, chips, unit_back, 0)
        finish(block_at(chips - 1))
        weight_grads(0, r.dg, r.h)
        some()
        relay(0)
        weight_grads(1, r.du, r.h)
        some()
        for point in range(1, chips - 2):
            relay(point)
    for block in range(chips):
        out_block(jnp.int32(block))
        some()
    relay(chips - 2)
    some()
    for index in range(2):
        put_out(0, index).wait()
    if reduced:
        for matrix in (2, 0, 1):
            for index, (start, width) in enumerate(chunks):
                here = place(matrix, start, width)
                passed(matrix, index).wait_recv()
                r.shard[here, :] = (r.shard[here, :].astype(F32) + r.got_rest[here, :].astype(F32)).astype(B16)
        for matrix in range(3):
            for index, (start, width) in enumerate(chunks):
                passed(matrix, index).wait_send()
                exchanged(matrix, index, start, width, (matrix + index) % 2 == 0).wait_send()
    for block in range(chips):
        swapped(block).wait_send()
        pl.when(chip < block)(along(block, True).wait_send)
        pl.when(chip > block)(along(block, False).wait_send)
    if has_next:
        gather_end()


def mlp(cot, hidden, wg, wu, wd, own, prior, rows, collective_id):
    total, depth = hidden.shape
    units = wg.shape[0]
    chips = total // (2 * rows)
    reduced = own is None and lax.axis_size("dp") == 4
    quarter = depth // 4
    count = pl.cdiv(units, CHUNK)
    anywhere = pl.BlockSpec(memory_space=pl.ANY)
    local = pl.BlockSpec(memory_space=pltpu.VMEM)
    dma = pltpu.SemaphoreType.DMA
    vmem = pltpu.VMEM
    held = jax.ShapeDtypeStruct((3 * units, quarter), B16)

    inputs = {"cot": cot, "h_hbm": hidden, "wg_hbm": wg, "wu_hbm": wu, "wd_hbm": wd}
    if own is not None:
        inputs["own"] = own
    if prior is not None:
        inputs["prior"] = prior
    outputs = {
        "out": (anywhere, jax.ShapeDtypeStruct((total, depth), B16)),
        "grad": (local, jax.ShapeDtypeStruct((rows, depth), F32)),
        "sums": (anywhere, jax.ShapeDtypeStruct((2, 2, 3 * units, quarter), B16)),
    }
    if own is not None:
        outputs["whole"] = (anywhere, jax.ShapeDtypeStruct((total, depth), B16))
    if reduced:
        outputs["shard"] = (local, held)
        outputs["landing"] = (anywhere, jax.ShapeDtypeStruct((2, 3 * units, quarter), B16))
    scratch = {
        "wg": vmem((units, depth), B16),
        "wu": vmem((units, depth), B16),
        "wd": vmem((units, depth), B16),
        "h": vmem((total, depth), B16),
        "g": vmem((total, depth), B16),
        "act": vmem((total, units), B16),
        "dg": vmem((total, units), B16),
        "du": vmem((total, units), B16),
        "part": vmem((total, depth), B16),
        "xrecv": vmem((chips, rows, depth), B16),
        "zrecv": vmem((chips + 1, rows, depth), B16),
        "stage_out": vmem((2 * rows, depth), B16),
        "stage": vmem((2, 2, 2, CHUNK, quarter), B16),
        "weight_sem": dma((3, count)),
        "load_sem": dma((2, chips)),
        "xsend": dma((chips,)),
        "xrecv_sem": dma((chips,)),
        "zsend": dma((chips,)),
        "zrecv_sem": dma((chips + 1,)),
        "out_sem": dma((2,)),
        "stage_sem": dma((2,)),
    }
    if own is not None:
        scratch["local_sem"] = dma
        scratch["gather_send"] = dma((3, chips))
        scratch["gather_recv"] = dma((chips, 2))
    if prior is not None:
        scratch["before"] = vmem((2, 2, CHUNK, quarter), B16)
        scratch["before_sem"] = dma
    if reduced:
        scratch["rest"] = vmem(held.shape, B16)
        scratch["got_rest"] = vmem(held.shape, B16)
        scratch["two_send"] = dma((3 * count,))
        scratch["two_recv"] = dma((3 * count,))
        scratch["held_own"] = vmem((2, 2, CHUNK, quarter), B16)
        scratch["held_got"] = vmem((2, 2, CHUNK, quarter), B16)
        scratch["held_sem"] = dma((2, 2))
        scratch["one_send"] = dma((3 * count,))
        scratch["one_recv"] = dma((3 * count,))
    names = [*inputs, *outputs, *scratch]
    out = pl.pallas_call(
        functools.partial(mlp_kernel, names, reduced),
        in_specs=[anywhere] * len(inputs),
        out_specs=[spec for spec, _ in outputs.values()],
        out_shape=[shape for _, shape in outputs.values()],
        scratch_shapes=list(scratch.values()),
        compiler_params=pltpu.CompilerParams(
            collective_id=collective_id, has_side_effects=True, vmem_limit_bytes=VMEM_MOST
        ),
        cost_estimate=pl.CostEstimate(
            flops=18 * total * depth * units, bytes_accessed=40 * total * depth, transcendentals=total * units
        ),
    )(*inputs.values())
    return dict(zip(outputs, out))


def widen_kernel(first_ref, second_ref, third_ref, *outs):
    for source, out in zip((first_ref, second_ref, third_ref), outs):
        quarter = source.shape[2]
        for at in range(4):
            out[:, at * quarter : (at + 1) * quarter] = source[at].astype(F32)


def widen(quarters, units):
    quarter = quarters.shape[2]
    steps = next(n for n in range(4, units) if units % (16 * n) == 0)
    size = units // steps
    return pl.pallas_call(
        widen_kernel,
        grid=(steps,),
        in_specs=[
            pl.BlockSpec((4, size, quarter), functools.partial(lambda base, i: (0, base + i, 0), at * steps))
            for at in range(3)
        ],
        out_specs=[pl.BlockSpec((size, 4 * quarter), lambda i: (i, 0))] * 3,
        out_shape=[jax.ShapeDtypeStruct((units, 4 * quarter), F32)] * 3,
        compiler_params=pltpu.CompilerParams(vmem_limit_bytes=VMEM_LIMIT),
        cost_estimate=pl.CostEstimate(flops=0, bytes_accessed=72 * units * quarter, transcendentals=0),
    )(quarters, quarters, quarters)


def norm_back(grad_out, normed, factor, gain):
    inner = grad_out * gain
    grad_rows = factor * (inner - normed * jnp.mean(inner * normed, axis=-1, keepdims=True))
    return (grad_rows, jnp.sum(grad_out * normed, axis=0))


def normalize(rows, gain):
    factor = lax.rsqrt(jnp.mean(rows * rows, axis=-1, keepdims=True) + EPS)
    normed = rows * factor
    return (normed, factor, (normed * gain).astype(B16))


def on_device(
    layer_input,
    lengths,
    attn_gain,
    query_proj,
    query_bias,
    key_proj,
    key_bias,
    value_proj,
    value_bias,
    out_proj,
    mlp_gain,
    gate_proj,
    up_proj,
    down_proj,
    cotangent,
):
    micros = layer_input.shape[0]
    rows = layer_input.shape[2]
    depth = layer_input.shape[3]
    tensor = lax.axis_index("tensor")
    total = rows * lax.axis_size("tensor")
    devices = lax.axis_size(("dp", "tensor"))
    size = query_proj.shape[0]
    small = key_bias.shape[0]
    offset = tensor * rows
    positions = offset + jnp.arange(rows, dtype=jnp.int32)
    cosine, sine = rope_tables(positions)

    valid = (positions[None, :] < lengths).astype(F32).reshape(micros, rows, 1)
    grad_rows = cotangent[:, 0].astype(F32) * valid
    low_rows = [grad_rows[m].astype(B16) for m in range(micros)]

    tail = jnp.concatenate([key_bias, value_bias, jnp.zeros((size - 2 * small,), B16)])
    extra = jnp.stack([attn_gain, query_bias, mlp_gain, tail], axis=1)
    extra = jnp.pad(extra, ((0, 0), (0, EXTRA - 4)))
    block = jnp.concatenate([query_proj, key_proj, value_proj, extra], axis=1)
    square = lax.axis_size("dp") == 4
    low = low_rows[0]
    if square:
        line = gather_line(block, 0)
        line, low = lax.optimization_barrier((line, low))
    cots = [lax.all_gather(low, "tensor", axis=0, tiled=True)]
    if square:
        packed, wout_line = gather_plane(line, 1, out_proj)
    else:
        packed = lax.all_gather(block, ("dp", "tensor"), axis=0, tiled=True)
    vectors = packed[:, QKV : QKV + 4].astype(F32)
    gain_one, gain_two = vectors[:, 0], vectors[:, 2]
    tails = vectors[:, 3].reshape(devices, size)
    bias = jnp.concatenate(
        [vectors[:, 1], tails[:, :small].reshape(-1), tails[:, small : 2 * small].reshape(-1)]
    )[None, :]

    inputs = layer_input[:, 0].astype(F32).reshape(micros * rows, depth)
    normed_one, factor_one, hidden = normalize(inputs, gain_one)
    qkv = project(
        hidden, packed, bias, jnp.tile(cosine, (micros, 1)), jnp.tile(sine, (micros, 1))
    )
    infos = [jnp.stack([lengths[m, 0], offset]) for m in range(micros)]

    own_kv = qkv[:, QW:].reshape(micros, rows, 2 * KW)
    own_kv, *cots = lax.optimization_barrier((own_kv, *cots))
    all_kv = lax.all_gather(own_kv, "tensor", axis=0)
    if square:
        wout_line, own_kv = lax.optimization_barrier((wout_line, own_kv))
        (wout,) = gather_plane(wout_line, 6)
    else:
        wout = lax.all_gather(out_proj, ("dp", "tensor"), axis=0, tiled=True)
    attended, logs, mixed, norm_two, hidden_two = [], [], [], [], []
    for m in range(micros):
        out, log = attend(infos[m], m, qkv, all_kv, rows)
        attended.append(out)
        logs.append(log)
        mixed.append(inputs[m * rows : (m + 1) * rows] + dot(out, wout))
        normed, factor, low = normalize(mixed[m], gain_two)
        norm_two.append((normed, factor))
        hidden_two.append(low)
        if m == 0:
            low, all_kv = lax.optimization_barrier((low, all_kv))
            whole = lax.all_gather(low, "tensor", axis=0, tiled=True)
    units = down_proj.shape[0]
    prior, grad_two, out_sums = None, [], []
    for m in range(1, micros):
        low, whole, *hidden_two = lax.optimization_barrier((low_rows[m], whole, *hidden_two))
        cots.append(lax.all_gather(low, "tensor", axis=0, tiled=True))
    for m in range(micros):
        own = hidden_two[m + 1] if m + 1 < micros else None
        done = mlp(cots[m], whole, gate_proj.T, up_proj.T, down_proj, own, prior, rows, 7 + m)
        whole, prior = done.get("whole"), done["sums"]
        grad_two.append(done["grad"])
        if m + 1 < micros:
            out_sums.append(lax.psum_scatter(done["out"], "tensor", scatter_dimension=0, tiled=True))
    if square:
        shard, *out_sums = lax.optimization_barrier((done["shard"], *out_sums))
        weight_grads = lax.all_gather(shard, "dp", axis=0)
    else:
        weight_grads = lax.psum(prior, "dp").reshape(4, 3 * units, depth // 4)
    grad_mixed, gain_two_grads = [], []
    for m in range(micros):
        normed, factor = norm_two[m]
        grad, gain_grad = norm_back(grad_two[m], normed, factor, gain_two)
        gain_two_grads.append(gain_grad)
        grad_mixed.append(grad + grad_rows[m])

    grad_low = jnp.concatenate(grad_mixed, axis=0).astype(B16)
    acc_out = t_dot(jnp.concatenate(attended, axis=0), grad_low).astype(B16)
    grad_attended = dot_t(grad_low, wout).astype(B16)
    grad_q, grad_kv = attend_back(
        lengths[:, 0], qkv, all_kv, grad_attended, jnp.concatenate(logs, axis=0), cosine, sine, rows, 3
    )
    grad_kv = grad_kv.reshape(micros * rows, 2 * KW)
    grad_hidden = dot_t(grad_q, packed[:, :QW]) + dot_t(grad_kv, packed[:, QW:QKV])
    grad_in, gain_one_grad = norm_back(grad_hidden, normed_one, factor_one, gain_one)
    grad_bias = jnp.concatenate(
        [jnp.sum(grad_q.astype(F32), axis=0), jnp.sum(grad_kv.astype(F32), axis=0)]
    )
    acc_q = t_dot(hidden, grad_q).astype(B16)
    acc_kv = t_dot(hidden, grad_kv).astype(B16)
    tails = jnp.concatenate(
        [
            grad_bias[QW : QW + KW].reshape(devices, small),
            grad_bias[QW + KW :].reshape(devices, small),
            jnp.zeros((devices, size - 2 * small), F32),
        ],
        axis=1,
    ).reshape(-1)
    columns = jnp.stack([gain_one_grad, grad_bias[:QW], sum(gain_two_grads), tails], axis=1)
    columns = jnp.pad(columns.astype(B16), ((0, 0), (0, EXTRA - 4)))
    acc_rest = jnp.concatenate([acc_kv, columns], axis=1)
    out_part, weight_grads, acc_out, acc_q, acc_rest = lax.optimization_barrier(
        (done["out"], weight_grads, acc_out, acc_q, acc_rest)
    )
    out_sums.append(lax.psum_scatter(out_part, "tensor", scatter_dimension=0, tiled=True))
    summed = scatter_weights([acc_out, acc_q, acc_rest], 2)
    out_sums, weight_grads, summed = lax.optimization_barrier((out_sums, weight_grads, summed))
    gate_total, up_total, down_total = widen(weight_grads, units)
    grad_out, grad_query, grad_rest = summed
    layer_output = jnp.stack(
        [(mixed[m] + out_sums[m].astype(F32)).astype(B16) for m in range(micros)]
    )[:, None]
    grad_input = (grad_in + jnp.concatenate(grad_mixed, axis=0)).reshape(micros, 1, rows, depth)
    return (
        layer_output,
        grad_input,
        grad_rest[:, 2 * KW],
        grad_query,
        grad_rest[:, 2 * KW + 1],
        grad_rest[:, :KW],
        grad_rest[:small, 2 * KW + 3],
        grad_rest[:, KW : 2 * KW],
        grad_rest[small : 2 * small, 2 * KW + 3],
        grad_out,
        grad_rest[:, 2 * KW + 2],
        gate_total.T,
        up_total.T,
        down_total,
    )


def solution(mesh):
    rows = P(None, "dp", "tensor", None)
    both = P(("dp", "tensor"))
    wide = P(("dp", "tensor"), None)
    placed = (
        rows,
        P(None, "dp"),
        both,
        wide,
        both,
        wide,
        both,
        wide,
        both,
        wide,
        both,
        P(None, "tensor"),
        P(None, "tensor"),
        P("tensor", None),
        rows,
    )
    return jax.shard_map(
        on_device,
        mesh=mesh,
        in_specs=placed,
        out_specs=(
            rows,
            rows,
            both,
            wide,
            both,
            wide,
            both,
            wide,
            both,
            wide,
            both,
            P(None, "tensor"),
            P(None, "tensor"),
            P("tensor", None),
        ),
        check_vma=False,
    )
```

```python
import functools

import jax
import jax.numpy as jnp
from jax import lax
from jax.experimental import pallas as pl
from jax.experimental.pallas import tpu as pltpu
from jax.sharding import PartitionSpec as P

H = 12
KV = 2
HD = 128
GROUPS = H // KV
QW = H * HD
KW = KV * HD
QKV = QW + 2 * KW
EXTRA = 128

ROPE_BASE = 1000000.0
EPS = 1e-06
MASKED = -1e30
LOG2E = 1.4426950408889634
HEADS = 3
F32 = jnp.float32
B16 = jnp.bfloat16
VMEM_LIMIT = 56 * 1024 * 1024
VMEM_MOST = 60 * 1024 * 1024
CHUNK = 256
SCATTER_LANES = 1024
MESH = pl.DeviceIdType.MESH


def dot(a, b):
    return jnp.dot(a, b, preferred_element_type=F32)


def dot_t(a, b):
    return lax.dot_general(a, b, (((1,), (1,)), ((), ())), preferred_element_type=F32)


def t_dot(a, b):
    return lax.dot_general(a, b, (((0,), (0,)), ((), ())), preferred_element_type=F32)


def rope_tables(positions):
    half = HD // 2
    freqs = ROPE_BASE ** (-(jnp.arange(half, dtype=F32) * 2.0 / HD))
    angles = positions.astype(F32)[:, None] * freqs[None, :]
    cosine = jnp.cos(angles)
    sine = jnp.sin(angles)
    return (
        jnp.concatenate([cosine, cosine], axis=1),
        jnp.concatenate([-sine, sine], axis=1),
    )


def swap(value, axis, bit):
    count = lax.axis_size(axis)
    return lax.ppermute(value, axis, [(i, i ^ bit) for i in range(count)])


def nearest(chips, place, step):
    found = 0
    for here in range(chips):
        for at, there in enumerate(sorted(range(chips), key=lambda there: abs(there - here))):
            found = found + jnp.where((place == here) & (step == at), there, 0)
    return found


class Spot:
    def __init__(self):
        self.chips = lax.axis_size("tensor") // 2
        dp, tensor = lax.axis_index("dp"), lax.axis_index("tensor")
        self.dp, self.tensor = dp, tensor
        self.row, self.col = dp // 2, dp % 2
        self.chip, self.core = tensor // 2, tensor % 2
        self.over_x = (self.row * 2 + 1 - self.col, tensor)
        self.over_y = ((1 - self.row) * 2 + self.col, tensor)
        self.beside = (dp, self.chip * 2 + 1 - self.core)
        self.left = (dp, jnp.maximum(tensor - 2, 0))
        self.right = (dp, jnp.minimum(tensor + 2, 2 * self.chips - 1))

    def on_line(self, chip):
        return (self.dp, chip * 2 + self.core)

    def index(self, row, col, chip, core):
        return ((row * 2 + col) * self.chips + chip) * 2 + core


def greet(spot, plane, line):
    barrier = pltpu.get_barrier_semaphore()
    peers = [spot.beside] + ([spot.over_x, spot.over_y] if plane else [])
    for peer in peers:
        pl.semaphore_signal(barrier, inc=1, device_id=peer, device_id_type=MESH)
    count = len(peers)
    if line == "all":
        for chip in range(spot.chips):

            @pl.when(spot.chip != chip)
            def _():
                pl.semaphore_signal(barrier, inc=1, device_id=spot.on_line(chip), device_id_type=MESH)

        count = count + spot.chips - 1
    elif line == "near":
        has_left, has_right = spot.chip > 0, spot.chip < spot.chips - 1

        @pl.when(has_left)
        def _():
            pl.semaphore_signal(barrier, inc=1, device_id=spot.left, device_id_type=MESH)

        @pl.when(has_right)
        def _():
            pl.semaphore_signal(barrier, inc=1, device_id=spot.right, device_id_type=MESH)

        count = count + jnp.where(has_left, 1, 0) + jnp.where(has_right, 1, 0)
    pl.semaphore_wait(barrier, count)


def remote(src, dst, send_sem, recv_sem, device):
    return pltpu.make_async_remote_copy(
        src_ref=src,
        dst_ref=dst,
        send_sem=send_sem,
        recv_sem=recv_sem,
        device_id=device,
        device_id_type=MESH,
    )


class Line:
    def __init__(self, spot, block_ref, line_ref, local_sem, send_sem, recv_sem):
        self.spot, self.line = spot, line_ref
        self.send_sem, self.recv_sem = send_sem, recv_sem
        self.local = pltpu.make_async_copy(block_ref, line_ref.at[spot.chip], local_sem)

    def copy(self, there, way):
        here = self.line.at[there]
        peer = (self.spot.left, self.spot.right)[way]
        return remote(here, here, self.send_sem.at[way, there], self.recv_sem.at[there], peer)

    def ways(self, there):
        chip, chips = self.spot.chip, self.spot.chips
        return ((chip > 0) & (there >= chip), (chip < chips - 1) & (there <= chip))

    def send(self, there):
        for way, when in enumerate(self.ways(there)):
            pl.when(when)(self.copy(there, way).start)

    def start(self):
        self.local.wait()
        self.send(self.spot.chip)

    def forward(self, step):
        for there in (self.spot.chip - step, self.spot.chip + step):

            @pl.when((there >= 0) & (there < self.spot.chips))
            def _():
                here = self.line.at[there]
                remote(here, here, self.send_sem.at[0, there], self.recv_sem.at[there], self.spot.beside).wait_recv()
                self.send(there)

    def end(self):
        for there in range(self.spot.chips):
            for way, when in enumerate(self.ways(there)):
                pl.when(when)(self.copy(there, way).wait_send)


def line_kernel(block_ref, line_ref, local_sem, send_sem, recv_sem):
    spot = Spot()
    line = Line(spot, block_ref, line_ref, local_sem, send_sem, recv_sem)
    line.local.start()
    greet(spot, False, "near")
    line.start()
    for step in range(1, spot.chips):
        line.forward(step)
    line.end()


def plane_kernel(more, line_ref, *refs):
    spot = Spot()
    if more:
        block_ref, whole_ref, next_ref, local_sem, send_sem, recv_sem, *sems = refs
        line = Line(spot, block_ref, next_ref, *sems)
        line.local.start()
    else:
        whole_ref, local_sem, send_sem, recv_sem = refs
    chips, chip, core, row, col = spot.chips, spot.chip, spot.core, spot.row, spot.col
    cut = chips // 2

    def local(there):
        return pltpu.make_async_copy(
            line_ref.at[there], whole_ref.at[spot.index(row, col, there, core)], local_sem.at[there]
        )

    for there in range(chips):
        local(there).start()
    greet(spot, True, "near" if more else None)
    if more:
        line.start()
    sent = []

    def send(index, device, source=None):
        source = whole_ref.at[index] if source is None else source
        copy = remote(source, whole_ref.at[index], send_sem.at[len(sent)], recv_sem.at[index], device)
        sent.append(copy)
        copy.start()

    def arrive(index):
        remote(
            whole_ref.at[index], whole_ref.at[index], send_sem.at[0], recv_sem.at[index], spot.beside
        ).wait_recv()

    for there in range(chips):
        index = spot.index(row, col, there, core)
        for peer in (spot.over_x, spot.over_y, spot.beside):
            send(index, peer, line_ref.at[there])
    for there in range(chips):
        across_x = spot.index(row, 1 - col, there, core)
        arrive(across_x)
        if there < cut:
            send(across_x, spot.over_y)
        send(across_x, spot.beside)
        across_y = spot.index(1 - row, col, there, core)
        arrive(across_y)
        if there >= cut:
            send(across_y, spot.over_x)
        send(across_y, spot.beside)
        if more and 0 < there:
            line.forward(there)
    for there in range(chips):
        index = spot.index(1 - row, 1 - col, there, core)
        arrive(index)
        send(index, spot.beside)
    for plane in range(4):
        for there in range(chips):
            arrive(spot.index(plane // 2, plane % 2, there, 1 - core))
    for there in range(chips):
        local(there).wait()
    for copy in sent:
        copy.wait_send()
    if more:
        line.end()


def gather_line(block, collective_id):
    chips = lax.axis_size("tensor") // 2
    dma = pltpu.SemaphoreType.DMA
    return pl.pallas_call(
        line_kernel,
        in_specs=[pl.BlockSpec(memory_space=pl.ANY)],
        out_specs=pl.BlockSpec(memory_space=pl.ANY),
        out_shape=jax.ShapeDtypeStruct((chips,) + block.shape, B16),
        scratch_shapes=[dma, dma((2, chips)), dma((chips,))],
        compiler_params=pltpu.CompilerParams(
            collective_id=collective_id, has_side_effects=True, vmem_limit_bytes=VMEM_LIMIT
        ),
        cost_estimate=pl.CostEstimate(flops=0, bytes_accessed=block.size * 100, transcendentals=0),
    )(block)


def gather_plane(line, collective_id, more=None):
    chips, size, width = line.shape
    dma = pltpu.SemaphoreType.DMA
    anywhere = pl.BlockSpec(memory_space=pl.ANY)
    shapes = [jax.ShapeDtypeStruct((8 * chips, size, width), B16)]
    sems = [dma((chips,)), dma((10 * chips,)), dma((8 * chips,))]
    if more is not None:
        shapes.append(jax.ShapeDtypeStruct((chips,) + more.shape, B16))
        sems += [dma, dma((2, chips)), dma((chips,))]
    out = pl.pallas_call(
        functools.partial(plane_kernel, more is not None),
        in_specs=[anywhere] * len(shapes),
        out_specs=[anywhere] * len(shapes),
        out_shape=shapes,
        scratch_shapes=sems,
        compiler_params=pltpu.CompilerParams(
            collective_id=collective_id, has_side_effects=True, vmem_limit_bytes=VMEM_LIMIT
        ),
        cost_estimate=pl.CostEstimate(flops=0, bytes_accessed=line.size * 60, transcendentals=0),
    )(line, *([] if more is None else [more]))
    return (out[0].reshape(8 * chips * size, width), *out[1:])


def scatter_kernel(parts, arrays, *refs):
    grads, outs = refs[:arrays], refs[arrays : 2 * arrays]
    mine, got, over_x, over_y, across_x, across_y, line, load_sem, send_sem, recv_sem = refs[2 * arrays :]
    spot = Spot()
    chips, chip, core, row, col = spot.chips, spot.chip, spot.core, spot.row, spot.col
    cut = chips // 2

    def at(r, c, z):
        return (r * 2 + c) * chips + z

    def lanes(p):
        return pl.ds(parts[p][0], parts[p][1])

    def source(p, which):
        _, width, array, start = parts[p]
        return grads[array].at[:, which, :, pl.ds(start, width)]

    def load(p):
        return pltpu.make_async_copy(source(p, core), mine.at[:, :, lanes(p)], load_sem.at[p])

    def swapped(p):
        return remote(
            source(p, 1 - core), got.at[:, :, lanes(p)], send_sem.at[p, 0], recv_sem.at[p, 0], spot.beside
        )

    def first(p):
        cols = lanes(p)
        copies = []
        for side in range(2):
            copies.append(
                remote(
                    mine.at[pl.ds(at(side, 1 - col, 0), cut), :, cols],
                    over_x.at[pl.ds(side * cut, cut), :, cols],
                    send_sem.at[p, 1 + side],
                    recv_sem.at[p, 1 + side],
                    spot.over_x,
                )
            )
            copies.append(
                remote(
                    mine.at[pl.ds(at(1 - row, side, cut), chips - cut), :, cols],
                    over_y.at[pl.ds(side * (chips - cut), chips - cut), :, cols],
                    send_sem.at[p, 3 + side],
                    recv_sem.at[p, 3 + side],
                    spot.over_y,
                )
            )
        return copies

    def second(p):
        cols = lanes(p)
        return [
            remote(
                mine.at[pl.ds(at(1 - row, col, 0), cut), :, cols],
                across_y.at[:, :, cols],
                send_sem.at[p, 5],
                recv_sem.at[p, 5],
                spot.over_y,
            ),
            remote(
                mine.at[pl.ds(at(row, 1 - col, cut), chips - cut), :, cols],
                across_x.at[:, :, cols],
                send_sem.at[p, 6],
                recv_sem.at[p, 6],
                spot.over_x,
            ),
        ]

    def third(p, other):
        cols = lanes(p)
        return remote(
            mine.at[at(row, col, other), :, cols],
            line.at[chip, :, cols],
            send_sem.at[p, 7 + other],
            recv_sem.at[p, 7 + chip],
            spot.on_line(other),
        )

    def add(p, target, start, source, begin, count):
        cols = lanes(p)

        def body(step, _):
            target[start + step, :, cols] = (
                target[start + step, :, cols].astype(F32) + source[begin + step, :, cols].astype(F32)
            ).astype(B16)
            return 0

        lax.fori_loop(0, count, body, 0)

    def stage_one(p):
        load(p).wait()
        swapped(p).wait()
        add(p, mine, 0, got, 0, 4 * chips)
        for copy in first(p):
            copy.start()

    def stage_two(p):
        for copy in first(p):
            copy.wait()
        for side in range(2):
            add(p, mine, at(side, col, 0), over_x, side * cut, cut)
            add(p, mine, at(row, side, cut), over_y, side * (chips - cut), chips - cut)
        for copy in second(p):
            copy.start()

    def stage_three(p):
        for copy in second(p):
            copy.wait()
        add(p, mine, at(row, col, 0), across_y, 0, cut)
        add(p, mine, at(row, col, cut), across_x, 0, chips - cut)
        for other in range(chips):
            pl.when(chip != other)(third(p, other).start)

    def stage_four(p):
        cols = lanes(p)
        total = mine[at(row, col, chip), :, cols].astype(F32)
        for other in range(chips):

            @pl.when(chip != other)
            def _():
                here = line.at[other, :, cols]
                remote(here, here, send_sem.at[p, 7 + other], recv_sem.at[p, 7 + other], spot.beside).wait_recv()

            total = total + line[other, :, cols].astype(F32)
        _, width, array, start = parts[p]
        outs[array][:, start : start + width] = total
        for other in range(chips):
            pl.when(chip != other)(third(p, other).wait_send)

    for p in range(len(parts)):
        load(p).start()
    line[chip] = jnp.zeros(line.shape[1:], B16)
    greet(spot, True, "all")
    for p in range(len(parts)):
        swapped(p).start()
    stages = (stage_one, stage_two, stage_three, stage_four)
    for step in range(len(parts) + len(stages) - 1):
        for late, stage in enumerate(stages):
            if 0 <= step - late < len(parts):
                stage(step - late)


def scatter_weights(grads, collective_id):
    total = grads[0].shape[0]
    devices = lax.axis_size(("dp", "tensor"))
    size = total // devices
    if lax.axis_size("dp") != 4:
        return [
            lax.psum_scatter(array, ("dp", "tensor"), scatter_dimension=0, tiled=True).astype(F32)
            for array in grads
        ]
    chips = lax.axis_size("tensor") // 2
    cut = chips // 2
    parts, width = [], 0
    for at, array in enumerate(grads):
        count = pl.cdiv(array.shape[1], SCATTER_LANES)
        tiles = array.shape[1] // 128
        ends = [tiles * p // count * 128 for p in range(count + 1)]
        for start, end in zip(ends, ends[1:]):
            parts.append((width + start, end - start, at, start))
        width += array.shape[1]
    dma = pltpu.SemaphoreType.DMA
    return pl.pallas_call(
        functools.partial(scatter_kernel, parts, len(grads)),
        in_specs=[pl.BlockSpec(memory_space=pl.ANY)] * len(grads),
        out_specs=[pl.BlockSpec(memory_space=pltpu.VMEM)] * len(grads),
        out_shape=[jax.ShapeDtypeStruct((size, array.shape[1]), F32) for array in grads],
        scratch_shapes=[
            pltpu.VMEM((4 * chips, size, width), B16),
            pltpu.VMEM((4 * chips, size, width), B16),
            pltpu.VMEM((2 * cut, size, width), B16),
            pltpu.VMEM((2 * (chips - cut), size, width), B16),
            pltpu.VMEM((chips - cut, size, width), B16),
            pltpu.VMEM((cut, size, width), B16),
            pltpu.VMEM((chips, size, width), B16),
            dma((len(parts),)),
            dma((len(parts), 7 + chips)),
            dma((len(parts), 7 + chips)),
        ],
        compiler_params=pltpu.CompilerParams(
            collective_id=collective_id, has_side_effects=True, vmem_limit_bytes=VMEM_LIMIT
        ),
        cost_estimate=pl.CostEstimate(flops=0, bytes_accessed=devices * size * width * 8, transcendentals=0),
    )(*[array.reshape(devices // 2, 2, size, array.shape[1]) for array in grads])


class Named:
    def __init__(self, names, refs):
        for name, ref in zip(names, refs, strict=True):
            setattr(self, name, ref)


def project_kernel(hidden_ref, weight_ref, bias_ref, cos_ref, sin_ref, out_ref):
    chunk = pl.program_id(0)
    turned = chunk < (QW + KW) // 256
    lin = dot(hidden_ref[...], weight_ref[...]) + bias_ref[...]
    for head in range(2):
        cut = pl.ds(head * HD, HD)
        one = lin[:, head * HD : (head + 1) * HD]
        rot = one * cos_ref[...] + pltpu.roll(one, HD // 2, 1) * sin_ref[...]
        out_ref[:, cut] = jnp.where(turned, rot, one).astype(B16)


def project(hidden, weights, bias, cosine, sine):
    rows, depth = hidden.shape
    return pl.pallas_call(
        project_kernel,
        grid=(QKV // 256,),
        in_specs=[
            pl.BlockSpec((rows, depth), lambda j: (0, 0)),
            pl.BlockSpec((depth, 256), lambda j: (0, j)),
            pl.BlockSpec((1, 256), lambda j: (0, j)),
            pl.BlockSpec((rows, HD), lambda j: (0, 0)),
            pl.BlockSpec((rows, HD), lambda j: (0, 0)),
        ],
        out_specs=pl.BlockSpec((rows, 256), lambda j: (0, j)),
        out_shape=jax.ShapeDtypeStruct((rows, QKV), B16),
        compiler_params=pltpu.CompilerParams(vmem_limit_bytes=VMEM_LIMIT),
        cost_estimate=pl.CostEstimate(
            flops=2 * rows * depth * QKV,
            bytes_accessed=2 * (depth * QKV + rows * depth + rows * QKV),
            transcendentals=0,
        ),
    )(hidden, weights, bias, cosine, sine)


def fill_bias(info_ref, bias):
    shape = bias.shape
    place = info_ref[1] + lax.broadcasted_iota(jnp.int32, shape, 0)
    keys = lax.broadcasted_iota(jnp.int32, shape, 1)
    bias[...] = jnp.where((keys <= place) & (keys < info_ref[0]), 0.0, MASKED)


def flat(ref):
    return ref[...].reshape(ref.shape[0] * ref.shape[2], ref.shape[3])


def attend_kernel(info_ref, q_ref, k_ref, v_ref, out_ref, log_ref, bias):
    @pl.when(pl.program_id(0) == 0)
    def _():
        fill_bias(info_ref, bias)

    keys, values = flat(k_ref), flat(v_ref)
    for head in range(HEADS):
        cut = slice(head * HD, (head + 1) * HD)
        scores = dot_t(q_ref[:, cut], keys) * (HD**-0.5 * LOG2E) + bias[...]
        top = jnp.max(scores, axis=-1, keepdims=True)
        expd = jnp.exp2(scores - top)
        summed = jnp.sum(expd, axis=-1, keepdims=True)
        out_ref[:, cut] = (dot(expd.astype(B16), values) * (1.0 / summed)).astype(B16)
        log_ref[:, cut] = jnp.broadcast_to(top + jnp.log2(summed), (q_ref.shape[0], HD))


def attend(info, micro, qkv, keys_values, rows):
    parts = keys_values.shape[0]
    total = parts * rows
    return pl.pallas_call(
        attend_kernel,
        grid_spec=pltpu.PrefetchScalarGridSpec(
            num_scalar_prefetch=1,
            grid=(H // HEADS,),
            in_specs=[
                pl.BlockSpec((rows, HEADS * HD), lambda h, info: (micro, h)),
                pl.BlockSpec((parts, 1, rows, HD), lambda h, info: (0, micro, 0, h * HEADS // GROUPS)),
                pl.BlockSpec((parts, 1, rows, HD), lambda h, info: (0, micro, 0, KV + h * HEADS // GROUPS)),
            ],
            out_specs=[
                pl.BlockSpec((rows, HEADS * HD), lambda h, info: (0, h)),
                pl.BlockSpec((rows, HEADS * HD), lambda h, info: (0, h)),
            ],
            scratch_shapes=[pltpu.VMEM((rows, total), F32)],
        ),
        out_shape=[
            jax.ShapeDtypeStruct((rows, QW), B16),
            jax.ShapeDtypeStruct((rows, QW), F32),
        ],
        compiler_params=pltpu.CompilerParams(vmem_limit_bytes=VMEM_LIMIT),
        cost_estimate=pl.CostEstimate(
            flops=8 * rows * total * QW,
            bytes_accessed=4 * total * KW + 8 * rows * QW,
            transcendentals=H * rows * total,
        ),
    )(info, qkv, keys_values, keys_values)


def attend_back_kernel(names, parts, *refs):
    r = Named(names, refs)
    spot = Spot()
    chips, chip, core = spot.chips, spot.chip, spot.core
    rows = r.q.shape[0]
    step = pl.program_id(0)
    micros = r.sums.shape[0]
    turns = H // HEADS
    micro, turn = step // turns, lax.rem(step, turns)
    span = GROUPS // HEADS
    pieces = micros * KV
    scale = HD**-0.5

    def rows_of(block, which):
        return pl.ds(pl.multiple_of((2 * block + which) * rows, rows), rows)

    def swapped(piece):
        mine = r.part.at[piece, :, 1 - core]
        return remote(mine, r.xrecv.at[piece], r.xsend.at[piece], r.xrecv_sem.at[piece], spot.beside)

    def along(piece, block):
        return remote(
            r.part.at[piece, block, core],
            r.zrecv.at[piece, chip],
            r.zsend.at[piece, block],
            r.zrecv_sem.at[piece, chip],
            spot.on_line(block),
        )

    def spread(piece):
        swapped(piece).wait_recv()
        for block in range(chips):
            total = r.part[piece, block, core].astype(F32) + r.xrecv[piece, block].astype(F32)
            r.part[piece, block, core] = total.astype(B16)
            pl.when(chip != block)(along(piece, block).start)

    @pl.when(step == 0)
    def _():
        greet(spot, False, "all")

    @pl.when(turn == 0)
    def _():
        shape = r.bias.shape
        place = spot.tensor * rows + lax.broadcasted_iota(jnp.int32, shape, 0)
        keys_at = lax.broadcasted_iota(jnp.int32, shape, 1)
        r.bias[...] = jnp.where((keys_at <= place) & (keys_at < r.length[micro]), 0.0, MASKED)

    keys, values = flat(r.k), flat(r.v)
    grad_k = grad_v = 0.0
    for head in range(HEADS):
        cut = slice(head * HD, (head + 1) * HD)
        queries, grads = r.q[:, cut], r.g[:, cut]
        scores = dot_t(queries, keys) * (scale * LOG2E) + r.bias[...]
        probs = jnp.exp2(scores - r.log[:, head * HD : head * HD + 1])
        grad_probs = dot_t(grads, values)
        inner = jnp.sum(grad_probs * probs, axis=-1, keepdims=True)
        grad_scores = (probs * (grad_probs - inner)).astype(B16)
        grad_q = dot(grad_scores, keys) * scale
        turned = grad_q * r.cos[...] - pltpu.roll(grad_q, HD // 2, 1) * r.sin[...]
        r.dq[:, cut] = turned.astype(B16)
        grad_k = grad_k + t_dot(grad_scores, queries)
        grad_v = grad_v + t_dot(probs.astype(B16), grads)
    first = lax.rem(turn, span) == 0

    @pl.when(first)
    def _():
        r.dk_acc[...] = grad_k
        r.dv_acc[...] = grad_v

    @pl.when(jnp.logical_not(first))
    def _():
        r.dk_acc[...] += grad_k
        r.dv_acc[...] += grad_v

    for piece in range(pieces):

        @pl.when(step == (piece + 1) * span - 1)
        def _():
            shape = (chips, 2, rows, HD)
            r.part[piece, :, :, :, :HD] = (r.dk_acc[...] * scale).reshape(shape).astype(B16)
            r.part[piece, :, :, :, HD:] = r.dv_acc[...].reshape(shape).astype(B16)
            swapped(piece).start()

        if piece + 1 < pieces:

            @pl.when(step == (piece + 1) * span)
            def _():
                spread(piece)

    @pl.when(step == pieces * span - 1)
    def _():
        spread(pieces - 1)
        for piece in range(pieces):
            total = r.part[piece, chip, core].astype(F32)
            for other in range(chips):

                @pl.when(chip != other)
                def _():
                    here = r.zrecv.at[piece, other]
                    remote(
                        here, here, r.zsend.at[piece, other], r.zrecv_sem.at[piece, other], spot.beside
                    ).wait_recv()

                got = jnp.where(chip != other, r.zrecv[piece, other], jnp.zeros((rows, 2 * HD), B16))
                total = total + got.astype(F32)
            at, group = piece // KV, piece % KV
            grad = total[:, :HD]
            grad = grad * r.cos[...] - pltpu.roll(grad, HD // 2, 1) * r.sin[...]
            r.sums[at, :, group * HD : (group + 1) * HD] = grad.astype(B16)
            r.sums[at, :, KW + group * HD : KW + (group + 1) * HD] = total[:, HD:].astype(B16)
        for piece in range(pieces):
            swapped(piece).wait_send()
            for block in range(chips):
                pl.when(chip != block)(along(piece, block).wait_send)


def attend_back(lengths, qkv, keys_values, grads, logs, cosine, sine, rows, collective_id):
    parts, micros = keys_values.shape[:2]
    chips = parts // 2
    total = parts * rows
    pieces = micros * KV
    turns = H // HEADS
    dma = pltpu.SemaphoreType.DMA
    vmem = pltpu.VMEM

    def heads(step):
        return (step // turns, step % turns)

    inputs = {
        "length": (pl.BlockSpec(memory_space=pltpu.SMEM), lengths),
        "q": (pl.BlockSpec((rows, HEADS * HD), heads), qkv),
        "k": (
            pl.BlockSpec((parts, 1, rows, HD), lambda s: (0, s // turns, 0, s % turns * HEADS // GROUPS)),
            keys_values,
        ),
        "v": (
            pl.BlockSpec((parts, 1, rows, HD), lambda s: (0, s // turns, 0, KV + s % turns * HEADS // GROUPS)),
            keys_values,
        ),
        "g": (pl.BlockSpec((rows, HEADS * HD), heads), grads),
        "log": (pl.BlockSpec((rows, HEADS * HD), heads), logs),
        "cos": (pl.BlockSpec((rows, HD), lambda s: (0, 0)), cosine),
        "sin": (pl.BlockSpec((rows, HD), lambda s: (0, 0)), sine),
    }
    outputs = {
        "dq": (pl.BlockSpec((rows, HEADS * HD), heads), jax.ShapeDtypeStruct((micros * rows, QW), B16)),
        "sums": (
            pl.BlockSpec((micros, rows, 2 * KW), lambda s: (0, 0, 0)),
            jax.ShapeDtypeStruct((micros, rows, 2 * KW), B16),
        ),
    }
    scratch = {
        "bias": vmem((rows, total), F32),
        "dk_acc": vmem((total, HD), F32),
        "dv_acc": vmem((total, HD), F32),
        "part": vmem((pieces, chips, 2, rows, 2 * HD), B16),
        "xrecv": vmem((pieces, chips, rows, 2 * HD), B16),
        "zrecv": vmem((pieces, chips, rows, 2 * HD), B16),
        "xsend": dma((pieces,)),
        "xrecv_sem": dma((pieces,)),
        "zsend": dma((pieces, chips)),
        "zrecv_sem": dma((pieces, chips)),
    }
    return pl.pallas_call(
        functools.partial(attend_back_kernel, [*inputs, *outputs, *scratch], parts),
        grid=(micros * turns,),
        in_specs=[spec for spec, _ in inputs.values()],
        out_specs=[spec for spec, _ in outputs.values()],
        out_shape=[shape for _, shape in outputs.values()],
        scratch_shapes=list(scratch.values()),
        compiler_params=pltpu.CompilerParams(
            collective_id=collective_id, has_side_effects=True, vmem_limit_bytes=VMEM_LIMIT
        ),
        cost_estimate=pl.CostEstimate(
            flops=20 * micros * rows * total * QW,
            bytes_accessed=micros * (8 * total * KW + 12 * rows * QW),
            transcendentals=micros * H * rows * total,
        ),
    )(*[value for _, value in inputs.values()])


def mlp_kernel(names, reduced, *refs):
    r = Named(names, refs)
    has_next, has_prior = "own" in names, "prior" in names
    spot = Spot()
    chips, chip, core, row, col = spot.chips, spot.chip, spot.core, spot.row, spot.col
    units, depth = r.wg.shape
    rows = r.grad.shape[0]
    pair = 2 * rows
    quarter = depth // 4
    chunks = [(i * CHUNK, min(CHUNK, units - i * CHUNK)) for i in range(pl.cdiv(units, CHUNK))]
    whole_chunks, rest = units // CHUNK, units % CHUNK
    wide = depth // 2

    def block_at(step):
        return nearest(chips, chip, chips - 1 - step)

    def span(block):
        return pl.ds(pl.multiple_of(block * pair, pair), pair)

    def rows_of(block, which):
        return pl.ds(pl.multiple_of(block * pair + which * rows, rows), rows)

    def columns(index, width=CHUNK):
        return pl.ds(pl.multiple_of(index * width, width), width)

    def weight_load(index):
        cut = pl.ds(*chunks[index])
        return [
            pltpu.make_async_copy(src.at[cut], dst.at[cut], r.weight_sem.at[i, index])
            for i, (src, dst) in enumerate(((r.wg_hbm, r.wg), (r.wu_hbm, r.wu), (r.wd_hbm, r.wd)))
        ]

    def weights_here(index, width=CHUNK):
        for i, dst in enumerate((r.wg, r.wu, r.wd)):
            cut = dst.at[pl.ds(index * CHUNK, width)]
            pltpu.make_async_copy(cut, cut, r.weight_sem.at[i, index]).wait()

    def h_load(block):
        return pltpu.make_async_copy(r.h_hbm.at[span(block)], r.h.at[span(block)], r.load_sem.at[0, block])

    def g_load(block):
        return pltpu.make_async_copy(r.cot.at[span(block)], r.g.at[span(block)], r.load_sem.at[1, block])

    def gather_send(block, way):
        here = r.whole.at[rows_of(block, core)]
        peer = (spot.left, spot.right, spot.beside)[way]
        return remote(here, here, r.gather_send.at[way, block], r.gather_recv.at[block, core], peer)

    def gather_first(way):
        peer = (spot.left, spot.right, spot.beside)[way]
        here = r.whole.at[rows_of(chip, core)]
        return remote(r.own, here, r.gather_send.at[way, chip], r.gather_recv.at[chip, core], peer)

    def gathered(block, which):
        here = r.whole.at[rows_of(block, which)]
        remote(here, here, r.gather_send.at[2, block], r.gather_recv.at[block, which], spot.beside).wait_recv()

    def own_copy():
        return pltpu.make_async_copy(r.own, r.whole.at[rows_of(chip, core)], r.local_sem)

    def gather_start():
        own_copy().start()
        pl.when(chip > 0)(gather_first(0).start)
        pl.when(chip < chips - 1)(gather_first(1).start)
        gather_first(2).start()

    def gather_forward(step):
        block = chip - step

        @pl.when(block >= 0)
        def _():
            gathered(block, core)
            pl.when(chip < chips - 1)(gather_send(block, 1).start)
            gather_send(block, 2).start()

        after = chip + step

        @pl.when(after < chips)
        def _():
            gathered(after, core)
            pl.when(chip > 0)(gather_send(after, 0).start)
            gather_send(after, 2).start()

    def gather_end():
        own_copy().wait()
        for block in range(chips):
            gathered(block, 1 - core)
        for block in range(chips):
            away = block != chip
            pl.when((chip > 0) & (block >= chip) & away)(gather_send(block, 0).wait_send)
            pl.when((chip < chips - 1) & (block <= chip) & away)(gather_send(block, 1).wait_send)
            pl.when(away)(gather_send(block, 2).wait_send)
        pl.when(chip > 0)(gather_first(0).wait_send)
        pl.when(chip < chips - 1)(gather_first(1).wait_send)
        gather_first(2).wait_send()

    def swapped(block):
        return remote(
            r.part.at[rows_of(block, 1 - core)],
            r.xrecv.at[block],
            r.xsend.at[block],
            r.xrecv_sem.at[block],
            spot.beside,
        )

    def along(block, ahead):
        slot = chips - 1 - block if ahead else chips - block
        return remote(
            r.part.at[rows_of(block, core)],
            r.zrecv.at[slot],
            r.zsend.at[block],
            r.zrecv_sem.at[slot],
            spot.right if ahead else spot.left,
        )

    def straight(block):
        return remote(
            r.part.at[rows_of(block, core)],
            r.zrecv.at[chip],
            r.zsend.at[block],
            r.zrecv_sem.at[chip],
            spot.on_line(block),
        )

    def straight_sum():
        for other in range(chips):

            @pl.when(chip != other)
            def _():
                here = r.zrecv.at[other]
                remote(here, here, r.zsend.at[other], r.zrecv_sem.at[other], spot.beside).wait_recv()
                r.grad[...] = r.grad[...] + r.zrecv[other].astype(F32)

    def finish(block):
        swapped(block).wait_recv()
        total = r.part[rows_of(block, core), :].astype(F32) + r.xrecv[block].astype(F32)

        @pl.when(block == chip)
        def _():
            r.grad[...] = total

        @pl.when(block != chip)
        def _():
            r.part[rows_of(block, core), :] = total.astype(B16)
            if has_next:
                pl.when(chip == 0)(along(block, True).start)
                pl.when(chip == chips - 1)(along(block, False).start)
            else:
                straight(block).start()

    def relay_one(block, ahead):
        slot = chips - 1 - block if ahead else chips - block
        remote(
            r.zrecv.at[slot], r.zrecv.at[slot], r.zsend.at[block], r.zrecv_sem.at[slot], spot.beside
        ).wait_recv()

        @pl.when(block == chip)
        def _():
            r.grad[...] = r.grad[...] + r.zrecv[slot].astype(F32)

        @pl.when(block != chip)
        def _():
            here = rows_of(block, core)
            r.part[here, :] = (r.part[here, :].astype(F32) + r.zrecv[slot].astype(F32)).astype(B16)
            along(block, ahead).start()

    def relay(point):
        step = point - (chip - 1)

        @pl.when((chip > 0) & (step >= 0) & (step < chips - chip))
        def _():
            relay_one(chips - 1 - step, True)

        back_step = point - (chips - 2 - chip)

        @pl.when((chip < chips - 1) & (back_step >= 0) & (back_step <= chip))
        def _():
            relay_one(back_step, False)

    def gate(here, start, width):
        cut = pl.ds(start, width)
        gate = dot_t(r.h[here, :], r.wg[cut, :])
        up = dot_t(r.h[here, :], r.wu[cut, :])
        grad = dot_t(r.g[here, :], r.wd[cut, :])
        sigma = jax.nn.sigmoid(gate)
        silu = gate * sigma
        r.act[here, cut] = (silu * up).astype(B16)
        r.dg[here, cut] = (grad * up * sigma * (1.0 + gate * (1.0 - sigma))).astype(B16)
        r.du[here, cut] = (grad * silu).astype(B16)

    def gates(step, block):
        here = span(block)

        def chunk(index, _):
            pl.when(step == 0)(functools.partial(weights_here, index))
            gate(here, pl.multiple_of(index * CHUNK, CHUNK), CHUNK)
            return 0

        lax.fori_loop(0, whole_chunks, chunk, 0)
        if rest:
            pl.when(step == 0)(functools.partial(weights_here, whole_chunks, rest))
            gate(here, whole_chunks * CHUNK, rest)

    def back(block):
        here = span(block)

        def chunk(index, _):
            cut = columns(index, wide)
            grad = dot(r.dg[here, :], r.wg[:, cut]) + dot(r.du[here, :], r.wu[:, cut])
            r.part[here, cut] = grad.astype(B16)
            return 0

        lax.fori_loop(0, depth // wide, chunk, 0)
        swapped(block).start()

    def put_out(block, index):
        cut = pl.ds(index * wide, wide)
        return pltpu.make_async_copy(
            r.stage_out.at[:, cut], r.out.at[span(block), cut], r.out_sem.at[index]
        )

    def out_block(block):
        for index in range(2):
            pl.when(block > 0)(put_out(block, index).wait)
            cut = slice(index * wide, (index + 1) * wide)
            r.stage_out[:, cut] = dot(r.act[span(block), :], r.wd[:, cut]).astype(B16)
            put_out(block, index).start()

    def place(matrix, start, width):
        return pl.ds(pl.multiple_of(matrix * units + start, 16), width)

    def exchanged(matrix, index, start, width, over_x):
        here = place(matrix, start, width)
        at = matrix * len(chunks) + index
        source = r.sums.at[:, 1 - col, here] if over_x else r.sums.at[1 - row, :, here]
        peer = spot.over_x if over_x else spot.over_y
        return remote(source, r.landing.at[:, here], r.one_send.at[at], r.one_recv.at[at], peer)

    def exchange_start(matrix, index, start, width):
        first = lax.rem(matrix + index, 2) == 0
        pl.when(first)(exchanged(matrix, index, start, width, True).start)
        pl.when(jnp.logical_not(first))(exchanged(matrix, index, start, width, False).start)

    def exchange_copies(matrix, index, slot):
        start, width = chunks[index]
        here = place(matrix, start, width)
        cut = pl.ds(0, width)
        own = r.sums.at[:, col, here] if (matrix + index) % 2 == 0 else r.sums.at[row, :, here]
        return [
            pltpu.make_async_copy(own, r.held_own.at[slot, :, cut], r.held_sem.at[slot, 0]),
            pltpu.make_async_copy(r.landing.at[:, here], r.held_got.at[slot, :, cut], r.held_sem.at[slot, 1]),
        ]

    def exchange_load(matrix, index, slot):
        exchanged(matrix, index, *chunks[index], (matrix + index) % 2 == 0).wait_recv()
        for copy in exchange_copies(matrix, index, slot):
            copy.start()

    def exchange(matrix, index, slot):
        start, width = chunks[index]
        for copy in exchange_copies(matrix, index, slot):
            copy.wait()
        mine = row if (matrix + index) % 2 == 0 else col
        r.shard[place(matrix, start, width), :] = (
            r.held_own[slot, mine, :width].astype(F32) + r.held_got[slot, mine, :width].astype(F32)
        ).astype(B16)
        r.rest[place(matrix, start, width), :] = (
            r.held_own[slot, 1 - mine, :width].astype(F32) + r.held_got[slot, 1 - mine, :width].astype(F32)
        ).astype(B16)
        passed(matrix, index).start()

    def passed(matrix, index):
        start, width = chunks[index]
        here = place(matrix, start, width)
        at = matrix * len(chunks) + index
        peer = spot.over_y if (matrix + index) % 2 == 0 else spot.over_x
        return remote(r.rest.at[here], r.got_rest.at[here], r.two_send.at[at], r.two_recv.at[at], peer)

    def weight_grads(matrix, left, right):
        def put(start, width, slot):
            return pltpu.make_async_copy(
                r.stage.at[slot, :, :, pl.ds(0, width)],
                r.sums.at[:, :, place(matrix, start, width)],
                r.stage_sem.at[slot],
            )

        def one(index, start, width, slot):
            if has_prior:
                fetch = pltpu.make_async_copy(
                    r.prior.at[:, :, place(matrix, start, width)],
                    r.before.at[:, :, pl.ds(0, width)],
                    r.before_sem,
                )
                fetch.start()
            value = t_dot(left[:, pl.ds(start, width)], right[...])
            if has_prior:
                fetch.wait()
            for at in range(4):
                piece = value[:, at * quarter : (at + 1) * quarter]
                if has_prior:
                    piece = piece + r.before[at // 2, at % 2, :width].astype(F32)
                r.stage[slot, at // 2, at % 2, :width] = piece.astype(B16)
            put(start, width, slot).start()

        def sent(index, start, width, slot):
            put(start, width, slot).wait()
            if reduced:
                exchange_start(matrix, index, start, width)

        def body(index, _):
            slot = lax.rem(index, 2)
            start = pl.multiple_of(index * CHUNK, CHUNK)
            one(index, start, CHUNK, slot)

            @pl.when(index > 0)
            def _():
                sent(index - 1, start - CHUNK, CHUNK, 1 - slot)

            return 0

        lax.fori_loop(0, whole_chunks, body, 0)
        index = whole_chunks
        if rest:
            one(index, index * CHUNK, rest, index % 2)
            if index:
                sent(index - 1, (index - 1) * CHUNK, CHUNK, (index - 1) % 2)
            sent(index, index * CHUNK, rest, index % 2)
        else:
            sent(index - 1, (index - 1) * CHUNK, CHUNK, (index - 1) % 2)

    for step in range(chips):
        h_load(block_at(step)).start()
        g_load(block_at(step)).start()
        if step == 0:
            for index in range(len(chunks)):
                for copy in weight_load(index):
                    copy.start()
    greet(spot, reduced, "near" if has_next else "all")
    if has_next:
        gather_start()

    def loaded(block):
        h_load(block).wait()
        g_load(block).wait()

    todo = []
    if reduced:
        todo = [(matrix, index) for matrix in (2, 0, 1) for index in range(len(chunks))]
    loading = []

    def some(count=2):
        for _ in range(count):
            if loading:
                exchange(*loading.pop(0))
            if todo:
                loading.append((*todo.pop(0), len(todo) % 2))
                exchange_load(*loading[-1])

    if has_next:

        def unit(step, _):
            block = block_at(step)
            loaded(block)
            gates(step, block)

            @pl.when(step > 0)
            def _():
                finish(block_at(step - 1))

            back(block)
            pl.when(step == 0)(functools.partial(gather_forward, 1))
            return 0

        lax.fori_loop(0, chips, unit, 0)
        finish(block_at(chips - 1))
        gather_forward(2)
        relay(0)
        weight_grads(2, r.act, r.g)
        for step in range(3, chips):
            gather_forward(step)
        weight_grads(0, r.dg, r.h)
        relay(1)
        weight_grads(1, r.du, r.h)
        for point in range(2, chips - 2):
            relay(point)
    else:

        def unit(step, _):
            block = block_at(step)
            loaded(block)
            gates(step, block)
            return 0

        def unit_back(step, _):
            back(block_at(step))

            @pl.when(step > 0)
            def _():
                finish(block_at(step - 1))

            return 0

        lax.fori_loop(0, chips, unit, 0)
        weight_grads(2, r.act, r.g)
        weight_grads(0, r.dg, r.h)
        some(1)
        lax.fori_loop(0, chips, unit_back, 0)
        finish(block_at(chips - 1))
        weight_grads(1, r.du, r.h)
        some(5)
        some(3)
    for block in range(chips):
        out_block(jnp.int32(block))
        some(2)
    if has_next:
        relay(chips - 2)
    some(len(todo) + 1)
    if not has_next:
        straight_sum()
    for index in range(2):
        put_out(0, index).wait()
    if reduced:
        for matrix in (2, 0, 1):
            for index, (start, width) in enumerate(chunks):
                here = place(matrix, start, width)
                passed(matrix, index).wait_recv()
                r.shard[here, :] = (r.shard[here, :].astype(F32) + r.got_rest[here, :].astype(F32)).astype(B16)
        for matrix in range(3):
            for index, (start, width) in enumerate(chunks):
                passed(matrix, index).wait_send()
                exchanged(matrix, index, start, width, (matrix + index) % 2 == 0).wait_send()
    for block in range(chips):
        swapped(block).wait_send()
        if has_next:
            pl.when(chip < block)(along(block, True).wait_send)
            pl.when(chip > block)(along(block, False).wait_send)
        else:
            pl.when(chip != block)(straight(block).wait_send)
    if has_next:
        gather_end()


def mlp(cot, hidden, wg, wu, wd, own, prior, rows, collective_id):
    total, depth = hidden.shape
    units = wg.shape[0]
    chips = total // (2 * rows)
    reduced = own is None and lax.axis_size("dp") == 4
    quarter = depth // 4
    count = pl.cdiv(units, CHUNK)
    anywhere = pl.BlockSpec(memory_space=pl.ANY)
    local = pl.BlockSpec(memory_space=pltpu.VMEM)
    dma = pltpu.SemaphoreType.DMA
    vmem = pltpu.VMEM
    held = jax.ShapeDtypeStruct((3 * units, quarter), B16)

    inputs = {"cot": cot, "h_hbm": hidden, "wg_hbm": wg, "wu_hbm": wu, "wd_hbm": wd}
    if own is not None:
        inputs["own"] = own
    if prior is not None:
        inputs["prior"] = prior
    outputs = {
        "out": (anywhere, jax.ShapeDtypeStruct((total, depth), B16)),
        "grad": (local, jax.ShapeDtypeStruct((rows, depth), F32)),
        "sums": (anywhere, jax.ShapeDtypeStruct((2, 2, 3 * units, quarter), B16)),
    }
    if own is not None:
        outputs["whole"] = (anywhere, jax.ShapeDtypeStruct((total, depth), B16))
    if reduced:
        outputs["shard"] = (local, held)
        outputs["landing"] = (anywhere, jax.ShapeDtypeStruct((2, 3 * units, quarter), B16))
    scratch = {
        "wg": vmem((units, depth), B16),
        "wu": vmem((units, depth), B16),
        "wd": vmem((units, depth), B16),
        "h": vmem((total, depth), B16),
        "g": vmem((total, depth), B16),
        "act": vmem((total, units), B16),
        "dg": vmem((total, units), B16),
        "du": vmem((total, units), B16),
        "part": vmem((total, depth), B16),
        "xrecv": vmem((chips, rows, depth), B16),
        "zrecv": vmem((chips + 1, rows, depth), B16),
        "stage_out": vmem((2 * rows, depth), B16),
        "stage": vmem((2, 2, 2, CHUNK, quarter), B16),
        "weight_sem": dma((3, count)),
        "load_sem": dma((2, chips)),
        "xsend": dma((chips,)),
        "xrecv_sem": dma((chips,)),
        "zsend": dma((chips,)),
        "zrecv_sem": dma((chips + 1,)),
        "out_sem": dma((2,)),
        "stage_sem": dma((2,)),
    }
    if own is not None:
        scratch["local_sem"] = dma
        scratch["gather_send"] = dma((3, chips))
        scratch["gather_recv"] = dma((chips, 2))
    if prior is not None:
        scratch["before"] = vmem((2, 2, CHUNK, quarter), B16)
        scratch["before_sem"] = dma
    if reduced:
        scratch["rest"] = vmem(held.shape, B16)
        scratch["got_rest"] = vmem(held.shape, B16)
        scratch["two_send"] = dma((3 * count,))
        scratch["two_recv"] = dma((3 * count,))
        scratch["held_own"] = vmem((2, 2, CHUNK, quarter), B16)
        scratch["held_got"] = vmem((2, 2, CHUNK, quarter), B16)
        scratch["held_sem"] = dma((2, 2))
        scratch["one_send"] = dma((3 * count,))
        scratch["one_recv"] = dma((3 * count,))
    names = [*inputs, *outputs, *scratch]
    out = pl.pallas_call(
        functools.partial(mlp_kernel, names, reduced),
        in_specs=[anywhere] * len(inputs),
        out_specs=[spec for spec, _ in outputs.values()],
        out_shape=[shape for _, shape in outputs.values()],
        scratch_shapes=list(scratch.values()),
        compiler_params=pltpu.CompilerParams(
            collective_id=collective_id, has_side_effects=True, vmem_limit_bytes=VMEM_MOST
        ),
        cost_estimate=pl.CostEstimate(
            flops=18 * total * depth * units, bytes_accessed=40 * total * depth, transcendentals=total * units
        ),
    )(*inputs.values())
    return dict(zip(outputs, out))


def widen_kernel(first_ref, second_ref, third_ref, *outs):
    for source, out in zip((first_ref, second_ref, third_ref), outs):
        quarter = source.shape[2]
        for at in range(4):
            out[:, at * quarter : (at + 1) * quarter] = source[at].astype(F32)


def widen(quarters, units):
    quarter = quarters.shape[2]
    steps = next(n for n in range(4, units) if units % (16 * n) == 0)
    size = units // steps
    return pl.pallas_call(
        widen_kernel,
        grid=(steps,),
        in_specs=[
            pl.BlockSpec((4, size, quarter), functools.partial(lambda base, i: (0, base + i, 0), at * steps))
            for at in range(3)
        ],
        out_specs=[pl.BlockSpec((size, 4 * quarter), lambda i: (i, 0))] * 3,
        out_shape=[jax.ShapeDtypeStruct((units, 4 * quarter), F32)] * 3,
        compiler_params=pltpu.CompilerParams(vmem_limit_bytes=VMEM_LIMIT),
        cost_estimate=pl.CostEstimate(flops=0, bytes_accessed=72 * units * quarter, transcendentals=0),
    )(quarters, quarters, quarters)


def norm_back(grad_out, normed, factor, gain):
    inner = grad_out * gain
    grad_rows = factor * (inner - normed * jnp.mean(inner * normed, axis=-1, keepdims=True))
    return (grad_rows, jnp.sum(grad_out * normed, axis=0))


def normalize(rows, gain):
    factor = lax.rsqrt(jnp.mean(rows * rows, axis=-1, keepdims=True) + EPS)
    normed = rows * factor
    return (normed, factor, (normed * gain).astype(B16))


def on_device(
    layer_input,
    lengths,
    attn_gain,
    query_proj,
    query_bias,
    key_proj,
    key_bias,
    value_proj,
    value_bias,
    out_proj,
    mlp_gain,
    gate_proj,
    up_proj,
    down_proj,
    cotangent,
):
    micros = layer_input.shape[0]
    rows = layer_input.shape[2]
    depth = layer_input.shape[3]
    tensor = lax.axis_index("tensor")
    total = rows * lax.axis_size("tensor")
    devices = lax.axis_size(("dp", "tensor"))
    size = query_proj.shape[0]
    small = key_bias.shape[0]
    offset = tensor * rows
    positions = offset + jnp.arange(rows, dtype=jnp.int32)
    cosine, sine = rope_tables(positions)

    valid = (positions[None, :] < lengths).astype(F32).reshape(micros, rows, 1)
    grad_rows = cotangent[:, 0].astype(F32) * valid
    low_rows = [grad_rows[m].astype(B16) for m in range(micros)]

    tail = jnp.concatenate([key_bias, value_bias, jnp.zeros((size - 2 * small,), B16)])
    extra = jnp.stack([attn_gain, query_bias, mlp_gain, tail], axis=1)
    extra = jnp.pad(extra, ((0, 0), (0, EXTRA - 4)))
    block = jnp.concatenate([query_proj, key_proj, value_proj, extra], axis=1)
    square = lax.axis_size("dp") == 4
    low = low_rows[0]
    if square:
        line = gather_line(block, 0)
        line, low = lax.optimization_barrier((line, low))
    cots = [lax.all_gather(low, "tensor", axis=0, tiled=True)]
    if square:
        packed, wout_line = gather_plane(line, 1, out_proj)
    else:
        packed = lax.all_gather(block, ("dp", "tensor"), axis=0, tiled=True)
    vectors = packed[:, QKV : QKV + 4].astype(F32)
    gain_one, gain_two = vectors[:, 0], vectors[:, 2]
    tails = vectors[:, 3].reshape(devices, size)
    bias = jnp.concatenate(
        [vectors[:, 1], tails[:, :small].reshape(-1), tails[:, small : 2 * small].reshape(-1)]
    )[None, :]

    inputs = layer_input[:, 0].astype(F32).reshape(micros * rows, depth)
    normed_one, factor_one, hidden = normalize(inputs, gain_one)
    qkv = project(
        hidden, packed, bias, jnp.tile(cosine, (micros, 1)), jnp.tile(sine, (micros, 1))
    )
    infos = [jnp.stack([lengths[m, 0], offset]) for m in range(micros)]

    own_kv = qkv[:, QW:].reshape(micros, rows, 2 * KW)
    own_kv, *cots = lax.optimization_barrier((own_kv, *cots))
    all_kv = lax.all_gather(own_kv, "tensor", axis=0)
    if square:
        wout_line, own_kv = lax.optimization_barrier((wout_line, own_kv))
        (wout,) = gather_plane(wout_line, 6)
    else:
        wout = lax.all_gather(out_proj, ("dp", "tensor"), axis=0, tiled=True)
    attended, logs, mixed, norm_two, hidden_two = [], [], [], [], []
    for m in range(micros):
        out, log = attend(infos[m], m, qkv, all_kv, rows)
        attended.append(out)
        logs.append(log)
        mixed.append(inputs[m * rows : (m + 1) * rows] + dot(out, wout))
        normed, factor, low = normalize(mixed[m], gain_two)
        norm_two.append((normed, factor))
        hidden_two.append(low)
        if m == 0:
            low, all_kv = lax.optimization_barrier((low, all_kv))
            whole = lax.all_gather(low, "tensor", axis=0, tiled=True)
    units = down_proj.shape[0]
    prior, grad_two, out_sums = None, [], []
    for m in range(1, micros):
        low, whole, *hidden_two = lax.optimization_barrier((low_rows[m], whole, *hidden_two))
        cots.append(lax.all_gather(low, "tensor", axis=0, tiled=True))
    for m in range(micros):
        own = hidden_two[m + 1] if m + 1 < micros else None
        done = mlp(cots[m], whole, gate_proj.T, up_proj.T, down_proj, own, prior, rows, 7 + m)
        whole, prior = done.get("whole"), done["sums"]
        grad_two.append(done["grad"])
        if m + 1 < micros:
            out_sums.append(lax.psum_scatter(done["out"], "tensor", scatter_dimension=0, tiled=True))
    if square:
        shard, *out_sums = lax.optimization_barrier((done["shard"], *out_sums))
        weight_grads = lax.all_gather(shard, "dp", axis=0)
    else:
        weight_grads = lax.psum(prior, "dp").reshape(4, 3 * units, depth // 4)
    grad_mixed, gain_two_grads = [], []
    for m in range(micros):
        normed, factor = norm_two[m]
        grad, gain_grad = norm_back(grad_two[m], normed, factor, gain_two)
        gain_two_grads.append(gain_grad)
        grad_mixed.append(grad + grad_rows[m])

    grad_low = jnp.concatenate(grad_mixed, axis=0).astype(B16)
    acc_out = t_dot(jnp.concatenate(attended, axis=0), grad_low).astype(B16)
    grad_attended = dot_t(grad_low, wout).astype(B16)
    grad_q, grad_kv = attend_back(
        lengths[:, 0], qkv, all_kv, grad_attended, jnp.concatenate(logs, axis=0), cosine, sine, rows, 3
    )
    grad_kv = grad_kv.reshape(micros * rows, 2 * KW)
    grad_hidden = dot_t(grad_q, packed[:, :QW]) + dot_t(grad_kv, packed[:, QW:QKV])
    grad_in, gain_one_grad = norm_back(grad_hidden, normed_one, factor_one, gain_one)
    grad_bias = jnp.concatenate(
        [jnp.sum(grad_q.astype(F32), axis=0), jnp.sum(grad_kv.astype(F32), axis=0)]
    )
    acc_q = t_dot(hidden, grad_q).astype(B16)
    acc_kv = t_dot(hidden, grad_kv).astype(B16)
    tails = jnp.concatenate(
        [
            grad_bias[QW : QW + KW].reshape(devices, small),
            grad_bias[QW + KW :].reshape(devices, small),
            jnp.zeros((devices, size - 2 * small), F32),
        ],
        axis=1,
    ).reshape(-1)
    columns = jnp.stack([gain_one_grad, grad_bias[:QW], sum(gain_two_grads), tails], axis=1)
    columns = jnp.pad(columns.astype(B16), ((0, 0), (0, EXTRA - 4)))
    out_part, weight_grads, acc_out, acc_q, acc_kv, columns = lax.optimization_barrier(
        (done["out"], weight_grads, acc_out, acc_q, acc_kv, columns)
    )
    out_sums.append(lax.psum_scatter(out_part, "tensor", scatter_dimension=0, tiled=True))
    summed = scatter_weights([acc_out, acc_q, acc_kv, columns], 2)
    out_sums, weight_grads, summed = lax.optimization_barrier((out_sums, weight_grads, summed))
    gate_total, up_total, down_total = widen(weight_grads, units)
    grad_out, grad_query, grad_kv, grad_rest = summed
    layer_output = jnp.stack(
        [(mixed[m] + out_sums[m].astype(F32)).astype(B16) for m in range(micros)]
    )[:, None]
    grad_input = (grad_in + jnp.concatenate(grad_mixed, axis=0)).reshape(micros, 1, rows, depth)
    return (
        layer_output,
        grad_input,
        grad_rest[:, 0],
        grad_query,
        grad_rest[:, 1],
        grad_kv[:, :KW],
        grad_rest[:small, 3],
        grad_kv[:, KW:],
        grad_rest[small : 2 * small, 3],
        grad_out,
        grad_rest[:, 2],
        gate_total.T,
        up_total.T,
        down_total,
    )


def solution(mesh):
    rows = P(None, "dp", "tensor", None)
    both = P(("dp", "tensor"))
    wide = P(("dp", "tensor"), None)
    placed = (
        rows,
        P(None, "dp"),
        both,
        wide,
        both,
        wide,
        both,
        wide,
        both,
        wide,
        both,
        P(None, "tensor"),
        P(None, "tensor"),
        P("tensor", None),
        rows,
    )
    return jax.shard_map(
        on_device,
        mesh=mesh,
        in_specs=placed,
        out_specs=(
            rows,
            rows,
            both,
            wide,
            both,
            wide,
            both,
            wide,
            both,
            wide,
            both,
            P(None, "tensor"),
            P(None, "tensor"),
            P("tensor", None),
        ),
        check_vma=False,
    )
```

```python
import functools

import jax
import jax.numpy as jnp
from jax import lax
from jax.experimental import pallas as pl
from jax.experimental.pallas import tpu as pltpu
from jax.sharding import PartitionSpec as P

H = 12
KV = 2
HD = 128
GROUPS = H // KV
QW = H * HD
KW = KV * HD
QKV = QW + 2 * KW
EXTRA = 128

ROPE_BASE = 1000000.0
EPS = 1e-06
MASKED = -1e30
LOG2E = 1.4426950408889634
HEADS = 3
F32 = jnp.float32
B16 = jnp.bfloat16
VMEM_LIMIT = 56 * 1024 * 1024
VMEM_MOST = 60 * 1024 * 1024
CHUNK = 256
SCATTER_LANES = 1024
MESH = pl.DeviceIdType.MESH


def dot(a, b):
    return jnp.dot(a, b, preferred_element_type=F32)


def dot_t(a, b):
    return lax.dot_general(a, b, (((1,), (1,)), ((), ())), preferred_element_type=F32)


def t_dot(a, b):
    return lax.dot_general(a, b, (((0,), (0,)), ((), ())), preferred_element_type=F32)


def rope_tables(positions):
    half = HD // 2
    freqs = ROPE_BASE ** (-(jnp.arange(half, dtype=F32) * 2.0 / HD))
    angles = positions.astype(F32)[:, None] * freqs[None, :]
    cosine = jnp.cos(angles)
    sine = jnp.sin(angles)
    return (
        jnp.concatenate([cosine, cosine], axis=1),
        jnp.concatenate([-sine, sine], axis=1),
    )


def swap(value, axis, bit):
    count = lax.axis_size(axis)
    return lax.ppermute(value, axis, [(i, i ^ bit) for i in range(count)])


def nearest(chips, place, step):
    found = 0
    for here in range(chips):
        for at, there in enumerate(sorted(range(chips), key=lambda there: abs(there - here))):
            found = found + jnp.where((place == here) & (step == at), there, 0)
    return found


class Spot:
    def __init__(self):
        self.chips = lax.axis_size("tensor") // 2
        dp, tensor = lax.axis_index("dp"), lax.axis_index("tensor")
        self.dp, self.tensor = dp, tensor
        self.row, self.col = dp // 2, dp % 2
        self.chip, self.core = tensor // 2, tensor % 2
        self.over_x = (self.row * 2 + 1 - self.col, tensor)
        self.over_y = ((1 - self.row) * 2 + self.col, tensor)
        self.beside = (dp, self.chip * 2 + 1 - self.core)
        self.left = (dp, jnp.maximum(tensor - 2, 0))
        self.right = (dp, jnp.minimum(tensor + 2, 2 * self.chips - 1))

    def on_line(self, chip):
        return (self.dp, chip * 2 + self.core)

    def index(self, row, col, chip, core):
        return ((row * 2 + col) * self.chips + chip) * 2 + core


def greet(spot, plane, line):
    barrier = pltpu.get_barrier_semaphore()
    peers = [spot.beside] + ([spot.over_x, spot.over_y] if plane else [])
    for peer in peers:
        pl.semaphore_signal(barrier, inc=1, device_id=peer, device_id_type=MESH)
    count = len(peers)
    if line == "all":
        for chip in range(spot.chips):

            @pl.when(spot.chip != chip)
            def _():
                pl.semaphore_signal(barrier, inc=1, device_id=spot.on_line(chip), device_id_type=MESH)

        count = count + spot.chips - 1
    elif line == "near":
        has_left, has_right = spot.chip > 0, spot.chip < spot.chips - 1

        @pl.when(has_left)
        def _():
            pl.semaphore_signal(barrier, inc=1, device_id=spot.left, device_id_type=MESH)

        @pl.when(has_right)
        def _():
            pl.semaphore_signal(barrier, inc=1, device_id=spot.right, device_id_type=MESH)

        count = count + jnp.where(has_left, 1, 0) + jnp.where(has_right, 1, 0)
    pl.semaphore_wait(barrier, count)


def remote(src, dst, send_sem, recv_sem, device):
    return pltpu.make_async_remote_copy(
        src_ref=src,
        dst_ref=dst,
        send_sem=send_sem,
        recv_sem=recv_sem,
        device_id=device,
        device_id_type=MESH,
    )


class Line:
    def __init__(self, spot, block_ref, line_ref, local_sem, send_sem, recv_sem):
        self.spot, self.line = spot, line_ref
        self.send_sem, self.recv_sem = send_sem, recv_sem
        self.local = pltpu.make_async_copy(block_ref, line_ref.at[spot.chip], local_sem)

    def copy(self, there, way):
        here = self.line.at[there]
        peer = (self.spot.left, self.spot.right)[way]
        return remote(here, here, self.send_sem.at[way, there], self.recv_sem.at[there], peer)

    def ways(self, there):
        chip, chips = self.spot.chip, self.spot.chips
        return ((chip > 0) & (there >= chip), (chip < chips - 1) & (there <= chip))

    def send(self, there):
        for way, when in enumerate(self.ways(there)):
            pl.when(when)(self.copy(there, way).start)

    def start(self):
        self.local.wait()
        self.send(self.spot.chip)

    def forward(self, step):
        for there in (self.spot.chip - step, self.spot.chip + step):

            @pl.when((there >= 0) & (there < self.spot.chips))
            def _():
                here = self.line.at[there]
                remote(here, here, self.send_sem.at[0, there], self.recv_sem.at[there], self.spot.beside).wait_recv()
                self.send(there)

    def end(self):
        for there in range(self.spot.chips):
            for way, when in enumerate(self.ways(there)):
                pl.when(when)(self.copy(there, way).wait_send)


def line_kernel(block_ref, line_ref, local_sem, send_sem, recv_sem):
    spot = Spot()
    line = Line(spot, block_ref, line_ref, local_sem, send_sem, recv_sem)
    line.local.start()
    greet(spot, False, "near")
    line.start()
    for step in range(1, spot.chips):
        line.forward(step)
    line.end()


def plane_kernel(more, line_ref, *refs):
    spot = Spot()
    if more:
        block_ref, whole_ref, next_ref, local_sem, send_sem, recv_sem, *sems = refs
        line = Line(spot, block_ref, next_ref, *sems)
        line.local.start()
    else:
        whole_ref, local_sem, send_sem, recv_sem = refs
    chips, chip, core, row, col = spot.chips, spot.chip, spot.core, spot.row, spot.col
    cut = chips // 2

    def local(there):
        return pltpu.make_async_copy(
            line_ref.at[there], whole_ref.at[spot.index(row, col, there, core)], local_sem.at[there]
        )

    for there in range(chips):
        local(there).start()
    greet(spot, True, "near" if more else None)
    if more:
        line.start()
    sent = []

    def send(index, device, source=None):
        source = whole_ref.at[index] if source is None else source
        copy = remote(source, whole_ref.at[index], send_sem.at[len(sent)], recv_sem.at[index], device)
        sent.append(copy)
        copy.start()

    def arrive(index):
        remote(
            whole_ref.at[index], whole_ref.at[index], send_sem.at[0], recv_sem.at[index], spot.beside
        ).wait_recv()

    for there in range(chips):
        index = spot.index(row, col, there, core)
        for peer in (spot.over_x, spot.over_y, spot.beside):
            send(index, peer, line_ref.at[there])
    for there in range(chips):
        across_x = spot.index(row, 1 - col, there, core)
        arrive(across_x)
        if there < cut:
            send(across_x, spot.over_y)
        send(across_x, spot.beside)
        across_y = spot.index(1 - row, col, there, core)
        arrive(across_y)
        if there >= cut:
            send(across_y, spot.over_x)
        send(across_y, spot.beside)
        if more and 0 < there:
            line.forward(there)
    for there in range(chips):
        index = spot.index(1 - row, 1 - col, there, core)
        arrive(index)
        send(index, spot.beside)
    for plane in range(4):
        for there in range(chips):
            arrive(spot.index(plane // 2, plane % 2, there, 1 - core))
    for there in range(chips):
        local(there).wait()
    for copy in sent:
        copy.wait_send()
    if more:
        line.end()


def gather_line(block, collective_id):
    chips = lax.axis_size("tensor") // 2
    dma = pltpu.SemaphoreType.DMA
    return pl.pallas_call(
        line_kernel,
        in_specs=[pl.BlockSpec(memory_space=pl.ANY)],
        out_specs=pl.BlockSpec(memory_space=pl.ANY),
        out_shape=jax.ShapeDtypeStruct((chips,) + block.shape, B16),
        scratch_shapes=[dma, dma((2, chips)), dma((chips,))],
        compiler_params=pltpu.CompilerParams(
            collective_id=collective_id, has_side_effects=True, vmem_limit_bytes=VMEM_LIMIT
        ),
        cost_estimate=pl.CostEstimate(flops=0, bytes_accessed=block.size * 100, transcendentals=0),
    )(block)


def gather_plane(line, collective_id, more=None):
    chips, size, width = line.shape
    dma = pltpu.SemaphoreType.DMA
    anywhere = pl.BlockSpec(memory_space=pl.ANY)
    shapes = [jax.ShapeDtypeStruct((8 * chips, size, width), B16)]
    sems = [dma((chips,)), dma((10 * chips,)), dma((8 * chips,))]
    if more is not None:
        shapes.append(jax.ShapeDtypeStruct((chips,) + more.shape, B16))
        sems += [dma, dma((2, chips)), dma((chips,))]
    out = pl.pallas_call(
        functools.partial(plane_kernel, more is not None),
        in_specs=[anywhere] * len(shapes),
        out_specs=[anywhere] * len(shapes),
        out_shape=shapes,
        scratch_shapes=sems,
        compiler_params=pltpu.CompilerParams(
            collective_id=collective_id, has_side_effects=True, vmem_limit_bytes=VMEM_LIMIT
        ),
        cost_estimate=pl.CostEstimate(flops=0, bytes_accessed=line.size * 60, transcendentals=0),
    )(line, *([] if more is None else [more]))
    return (out[0].reshape(8 * chips * size, width), *out[1:])


def scatter_kernel(parts, arrays, *refs):
    grads, outs = refs[:arrays], refs[arrays : 2 * arrays]
    mine, got, over_x, over_y, across_x, across_y, line, load_sem, send_sem, recv_sem = refs[2 * arrays :]
    spot = Spot()
    chips, chip, core, row, col = spot.chips, spot.chip, spot.core, spot.row, spot.col
    cut = chips // 2

    def at(r, c, z):
        return (r * 2 + c) * chips + z

    def lanes(p):
        return pl.ds(parts[p][0], parts[p][1])

    def source(p, which):
        _, width, array, start = parts[p]
        return grads[array].at[:, which, :, pl.ds(start, width)]

    def load(p):
        return pltpu.make_async_copy(source(p, core), mine.at[:, :, lanes(p)], load_sem.at[p])

    def swapped(p):
        return remote(
            source(p, 1 - core), got.at[:, :, lanes(p)], send_sem.at[p, 0], recv_sem.at[p, 0], spot.beside
        )

    def first(p):
        cols = lanes(p)
        copies = []
        for side in range(2):
            copies.append(
                remote(
                    mine.at[pl.ds(at(side, 1 - col, 0), cut), :, cols],
                    over_x.at[pl.ds(side * cut, cut), :, cols],
                    send_sem.at[p, 1 + side],
                    recv_sem.at[p, 1 + side],
                    spot.over_x,
                )
            )
            copies.append(
                remote(
                    mine.at[pl.ds(at(1 - row, side, cut), chips - cut), :, cols],
                    over_y.at[pl.ds(side * (chips - cut), chips - cut), :, cols],
                    send_sem.at[p, 3 + side],
                    recv_sem.at[p, 3 + side],
                    spot.over_y,
                )
            )
        return copies

    def second(p):
        cols = lanes(p)
        return [
            remote(
                mine.at[pl.ds(at(1 - row, col, 0), cut), :, cols],
                across_y.at[:, :, cols],
                send_sem.at[p, 5],
                recv_sem.at[p, 5],
                spot.over_y,
            ),
            remote(
                mine.at[pl.ds(at(row, 1 - col, cut), chips - cut), :, cols],
                across_x.at[:, :, cols],
                send_sem.at[p, 6],
                recv_sem.at[p, 6],
                spot.over_x,
            ),
        ]

    def third(p, other):
        cols = lanes(p)
        return remote(
            mine.at[at(row, col, other), :, cols],
            line.at[chip, :, cols],
            send_sem.at[p, 7 + other],
            recv_sem.at[p, 7 + chip],
            spot.on_line(other),
        )

    def add(p, target, start, source, begin, count):
        cols = lanes(p)

        def body(step, _):
            target[start + step, :, cols] = (
                target[start + step, :, cols].astype(F32) + source[begin + step, :, cols].astype(F32)
            ).astype(B16)
            return 0

        lax.fori_loop(0, count, body, 0)

    def stage_one(p):
        load(p).wait()
        swapped(p).wait()
        add(p, mine, 0, got, 0, 4 * chips)
        for copy in first(p):
            copy.start()

    def stage_two(p):
        for copy in first(p):
            copy.wait()
        for side in range(2):
            add(p, mine, at(side, col, 0), over_x, side * cut, cut)
            add(p, mine, at(row, side, cut), over_y, side * (chips - cut), chips - cut)
        for copy in second(p):
            copy.start()

    def stage_three(p):
        for copy in second(p):
            copy.wait()
        add(p, mine, at(row, col, 0), across_y, 0, cut)
        add(p, mine, at(row, col, cut), across_x, 0, chips - cut)
        for other in range(chips):
            pl.when(chip != other)(third(p, other).start)

    def stage_four(p):
        cols = lanes(p)
        total = mine[at(row, col, chip), :, cols].astype(F32)
        for other in range(chips):

            @pl.when(chip != other)
            def _():
                here = line.at[other, :, cols]
                remote(here, here, send_sem.at[p, 7 + other], recv_sem.at[p, 7 + other], spot.beside).wait_recv()

            total = total + line[other, :, cols].astype(F32)
        _, width, array, start = parts[p]
        outs[array][:, start : start + width] = total
        for other in range(chips):
            pl.when(chip != other)(third(p, other).wait_send)

    for p in range(len(parts)):
        load(p).start()
    line[chip] = jnp.zeros(line.shape[1:], B16)
    greet(spot, True, "all")
    for p in range(len(parts)):
        swapped(p).start()
    stages = (stage_one, stage_two, stage_three, stage_four)
    for step in range(len(parts) + len(stages) - 1):
        for late, stage in enumerate(stages):
            if 0 <= step - late < len(parts):
                stage(step - late)


def scatter_weights(grads, collective_id):
    total = grads[0].shape[0]
    devices = lax.axis_size(("dp", "tensor"))
    size = total // devices
    if lax.axis_size("dp") != 4:
        return [
            lax.psum_scatter(array, ("dp", "tensor"), scatter_dimension=0, tiled=True).astype(F32)
            for array in grads
        ]
    chips = lax.axis_size("tensor") // 2
    cut = chips // 2
    parts, width = [], 0
    for at, array in enumerate(grads):
        count = pl.cdiv(array.shape[1], SCATTER_LANES)
        tiles = array.shape[1] // 128
        ends = [tiles * p // count * 128 for p in range(count + 1)]
        for start, end in zip(ends, ends[1:]):
            parts.append((width + start, end - start, at, start))
        width += array.shape[1]
    dma = pltpu.SemaphoreType.DMA
    return pl.pallas_call(
        functools.partial(scatter_kernel, parts, len(grads)),
        in_specs=[pl.BlockSpec(memory_space=pl.ANY)] * len(grads),
        out_specs=[pl.BlockSpec(memory_space=pltpu.VMEM)] * len(grads),
        out_shape=[jax.ShapeDtypeStruct((size, array.shape[1]), F32) for array in grads],
        scratch_shapes=[
            pltpu.VMEM((4 * chips, size, width), B16),
            pltpu.VMEM((4 * chips, size, width), B16),
            pltpu.VMEM((2 * cut, size, width), B16),
            pltpu.VMEM((2 * (chips - cut), size, width), B16),
            pltpu.VMEM((chips - cut, size, width), B16),
            pltpu.VMEM((cut, size, width), B16),
            pltpu.VMEM((chips, size, width), B16),
            dma((len(parts),)),
            dma((len(parts), 7 + chips)),
            dma((len(parts), 7 + chips)),
        ],
        compiler_params=pltpu.CompilerParams(
            collective_id=collective_id, has_side_effects=True, vmem_limit_bytes=VMEM_LIMIT
        ),
        cost_estimate=pl.CostEstimate(flops=0, bytes_accessed=devices * size * width * 8, transcendentals=0),
    )(*[array.reshape(devices // 2, 2, size, array.shape[1]) for array in grads])


class Named:
    def __init__(self, names, refs):
        for name, ref in zip(names, refs, strict=True):
            setattr(self, name, ref)


def project_kernel(hidden_ref, weight_ref, bias_ref, cos_ref, sin_ref, out_ref):
    chunk = pl.program_id(0)
    turned = chunk < (QW + KW) // 256
    lin = dot(hidden_ref[...], weight_ref[...]) + bias_ref[...]
    for head in range(2):
        cut = pl.ds(head * HD, HD)
        one = lin[:, head * HD : (head + 1) * HD]
        rot = one * cos_ref[...] + pltpu.roll(one, HD // 2, 1) * sin_ref[...]
        out_ref[:, cut] = jnp.where(turned, rot, one).astype(B16)


def project(hidden, weights, bias, cosine, sine):
    rows, depth = hidden.shape
    return pl.pallas_call(
        project_kernel,
        grid=(QKV // 256,),
        in_specs=[
            pl.BlockSpec((rows, depth), lambda j: (0, 0)),
            pl.BlockSpec((depth, 256), lambda j: (0, j)),
            pl.BlockSpec((1, 256), lambda j: (0, j)),
            pl.BlockSpec((rows, HD), lambda j: (0, 0)),
            pl.BlockSpec((rows, HD), lambda j: (0, 0)),
        ],
        out_specs=pl.BlockSpec((rows, 256), lambda j: (0, j)),
        out_shape=jax.ShapeDtypeStruct((rows, QKV), B16),
        compiler_params=pltpu.CompilerParams(vmem_limit_bytes=VMEM_LIMIT),
        cost_estimate=pl.CostEstimate(
            flops=2 * rows * depth * QKV,
            bytes_accessed=2 * (depth * QKV + rows * depth + rows * QKV),
            transcendentals=0,
        ),
    )(hidden, weights, bias, cosine, sine)


def fill_bias(info_ref, bias):
    shape = bias.shape
    place = info_ref[1] + lax.broadcasted_iota(jnp.int32, shape, 0)
    keys = lax.broadcasted_iota(jnp.int32, shape, 1)
    bias[...] = jnp.where((keys <= place) & (keys < info_ref[0]), 0.0, MASKED)


def flat(ref):
    return ref[...].reshape(ref.shape[0] * ref.shape[2], ref.shape[3])


def attend_kernel(info_ref, q_ref, k_ref, v_ref, out_ref, log_ref, bias):
    @pl.when(pl.program_id(0) == 0)
    def _():
        fill_bias(info_ref, bias)

    keys, values = flat(k_ref), flat(v_ref)
    for head in range(HEADS):
        cut = slice(head * HD, (head + 1) * HD)
        scores = dot_t(q_ref[:, cut], keys) * (HD**-0.5 * LOG2E) + bias[...]
        top = jnp.max(scores, axis=-1, keepdims=True)
        expd = jnp.exp2(scores - top)
        summed = jnp.sum(expd, axis=-1, keepdims=True)
        out_ref[:, cut] = (dot(expd.astype(B16), values) * (1.0 / summed)).astype(B16)
        log_ref[:, cut] = jnp.broadcast_to(top + jnp.log2(summed), (q_ref.shape[0], HD))


def attend(info, micro, qkv, keys_values, rows):
    parts = keys_values.shape[0]
    total = parts * rows
    return pl.pallas_call(
        attend_kernel,
        grid_spec=pltpu.PrefetchScalarGridSpec(
            num_scalar_prefetch=1,
            grid=(H // HEADS,),
            in_specs=[
                pl.BlockSpec((rows, HEADS * HD), lambda h, info: (micro, h)),
                pl.BlockSpec((parts, 1, rows, HD), lambda h, info: (0, micro, 0, h * HEADS // GROUPS)),
                pl.BlockSpec((parts, 1, rows, HD), lambda h, info: (0, micro, 0, KV + h * HEADS // GROUPS)),
            ],
            out_specs=[
                pl.BlockSpec((rows, HEADS * HD), lambda h, info: (0, h)),
                pl.BlockSpec((rows, HEADS * HD), lambda h, info: (0, h)),
            ],
            scratch_shapes=[pltpu.VMEM((rows, total), F32)],
        ),
        out_shape=[
            jax.ShapeDtypeStruct((rows, QW), B16),
            jax.ShapeDtypeStruct((rows, QW), F32),
        ],
        compiler_params=pltpu.CompilerParams(vmem_limit_bytes=VMEM_LIMIT),
        cost_estimate=pl.CostEstimate(
            flops=8 * rows * total * QW,
            bytes_accessed=4 * total * KW + 8 * rows * QW,
            transcendentals=H * rows * total,
        ),
    )(info, qkv, keys_values, keys_values)


def attend_back_kernel(names, parts, *refs):
    r = Named(names, refs)
    spot = Spot()
    chips, chip, core = spot.chips, spot.chip, spot.core
    rows = r.q.shape[0]
    step = pl.program_id(0)
    micros = r.sums.shape[0]
    turns = H // HEADS
    micro, turn = step // turns, lax.rem(step, turns)
    span = GROUPS // HEADS
    pieces = micros * KV
    scale = HD**-0.5

    def rows_of(block, which):
        return pl.ds(pl.multiple_of((2 * block + which) * rows, rows), rows)

    def swapped(piece):
        mine = r.part.at[piece, :, 1 - core]
        return remote(mine, r.xrecv.at[piece], r.xsend.at[piece], r.xrecv_sem.at[piece], spot.beside)

    def along(piece, block):
        return remote(
            r.part.at[piece, block, core],
            r.zrecv.at[piece, chip],
            r.zsend.at[piece, block],
            r.zrecv_sem.at[piece, chip],
            spot.on_line(block),
        )

    def spread(piece):
        swapped(piece).wait_recv()
        for block in range(chips):
            total = r.part[piece, block, core].astype(F32) + r.xrecv[piece, block].astype(F32)
            r.part[piece, block, core] = total.astype(B16)
            pl.when(chip != block)(along(piece, block).start)

    @pl.when(step == 0)
    def _():
        greet(spot, False, "all")

    @pl.when(turn == 0)
    def _():
        shape = r.bias.shape
        place = spot.tensor * rows + lax.broadcasted_iota(jnp.int32, shape, 0)
        keys_at = lax.broadcasted_iota(jnp.int32, shape, 1)
        r.bias[...] = jnp.where((keys_at <= place) & (keys_at < r.length[micro]), 0.0, MASKED)

    keys, values = flat(r.k), flat(r.v)
    grad_k = grad_v = 0.0
    for head in range(HEADS):
        cut = slice(head * HD, (head + 1) * HD)
        queries, grads = r.q[:, cut], r.g[:, cut]
        scores = dot_t(queries, keys) * (scale * LOG2E) + r.bias[...]
        probs = jnp.exp2(scores - r.log[:, head * HD : head * HD + 1])
        grad_probs = dot_t(grads, values)
        inner = jnp.sum(grad_probs * probs, axis=-1, keepdims=True)
        grad_scores = (probs * (grad_probs - inner)).astype(B16)
        grad_q = dot(grad_scores, keys) * scale
        turned = grad_q * r.cos[...] - pltpu.roll(grad_q, HD // 2, 1) * r.sin[...]
        r.dq[:, cut] = turned.astype(B16)
        grad_k = grad_k + t_dot(grad_scores, queries)
        grad_v = grad_v + t_dot(probs.astype(B16), grads)
    first = lax.rem(turn, span) == 0

    @pl.when(first)
    def _():
        r.dk_acc[...] = grad_k
        r.dv_acc[...] = grad_v

    @pl.when(jnp.logical_not(first))
    def _():
        r.dk_acc[...] += grad_k
        r.dv_acc[...] += grad_v

    for piece in range(pieces):

        @pl.when(step == (piece + 1) * span - 1)
        def _():
            shape = (chips, 2, rows, HD)
            r.part[piece, :, :, :, :HD] = (r.dk_acc[...] * scale).reshape(shape).astype(B16)
            r.part[piece, :, :, :, HD:] = r.dv_acc[...].reshape(shape).astype(B16)
            swapped(piece).start()

        if piece + 1 < pieces:

            @pl.when(step == (piece + 1) * span)
            def _():
                spread(piece)

    @pl.when(step == pieces * span - 1)
    def _():
        spread(pieces - 1)
        for piece in range(pieces):
            total = r.part[piece, chip, core].astype(F32)
            for other in range(chips):

                @pl.when(chip != other)
                def _():
                    here = r.zrecv.at[piece, other]
                    remote(
                        here, here, r.zsend.at[piece, other], r.zrecv_sem.at[piece, other], spot.beside
                    ).wait_recv()

                got = jnp.where(chip != other, r.zrecv[piece, other], jnp.zeros((rows, 2 * HD), B16))
                total = total + got.astype(F32)
            at, group = piece // KV, piece % KV
            grad = total[:, :HD]
            grad = grad * r.cos[...] - pltpu.roll(grad, HD // 2, 1) * r.sin[...]
            r.sums[at, :, group * HD : (group + 1) * HD] = grad.astype(B16)
            r.sums[at, :, KW + group * HD : KW + (group + 1) * HD] = total[:, HD:].astype(B16)
        for piece in range(pieces):
            swapped(piece).wait_send()
            for block in range(chips):
                pl.when(chip != block)(along(piece, block).wait_send)


def attend_back(lengths, qkv, keys_values, grads, logs, cosine, sine, rows, collective_id):
    parts, micros = keys_values.shape[:2]
    chips = parts // 2
    total = parts * rows
    pieces = micros * KV
    turns = H // HEADS
    dma = pltpu.SemaphoreType.DMA
    vmem = pltpu.VMEM

    def heads(step):
        return (step // turns, step % turns)

    inputs = {
        "length": (pl.BlockSpec(memory_space=pltpu.SMEM), lengths),
        "q": (pl.BlockSpec((rows, HEADS * HD), heads), qkv),
        "k": (
            pl.BlockSpec((parts, 1, rows, HD), lambda s: (0, s // turns, 0, s % turns * HEADS // GROUPS)),
            keys_values,
        ),
        "v": (
            pl.BlockSpec((parts, 1, rows, HD), lambda s: (0, s // turns, 0, KV + s % turns * HEADS // GROUPS)),
            keys_values,
        ),
        "g": (pl.BlockSpec((rows, HEADS * HD), heads), grads),
        "log": (pl.BlockSpec((rows, HEADS * HD), heads), logs),
        "cos": (pl.BlockSpec((rows, HD), lambda s: (0, 0)), cosine),
        "sin": (pl.BlockSpec((rows, HD), lambda s: (0, 0)), sine),
    }
    outputs = {
        "dq": (pl.BlockSpec((rows, HEADS * HD), heads), jax.ShapeDtypeStruct((micros * rows, QW), B16)),
        "sums": (
            pl.BlockSpec((micros, rows, 2 * KW), lambda s: (0, 0, 0)),
            jax.ShapeDtypeStruct((micros, rows, 2 * KW), B16),
        ),
    }
    scratch = {
        "bias": vmem((rows, total), F32),
        "dk_acc": vmem((total, HD), F32),
        "dv_acc": vmem((total, HD), F32),
        "part": vmem((pieces, chips, 2, rows, 2 * HD), B16),
        "xrecv": vmem((pieces, chips, rows, 2 * HD), B16),
        "zrecv": vmem((pieces, chips, rows, 2 * HD), B16),
        "xsend": dma((pieces,)),
        "xrecv_sem": dma((pieces,)),
        "zsend": dma((pieces, chips)),
        "zrecv_sem": dma((pieces, chips)),
    }
    return pl.pallas_call(
        functools.partial(attend_back_kernel, [*inputs, *outputs, *scratch], parts),
        grid=(micros * turns,),
        in_specs=[spec for spec, _ in inputs.values()],
        out_specs=[spec for spec, _ in outputs.values()],
        out_shape=[shape for _, shape in outputs.values()],
        scratch_shapes=list(scratch.values()),
        compiler_params=pltpu.CompilerParams(
            collective_id=collective_id, has_side_effects=True, vmem_limit_bytes=VMEM_LIMIT
        ),
        cost_estimate=pl.CostEstimate(
            flops=20 * micros * rows * total * QW,
            bytes_accessed=micros * (8 * total * KW + 12 * rows * QW),
            transcendentals=micros * H * rows * total,
        ),
    )(*[value for _, value in inputs.values()])


def mlp_kernel(names, reduced, *refs):
    r = Named(names, refs)
    has_next, has_prior = "own" in names, "prior" in names
    spot = Spot()
    chips, chip, core, row, col = spot.chips, spot.chip, spot.core, spot.row, spot.col
    units, depth = r.wg.shape
    rows = r.grad.shape[0]
    pair = 2 * rows
    quarter = depth // 4
    chunks = [(i * CHUNK, min(CHUNK, units - i * CHUNK)) for i in range(pl.cdiv(units, CHUNK))]
    whole_chunks, rest = units // CHUNK, units % CHUNK
    wide = depth // 2

    def block_at(step):
        return nearest(chips, chip, chips - 1 - step)

    def span(block):
        return pl.ds(pl.multiple_of(block * pair, pair), pair)

    def rows_of(block, which):
        return pl.ds(pl.multiple_of(block * pair + which * rows, rows), rows)

    def columns(index, width=CHUNK):
        return pl.ds(pl.multiple_of(index * width, width), width)

    def weight_load(index):
        cut = pl.ds(*chunks[index])
        return [
            pltpu.make_async_copy(src.at[cut], dst.at[cut], r.weight_sem.at[i, index])
            for i, (src, dst) in enumerate(((r.wg_hbm, r.wg), (r.wu_hbm, r.wu), (r.wd_hbm, r.wd)))
        ]

    def weights_here(index, width=CHUNK):
        for i, dst in enumerate((r.wg, r.wu, r.wd)):
            cut = dst.at[pl.ds(index * CHUNK, width)]
            pltpu.make_async_copy(cut, cut, r.weight_sem.at[i, index]).wait()

    def h_load(block):
        return pltpu.make_async_copy(r.h_hbm.at[span(block)], r.h.at[span(block)], r.load_sem.at[0, block])

    def g_load(block):
        return pltpu.make_async_copy(r.cot.at[span(block)], r.g.at[span(block)], r.load_sem.at[1, block])

    def gather_send(block, way):
        here = r.whole.at[rows_of(block, core)]
        peer = (spot.left, spot.right, spot.beside)[way]
        return remote(here, here, r.gather_send.at[way, block], r.gather_recv.at[block, core], peer)

    def gather_first(way):
        peer = (spot.left, spot.right, spot.beside)[way]
        here = r.whole.at[rows_of(chip, core)]
        return remote(r.own, here, r.gather_send.at[way, chip], r.gather_recv.at[chip, core], peer)

    def gathered(block, which):
        here = r.whole.at[rows_of(block, which)]
        remote(here, here, r.gather_send.at[2, block], r.gather_recv.at[block, which], spot.beside).wait_recv()

    def own_copy():
        return pltpu.make_async_copy(r.own, r.whole.at[rows_of(chip, core)], r.local_sem)

    def gather_start():
        own_copy().start()
        pl.when(chip > 0)(gather_first(0).start)
        pl.when(chip < chips - 1)(gather_first(1).start)
        gather_first(2).start()

    def gather_forward(step):
        block = chip - step

        @pl.when(block >= 0)
        def _():
            gathered(block, core)
            pl.when(chip < chips - 1)(gather_send(block, 1).start)
            gather_send(block, 2).start()

        after = chip + step

        @pl.when(after < chips)
        def _():
            gathered(after, core)
            pl.when(chip > 0)(gather_send(after, 0).start)
            gather_send(after, 2).start()

    def gather_end():
        own_copy().wait()
        for block in range(chips):
            gathered(block, 1 - core)
        for block in range(chips):
            away = block != chip
            pl.when((chip > 0) & (block >= chip) & away)(gather_send(block, 0).wait_send)
            pl.when((chip < chips - 1) & (block <= chip) & away)(gather_send(block, 1).wait_send)
            pl.when(away)(gather_send(block, 2).wait_send)
        pl.when(chip > 0)(gather_first(0).wait_send)
        pl.when(chip < chips - 1)(gather_first(1).wait_send)
        gather_first(2).wait_send()

    def swapped(block):
        return remote(
            r.part.at[rows_of(block, 1 - core)],
            r.xrecv.at[block],
            r.xsend.at[block],
            r.xrecv_sem.at[block],
            spot.beside,
        )

    def along(block, ahead):
        slot = chips - 1 - block if ahead else chips - block
        return remote(
            r.part.at[rows_of(block, core)],
            r.zrecv.at[slot],
            r.zsend.at[block],
            r.zrecv_sem.at[slot],
            spot.right if ahead else spot.left,
        )

    def straight(block):
        return remote(
            r.part.at[rows_of(block, core)],
            r.zrecv.at[chip],
            r.zsend.at[block],
            r.zrecv_sem.at[chip],
            spot.on_line(block),
        )

    def straight_sum():
        for other in range(chips):

            @pl.when(chip != other)
            def _():
                here = r.zrecv.at[other]
                remote(here, here, r.zsend.at[other], r.zrecv_sem.at[other], spot.beside).wait_recv()
                r.grad[...] = r.grad[...] + r.zrecv[other].astype(F32)

    def finish(block):
        swapped(block).wait_recv()
        total = r.part[rows_of(block, core), :].astype(F32) + r.xrecv[block].astype(F32)

        @pl.when(block == chip)
        def _():
            r.grad[...] = total

        @pl.when(block != chip)
        def _():
            r.part[rows_of(block, core), :] = total.astype(B16)
            if has_next:
                pl.when(chip == 0)(along(block, True).start)
                pl.when(chip == chips - 1)(along(block, False).start)
            else:
                straight(block).start()

    def relay_one(block, ahead):
        slot = chips - 1 - block if ahead else chips - block
        remote(
            r.zrecv.at[slot], r.zrecv.at[slot], r.zsend.at[block], r.zrecv_sem.at[slot], spot.beside
        ).wait_recv()

        @pl.when(block == chip)
        def _():
            r.grad[...] = r.grad[...] + r.zrecv[slot].astype(F32)

        @pl.when(block != chip)
        def _():
            here = rows_of(block, core)
            r.part[here, :] = (r.part[here, :].astype(F32) + r.zrecv[slot].astype(F32)).astype(B16)
            along(block, ahead).start()

    def relay(point):
        step = point - (chip - 1)

        @pl.when((chip > 0) & (step >= 0) & (step < chips - chip))
        def _():
            relay_one(chips - 1 - step, True)

        back_step = point - (chips - 2 - chip)

        @pl.when((chip < chips - 1) & (back_step >= 0) & (back_step <= chip))
        def _():
            relay_one(back_step, False)

    def gate(here, start, width):
        cut = pl.ds(start, width)
        gate = dot_t(r.h[here, :], r.wg[cut, :])
        up = dot_t(r.h[here, :], r.wu[cut, :])
        grad = dot_t(r.g[here, :], r.wd[cut, :])
        sigma = jax.nn.sigmoid(gate)
        silu = gate * sigma
        r.act[here, cut] = (silu * up).astype(B16)
        r.dg[here, cut] = (grad * up * sigma * (1.0 + gate * (1.0 - sigma))).astype(B16)
        r.du[here, cut] = (grad * silu).astype(B16)

    def gates(step, block):
        here = span(block)

        def chunk(index, _):
            pl.when(step == 0)(functools.partial(weights_here, index))
            gate(here, pl.multiple_of(index * CHUNK, CHUNK), CHUNK)
            return 0

        lax.fori_loop(0, whole_chunks, chunk, 0)
        if rest:
            pl.when(step == 0)(functools.partial(weights_here, whole_chunks, rest))
            gate(here, whole_chunks * CHUNK, rest)

    def back(block):
        here = span(block)

        def chunk(index, _):
            cut = columns(index, wide)
            grad = dot(r.dg[here, :], r.wg[:, cut]) + dot(r.du[here, :], r.wu[:, cut])
            r.part[here, cut] = grad.astype(B16)
            return 0

        lax.fori_loop(0, depth // wide, chunk, 0)
        swapped(block).start()

    def put_out(block, index):
        cut = pl.ds(index * wide, wide)
        return pltpu.make_async_copy(
            r.stage_out.at[:, cut], r.out.at[span(block), cut], r.out_sem.at[index]
        )

    def out_block(block):
        for index in range(2):
            pl.when(block > 0)(put_out(block, index).wait)
            cut = slice(index * wide, (index + 1) * wide)
            r.stage_out[:, cut] = dot(r.act[span(block), :], r.wd[:, cut]).astype(B16)
            put_out(block, index).start()

    def place(matrix, start, width):
        return pl.ds(pl.multiple_of(matrix * units + start, 16), width)

    def exchanged(matrix, index, start, width, over_x):
        here = place(matrix, start, width)
        at = matrix * len(chunks) + index
        source = r.sums.at[:, 1 - col, here] if over_x else r.sums.at[1 - row, :, here]
        peer = spot.over_x if over_x else spot.over_y
        return remote(source, r.landing.at[:, here], r.one_send.at[at], r.one_recv.at[at], peer)

    def exchange_start(matrix, index, start, width):
        first = lax.rem(matrix + index, 2) == 0
        pl.when(first)(exchanged(matrix, index, start, width, True).start)
        pl.when(jnp.logical_not(first))(exchanged(matrix, index, start, width, False).start)

    def exchange_copies(matrix, index, slot):
        start, width = chunks[index]
        here = place(matrix, start, width)
        cut = pl.ds(0, width)
        own = r.sums.at[:, col, here] if (matrix + index) % 2 == 0 else r.sums.at[row, :, here]
        return [
            pltpu.make_async_copy(own, r.held_own.at[slot, :, cut], r.held_sem.at[slot, 0]),
            pltpu.make_async_copy(r.landing.at[:, here], r.held_got.at[slot, :, cut], r.held_sem.at[slot, 1]),
        ]

    def exchange_load(matrix, index, slot):
        exchanged(matrix, index, *chunks[index], (matrix + index) % 2 == 0).wait_recv()
        for copy in exchange_copies(matrix, index, slot):
            copy.start()

    def exchange(matrix, index, slot):
        start, width = chunks[index]
        for copy in exchange_copies(matrix, index, slot):
            copy.wait()
        mine = row if (matrix + index) % 2 == 0 else col
        r.shard[place(matrix, start, width), :] = (
            r.held_own[slot, mine, :width].astype(F32) + r.held_got[slot, mine, :width].astype(F32)
        ).astype(B16)
        r.rest[place(matrix, start, width), :] = (
            r.held_own[slot, 1 - mine, :width].astype(F32) + r.held_got[slot, 1 - mine, :width].astype(F32)
        ).astype(B16)
        passed(matrix, index).start()

    def passed(matrix, index):
        start, width = chunks[index]
        here = place(matrix, start, width)
        at = matrix * len(chunks) + index
        peer = spot.over_y if (matrix + index) % 2 == 0 else spot.over_x
        return remote(r.rest.at[here], r.got_rest.at[here], r.two_send.at[at], r.two_recv.at[at], peer)

    def weight_grads(matrix, left, right):
        def put(start, width, slot):
            return pltpu.make_async_copy(
                r.stage.at[slot, :, :, pl.ds(0, width)],
                r.sums.at[:, :, place(matrix, start, width)],
                r.stage_sem.at[slot],
            )

        def one(index, start, width, slot):
            if has_prior:
                fetch = pltpu.make_async_copy(
                    r.prior.at[:, :, place(matrix, start, width)],
                    r.before.at[:, :, pl.ds(0, width)],
                    r.before_sem,
                )
                fetch.start()
            value = t_dot(left[:, pl.ds(start, width)], right[...])
            if has_prior:
                fetch.wait()
            for at in range(4):
                piece = value[:, at * quarter : (at + 1) * quarter]
                if has_prior:
                    piece = piece + r.before[at // 2, at % 2, :width].astype(F32)
                r.stage[slot, at // 2, at % 2, :width] = piece.astype(B16)
            put(start, width, slot).start()

        def sent(index, start, width, slot):
            put(start, width, slot).wait()
            if reduced:
                exchange_start(matrix, index, start, width)

        def body(index, _):
            slot = lax.rem(index, 2)
            start = pl.multiple_of(index * CHUNK, CHUNK)
            one(index, start, CHUNK, slot)

            @pl.when(index > 0)
            def _():
                sent(index - 1, start - CHUNK, CHUNK, 1 - slot)

            return 0

        lax.fori_loop(0, whole_chunks, body, 0)
        index = whole_chunks
        if rest:
            one(index, index * CHUNK, rest, index % 2)
            if index:
                sent(index - 1, (index - 1) * CHUNK, CHUNK, (index - 1) % 2)
            sent(index, index * CHUNK, rest, index % 2)
        else:
            sent(index - 1, (index - 1) * CHUNK, CHUNK, (index - 1) % 2)

    for step in range(chips):
        h_load(block_at(step)).start()
        g_load(block_at(step)).start()
        if step == 0:
            for index in range(len(chunks)):
                for copy in weight_load(index):
                    copy.start()
    greet(spot, reduced, "near" if has_next else "all")
    if has_next:
        gather_start()

    def loaded(block):
        h_load(block).wait()
        g_load(block).wait()

    todo = []
    if reduced:
        todo = [(matrix, index) for matrix in (2, 0, 1) for index in range(len(chunks))]
    loading = []

    def some(count=2):
        for _ in range(count):
            if loading:
                exchange(*loading.pop(0))
            if todo:
                loading.append((*todo.pop(0), len(todo) % 2))
                exchange_load(*loading[-1])

    if has_next:

        def unit(step, _):
            block = block_at(step)
            loaded(block)
            gates(step, block)

            @pl.when(step > 0)
            def _():
                finish(block_at(step - 1))

            back(block)
            pl.when(step == 0)(functools.partial(gather_forward, 1))
            return 0

        lax.fori_loop(0, chips, unit, 0)
        finish(block_at(chips - 1))
        gather_forward(2)
        relay(0)
        weight_grads(2, r.act, r.g)
        for step in range(3, chips):
            gather_forward(step)
        weight_grads(0, r.dg, r.h)
        relay(1)
        weight_grads(1, r.du, r.h)
        for point in range(2, chips - 2):
            relay(point)
    else:

        def unit(step, _):
            block = block_at(step)
            loaded(block)
            gates(step, block)
            return 0

        def unit_back(step, _):
            back(block_at(step))

            @pl.when(step > 0)
            def _():
                finish(block_at(step - 1))

            return 0

        lax.fori_loop(0, chips, unit, 0)
        weight_grads(2, r.act, r.g)
        weight_grads(0, r.dg, r.h)
        some(1)
        lax.fori_loop(0, chips, unit_back, 0)
        finish(block_at(chips - 1))
        weight_grads(1, r.du, r.h)
        some(5)
        some(3)
    for block in range(chips):
        out_block(jnp.int32(block))
        some(2)
    if has_next:
        relay(chips - 2)
    some(len(todo) + 1)
    if not has_next:
        straight_sum()
    for index in range(2):
        put_out(0, index).wait()
    if reduced:
        for matrix in (2, 0, 1):
            for index, (start, width) in enumerate(chunks):
                here = place(matrix, start, width)
                passed(matrix, index).wait_recv()
                r.shard[here, :] = (r.shard[here, :].astype(F32) + r.got_rest[here, :].astype(F32)).astype(B16)
        for matrix in range(3):
            for index, (start, width) in enumerate(chunks):
                passed(matrix, index).wait_send()
                exchanged(matrix, index, start, width, (matrix + index) % 2 == 0).wait_send()
    for block in range(chips):
        swapped(block).wait_send()
        if has_next:
            pl.when(chip < block)(along(block, True).wait_send)
            pl.when(chip > block)(along(block, False).wait_send)
        else:
            pl.when(chip != block)(straight(block).wait_send)
    if has_next:
        gather_end()


def mlp(cot, hidden, wg, wu, wd, own, prior, rows, collective_id):
    total, depth = hidden.shape
    units = wg.shape[0]
    chips = total // (2 * rows)
    reduced = own is None and lax.axis_size("dp") == 4
    quarter = depth // 4
    count = pl.cdiv(units, CHUNK)
    anywhere = pl.BlockSpec(memory_space=pl.ANY)
    local = pl.BlockSpec(memory_space=pltpu.VMEM)
    dma = pltpu.SemaphoreType.DMA
    vmem = pltpu.VMEM
    held = jax.ShapeDtypeStruct((3 * units, quarter), B16)

    inputs = {"cot": cot, "h_hbm": hidden, "wg_hbm": wg, "wu_hbm": wu, "wd_hbm": wd}
    if own is not None:
        inputs["own"] = own
    if prior is not None:
        inputs["prior"] = prior
    outputs = {
        "out": (anywhere, jax.ShapeDtypeStruct((total, depth), B16)),
        "grad": (local, jax.ShapeDtypeStruct((rows, depth), F32)),
        "sums": (anywhere, jax.ShapeDtypeStruct((2, 2, 3 * units, quarter), B16)),
    }
    if own is not None:
        outputs["whole"] = (anywhere, jax.ShapeDtypeStruct((total, depth), B16))
    if reduced:
        outputs["shard"] = (local, held)
        outputs["landing"] = (anywhere, jax.ShapeDtypeStruct((2, 3 * units, quarter), B16))
    scratch = {
        "wg": vmem((units, depth), B16),
        "wu": vmem((units, depth), B16),
        "wd": vmem((units, depth), B16),
        "h": vmem((total, depth), B16),
        "g": vmem((total, depth), B16),
        "act": vmem((total, units), B16),
        "dg": vmem((total, units), B16),
        "du": vmem((total, units), B16),
        "part": vmem((total, depth), B16),
        "xrecv": vmem((chips, rows, depth), B16),
        "zrecv": vmem((chips + 1, rows, depth), B16),
        "stage_out": vmem((2 * rows, depth), B16),
        "stage": vmem((2, 2, 2, CHUNK, quarter), B16),
        "weight_sem": dma((3, count)),
        "load_sem": dma((2, chips)),
        "xsend": dma((chips,)),
        "xrecv_sem": dma((chips,)),
        "zsend": dma((chips,)),
        "zrecv_sem": dma((chips + 1,)),
        "out_sem": dma((2,)),
        "stage_sem": dma((2,)),
    }
    if own is not None:
        scratch["local_sem"] = dma
        scratch["gather_send"] = dma((3, chips))
        scratch["gather_recv"] = dma((chips, 2))
    if prior is not None:
        scratch["before"] = vmem((2, 2, CHUNK, quarter), B16)
        scratch["before_sem"] = dma
    if reduced:
        scratch["rest"] = vmem(held.shape, B16)
        scratch["got_rest"] = vmem(held.shape, B16)
        scratch["two_send"] = dma((3 * count,))
        scratch["two_recv"] = dma((3 * count,))
        scratch["held_own"] = vmem((2, 2, CHUNK, quarter), B16)
        scratch["held_got"] = vmem((2, 2, CHUNK, quarter), B16)
        scratch["held_sem"] = dma((2, 2))
        scratch["one_send"] = dma((3 * count,))
        scratch["one_recv"] = dma((3 * count,))
    names = [*inputs, *outputs, *scratch]
    out = pl.pallas_call(
        functools.partial(mlp_kernel, names, reduced),
        in_specs=[anywhere] * len(inputs),
        out_specs=[spec for spec, _ in outputs.values()],
        out_shape=[shape for _, shape in outputs.values()],
        scratch_shapes=list(scratch.values()),
        compiler_params=pltpu.CompilerParams(
            collective_id=collective_id, has_side_effects=True, vmem_limit_bytes=VMEM_MOST
        ),
        cost_estimate=pl.CostEstimate(
            flops=18 * total * depth * units, bytes_accessed=40 * total * depth, transcendentals=total * units
        ),
    )(*inputs.values())
    return dict(zip(outputs, out))


def widen_kernel(first_ref, second_ref, third_ref, *outs):
    for source, out in zip((first_ref, second_ref, third_ref), outs):
        quarter = source.shape[2]
        for at in range(4):
            out[:, at * quarter : (at + 1) * quarter] = source[at].astype(F32)


def widen(quarters, units):
    quarter = quarters.shape[2]
    steps = next(n for n in range(4, units) if units % (16 * n) == 0)
    size = units // steps
    return pl.pallas_call(
        widen_kernel,
        grid=(steps,),
        in_specs=[
            pl.BlockSpec((4, size, quarter), functools.partial(lambda base, i: (0, base + i, 0), at * steps))
            for at in range(3)
        ],
        out_specs=[pl.BlockSpec((size, 4 * quarter), lambda i: (i, 0))] * 3,
        out_shape=[jax.ShapeDtypeStruct((units, 4 * quarter), F32)] * 3,
        compiler_params=pltpu.CompilerParams(vmem_limit_bytes=VMEM_LIMIT),
        cost_estimate=pl.CostEstimate(flops=0, bytes_accessed=72 * units * quarter, transcendentals=0),
    )(quarters, quarters, quarters)


def norm_back(grad_out, normed, factor, gain):
    inner = grad_out * gain
    grad_rows = factor * (inner - normed * jnp.mean(inner * normed, axis=-1, keepdims=True))
    return (grad_rows, jnp.sum(grad_out * normed, axis=0))


def normalize(rows, gain):
    factor = lax.rsqrt(jnp.mean(rows * rows, axis=-1, keepdims=True) + EPS)
    normed = rows * factor
    return (normed, factor, (normed * gain).astype(B16))


def on_device(
    layer_input,
    lengths,
    attn_gain,
    query_proj,
    query_bias,
    key_proj,
    key_bias,
    value_proj,
    value_bias,
    out_proj,
    mlp_gain,
    gate_proj,
    up_proj,
    down_proj,
    cotangent,
):
    micros = layer_input.shape[0]
    rows = layer_input.shape[2]
    depth = layer_input.shape[3]
    tensor = lax.axis_index("tensor")
    total = rows * lax.axis_size("tensor")
    devices = lax.axis_size(("dp", "tensor"))
    size = query_proj.shape[0]
    small = key_bias.shape[0]
    offset = tensor * rows
    positions = offset + jnp.arange(rows, dtype=jnp.int32)
    cosine, sine = rope_tables(positions)

    valid = (positions[None, :] < lengths).astype(F32).reshape(micros, rows, 1)
    grad_rows = cotangent[:, 0].astype(F32) * valid
    low_rows = [grad_rows[m].astype(B16) for m in range(micros)]

    tail = jnp.concatenate([key_bias, value_bias, jnp.zeros((size - 2 * small,), B16)])
    extra = jnp.stack([attn_gain, query_bias, mlp_gain, tail], axis=1)
    extra = jnp.pad(extra, ((0, 0), (0, EXTRA - 4)))
    block = jnp.concatenate([query_proj, key_proj, value_proj, extra], axis=1)
    square = lax.axis_size("dp") == 4
    low = low_rows[0]
    if square:
        line = gather_line(block, 0)
        line, low = lax.optimization_barrier((line, low))
    cots = [lax.all_gather(low, "tensor", axis=0, tiled=True)]
    if square:
        packed, wout_line = gather_plane(line, 1, out_proj)
    else:
        packed = lax.all_gather(block, ("dp", "tensor"), axis=0, tiled=True)
    vectors = packed[:, QKV : QKV + 4].astype(F32)
    gain_one, gain_two = vectors[:, 0], vectors[:, 2]
    tails = vectors[:, 3].reshape(devices, size)
    bias = jnp.concatenate(
        [vectors[:, 1], tails[:, :small].reshape(-1), tails[:, small : 2 * small].reshape(-1)]
    )[None, :]

    inputs = layer_input[:, 0].astype(F32).reshape(micros * rows, depth)
    normed_one, factor_one, hidden = normalize(inputs, gain_one)
    qkv = project(
        hidden, packed, bias, jnp.tile(cosine, (micros, 1)), jnp.tile(sine, (micros, 1))
    )
    infos = [jnp.stack([lengths[m, 0], offset]) for m in range(micros)]

    own_kv = qkv[:, QW:].reshape(micros, rows, 2 * KW)
    own_kv, *cots = lax.optimization_barrier((own_kv, *cots))
    all_kv = lax.all_gather(own_kv, "tensor", axis=0)
    if square:
        wout_line, own_kv = lax.optimization_barrier((wout_line, own_kv))
        (wout,) = gather_plane(wout_line, 6)
    else:
        wout = lax.all_gather(out_proj, ("dp", "tensor"), axis=0, tiled=True)
    attended, logs, mixed, norm_two, hidden_two = [], [], [], [], []
    for m in range(micros):
        out, log = attend(infos[m], m, qkv, all_kv, rows)
        attended.append(out)
        logs.append(log)
        mixed.append(inputs[m * rows : (m + 1) * rows] + dot(out, wout))
        normed, factor, low = normalize(mixed[m], gain_two)
        norm_two.append((normed, factor))
        hidden_two.append(low)
        if m == 0:
            low, all_kv = lax.optimization_barrier((low, all_kv))
            whole = lax.all_gather(low, "tensor", axis=0, tiled=True)
    units = down_proj.shape[0]
    prior, grad_two, out_sums = None, [], []
    for m in range(1, micros):
        low, whole, *hidden_two = lax.optimization_barrier((low_rows[m], whole, *hidden_two))
        cots.append(lax.all_gather(low, "tensor", axis=0, tiled=True))
    for m in range(micros):
        own = hidden_two[m + 1] if m + 1 < micros else None
        done = mlp(cots[m], whole, gate_proj.T, up_proj.T, down_proj, own, prior, rows, 7 + m)
        whole, prior = done.get("whole"), done["sums"]
        grad_two.append(done["grad"])
        if m + 1 < micros:
            out_sums.append(lax.psum_scatter(done["out"], "tensor", scatter_dimension=0, tiled=True))
    if square:
        shard, *out_sums = lax.optimization_barrier((done["shard"], *out_sums))
        weight_grads = lax.all_gather(shard, "dp", axis=0)
    else:
        weight_grads = lax.psum(prior, "dp").reshape(4, 3 * units, depth // 4)
    grad_mixed, gain_two_grads = [], []
    for m in range(micros):
        normed, factor = norm_two[m]
        grad, gain_grad = norm_back(grad_two[m], normed, factor, gain_two)
        gain_two_grads.append(gain_grad)
        grad_mixed.append(grad + grad_rows[m])

    grad_low = jnp.concatenate(grad_mixed, axis=0).astype(B16)
    acc_out = t_dot(jnp.concatenate(attended, axis=0), grad_low).astype(B16)
    grad_attended = dot_t(grad_low, wout).astype(B16)
    grad_q, grad_kv = attend_back(
        lengths[:, 0], qkv, all_kv, grad_attended, jnp.concatenate(logs, axis=0), cosine, sine, rows, 3
    )
    grad_kv = grad_kv.reshape(micros * rows, 2 * KW)
    grad_hidden = dot_t(grad_q, packed[:, :QW]) + dot_t(grad_kv, packed[:, QW:QKV])
    grad_in, gain_one_grad = norm_back(grad_hidden, normed_one, factor_one, gain_one)
    grad_bias = jnp.concatenate(
        [jnp.sum(grad_q.astype(F32), axis=0), jnp.sum(grad_kv.astype(F32), axis=0)]
    )
    acc_q = t_dot(hidden, grad_q).astype(B16)
    acc_kv = t_dot(hidden, grad_kv).astype(B16)
    tails = jnp.concatenate(
        [
            grad_bias[QW : QW + KW].reshape(devices, small),
            grad_bias[QW + KW :].reshape(devices, small),
            jnp.zeros((devices, size - 2 * small), F32),
        ],
        axis=1,
    ).reshape(-1)
    columns = jnp.stack([gain_one_grad, grad_bias[:QW], sum(gain_two_grads), tails], axis=1)
    columns = jnp.pad(columns.astype(B16), ((0, 0), (0, EXTRA - 4)))
    grad_input = (grad_in + jnp.concatenate(grad_mixed, axis=0)).reshape(micros, 1, rows, depth)
    out_part, weight_grads, acc_out, acc_q, acc_kv, columns, grad_input = lax.optimization_barrier(
        (done["out"], weight_grads, acc_out, acc_q, acc_kv, columns, grad_input)
    )
    out_sums.append(lax.psum_scatter(out_part, "tensor", scatter_dimension=0, tiled=True))
    summed = scatter_weights([acc_out, acc_q, acc_kv, columns], 2)
    out_sums, weight_grads, summed = lax.optimization_barrier((out_sums, weight_grads, summed))
    gate_total, up_total, down_total = widen(weight_grads, units)
    grad_out, grad_query, grad_kv, grad_rest = summed
    layer_output = jnp.stack(
        [(mixed[m] + out_sums[m].astype(F32)).astype(B16) for m in range(micros)]
    )[:, None]
    return (
        layer_output,
        grad_input,
        grad_rest[:, 0],
        grad_query,
        grad_rest[:, 1],
        grad_kv[:, :KW],
        grad_rest[:small, 3],
        grad_kv[:, KW:],
        grad_rest[small : 2 * small, 3],
        grad_out,
        grad_rest[:, 2],
        gate_total.T,
        up_total.T,
        down_total,
    )


def solution(mesh):
    rows = P(None, "dp", "tensor", None)
    both = P(("dp", "tensor"))
    wide = P(("dp", "tensor"), None)
    placed = (
        rows,
        P(None, "dp"),
        both,
        wide,
        both,
        wide,
        both,
        wide,
        both,
        wide,
        both,
        P(None, "tensor"),
        P(None, "tensor"),
        P("tensor", None),
        rows,
    )
    return jax.shard_map(
        on_device,
        mesh=mesh,
        in_specs=placed,
        out_specs=(
            rows,
            rows,
            both,
            wide,
            both,
            wide,
            both,
            wide,
            both,
            wide,
            both,
            P(None, "tensor"),
            P(None, "tensor"),
            P("tensor", None),
        ),
        check_vma=False,
    )
```
